128 devices in a mesh: tseg: 2 (over y_lo), inp: 64 (over x, z, y_hi, core).
Axes of the slice: x: 4, y: 4 (y_hi: 2, y_lo: 2; y = y_hi * 2 + y_lo), z: 4, core: 2. Of those that a mesh axis runs over, the one named last changes fastest.
Arguments:
- samples: bfloat16 [512, 524288], P('inp', 'tseg')
- delays: int32 [512], P('inp'), may hold values from 0 to 8192, as said below
- flags: int32 [512], P('inp'), may hold values 0 or 1
- taps: float32 [16, 1024], replicated, may hold values from -1.5 to 1.5
Outputs:
- vis_real: float32 [512, 512, 512], P(('tseg', 'inp'))
- vis_imag: float32 [512, 512, 512], P(('tseg', 'inp'))
The draws below stay inside these ranges and needn't reach their ends.
Inputs may be any that keep to these rules, and one draw needn't show every extreme that they name: `delays`: some input has delay 0 and some input has delay 8192.
All inputs are finite; a program needn't handle non-finite values. No bound on the sum of `flags` on one device may be relied on, other than what follows from the above.
Results may differ from the reference program's by a relative error of at most 0.0075.
Values may be sent and summed in bfloat16 or wider, within the bound.
A program may use at most 64 MiB of HBM per device.

```python
import math
import jax
import jax.numpy as jnp
from jax import lax

NI = 512
C = 512
TAPS = 16
DMAX = 8192
FRAME = 1024
SPECTRA = 512
SAMPLES = 524288
HALO = 23552


def common_delays(key):
    base = jax.random.fold_in(key, 101)
    drawn = jax.random.randint(base, (NI,), 0, DMAX + 1)
    chosen = jax.random.randint(jax.random.fold_in(base, 1), (), 0, NI)
    position = jnp.arange(NI)
    drawn = jnp.where(position == chosen, DMAX, drawn)
    drawn = jnp.where(position == (chosen + 1) % NI, 0, drawn)
    return drawn.astype(jnp.int32)


def draw_delays(key, part):
    drawn = common_delays(key)
    return drawn


def draw_samples(key, part):
    drawn = common_delays(key)
    key = jax.random.fold_in(key, 2)
    key_source, key_gain, key_noise = jax.random.split(key, 3)
    source = jax.random.normal(key_source, (SAMPLES + DMAX,), jnp.float32)
    gains = jax.random.uniform(key_gain, (NI,), jnp.float32, 0.5, 1.5)
    noise = jax.random.normal(key_noise, (NI, SAMPLES), jnp.float32)
    aligned = jax.vmap(lambda start: lax.dynamic_slice_in_dim(source, start, SAMPLES))(drawn)
    return (gains[:, None] * aligned + noise).astype(jnp.bfloat16)


def plant(values, rng, least, top_value):
    longest = values.shape.index(max(values.shape))
    spots = []
    for shift in (0, 1):
        where = [jax.random.randint(jax.random.fold_in(rng, axis), (), 0, length) for axis, length in enumerate(values.shape)]
        where[longest] = (where[longest] + shift) % values.shape[longest]
        spots.append(tuple(where))
    return values.at[spots[0]].set(least).at[spots[1]].set(top_value)


def normal_values(key, shape, width, reach, kind=jnp.bfloat16):
    return jnp.clip(width * jax.random.normal(key, shape, jnp.float32), -reach, reach).astype(kind)


def setup_inputs(seed: int = 0) -> dict:
    key_list = jax.random.split(jax.random.key(seed), 5)
    return {
        "samples": draw_samples(jax.random.fold_in(key_list[4], 71), 0),
        "delays": draw_delays(jax.random.fold_in(key_list[4], 71), 0),
        "flags": plant((jax.random.randint(key_list[2], (NI,), 0, 8) < 7).astype(jnp.int32), jax.random.fold_in(key_list[2], 1), 0, 1),
        "taps": normal_values(key_list[3], (TAPS, FRAME), TAPS ** -0.5, 1.5, jnp.float32),
    }


def dft_table():
    sample_index = jnp.arange(FRAME, dtype=jnp.int32)[:, None]
    chan_index = jnp.arange(C, dtype=jnp.int32)[None, :]
    phase = (sample_index * chan_index % FRAME).astype(jnp.float32) * (2.0 * math.pi / FRAME)
    factor = 1.0 / math.sqrt(FRAME)
    return jnp.concatenate([jnp.cos(phase) * factor, -jnp.sin(phase) * factor], axis=1).astype(jnp.bfloat16)

def reference(samples, delays, flags, taps):
    dft_values = dft_table().astype(jnp.float32)

    def one_input(item):
        sample_row, lag_count, flag_value = item
        padded = jnp.concatenate([jnp.zeros((HALO,), jnp.float32), sample_row.astype(jnp.float32)])
        window = lax.dynamic_slice_in_dim(padded, (DMAX - lag_count).astype(jnp.int32), (TAPS - 1) * FRAME + SAMPLES)
        frames = window.reshape(TAPS - 1 + SPECTRA, FRAME)
        filtered = jnp.zeros((SPECTRA, FRAME), jnp.float32)
        for tap_index in range(TAPS):
            filtered = filtered + taps[tap_index][None, :] * frames[tap_index:tap_index + SPECTRA]
        filtered = (filtered * flag_value.astype(jnp.float32)).astype(jnp.bfloat16)
        spectrum = jnp.einsum('kq,sk->qs', dft_values, filtered.astype(jnp.float32))
        return spectrum.astype(jnp.bfloat16)
    spectra = lax.map(one_input, (samples, delays, flags))
    spectra = spectra.reshape(NI, 2, C, SPECTRA).transpose(2, 1, 0, 3)

    def one_channel(block):
        real_part = block[0].astype(jnp.float32)
        imag_part = block[1].astype(jnp.float32)
        rr_sum = jnp.dot(real_part, real_part.T, preferred_element_type=jnp.float32)
        ii_sum = jnp.dot(imag_part, imag_part.T, preferred_element_type=jnp.float32)
        ri_sum = jnp.dot(real_part, imag_part.T, preferred_element_type=jnp.float32)
        ir_sum = jnp.dot(imag_part, real_part.T, preferred_element_type=jnp.float32)
        return ((rr_sum + ii_sum) / SPECTRA, (ri_sum - ir_sum) / SPECTRA)
    vis_real, vis_imag = lax.map(one_channel, spectra)
    return (vis_real, vis_imag)
```

```python
import functools
import math

import jax
import jax.numpy as jnp
import ml_dtypes
import numpy as np
from jax import lax
from jax.experimental import pallas as pl
from jax.experimental.pallas import tpu as pltpu
from jax.sharding import PartitionSpec as P

MESH = pl.DeviceIdType.MESH
TAPS = 16
FRAME = 1024
HALO = 23552
LANES = 128
BLOCKS = FRAME // LANES
HERE = 8
S_DEV = 256
HALF = 128
CHAN = 4
ROWS = CHAN * 2 * HERE
HALO_BLOCKS = HALO // LANES
FIRST = HALO_BLOCKS + 8
STRIDE = FIRST + S_DEV * BLOCKS + 1
SPLIT = 824
F_STRIDE = HALF + 1
O_STRIDE = HERE + 1
SHAPES = {64: (4, 4, 2), 4: (2, 1, 1)}


def dft_rows(nx, ny, nz):
    count = nx * ny * nz * 2
    inp = count // 2
    k = np.arange(FRAME)[None, :]
    q = np.arange(count * CHAN)[:, None]
    phase = ((q * k) % FRAME).astype(np.float64) * (2.0 * math.pi / FRAME)
    parts = np.stack([np.cos(phase), -np.sin(phase)], axis=1) / math.sqrt(FRAME)
    parts = parts.astype(np.float32).astype(ml_dtypes.bfloat16)
    parts = parts.reshape(2, nx, nz, ny // 2, 2, CHAN * 2, FRAME)
    parts = parts.transpose(1, 3, 0, 2, 4, 5, 6)
    assert inp * 2 == count
    return parts.reshape(nx * ny * nz, 2 * CHAN * 2, FRAME)


def exchange_kernel(
    dims,
    samples,
    delays,
    flags,
    taps,
    table,
    out,
    raw,
    rim,
    rows_table,
    late,
    tap_rows,
    filtered,
    frames,
    turned,
    ready,
    load_sem,
    table_sem,
    rim_send,
    rim_recv,
    send_sem,
    recv_sem,
    own_sem,
):
    nx, ny, nz = dims
    inp = nx * nz * ny
    devices = 2 * inp
    groups = nz
    per_group = nx * ny
    tseg = lax.axis_index("tseg")
    here = lax.axis_index("inp")
    me = tseg * inp + here
    my_core = here % 2
    my_y = ((here // 2) % (ny // 2)) * 2 + tseg
    my_z = (here // ny) % nz
    my_x = here // (ny * nz)

    def chip_of(group, step):
        dx = step % nx
        dy = step // nx
        dz = (group + 2 * nz + 2 * nx + 2 * ny - dx - dy) % nz
        return (my_x + dx) % nx, (my_y + dy) % ny, (my_z + dz) % nz

    late_load = pltpu.make_async_copy(
        samples.at[:, pl.ds(SPLIT * LANES, (S_DEV * BLOCKS - SPLIT) * LANES)],
        raw.at[:, pl.ds(SPLIT * LANES, (S_DEV * BLOCKS - SPLIT) * LANES)],
        load_sem.at[0],
    )
    late_load.start()
    early_load = pltpu.make_async_copy(
        samples.at[:, pl.ds(0, SPLIT * LANES)],
        raw.at[:, pl.ds(0, SPLIT * LANES)],
        load_sem.at[1],
    )
    early_load.start()

    barrier = pltpu.get_barrier_semaphore()

    def greet(step, carry):
        other = (me + step) % devices
        pl.semaphore_signal(
            barrier, inc=1, device_id=(other // inp, other % inp), device_id_type=MESH
        )
        return carry

    lax.fori_loop(1, devices, greet, 0)

    def fetch(step, carry):
        x, y, z = chip_of(step // per_group, step % per_group)
        pltpu.make_async_copy(
            table.at[(x * ny + y) * nz + z],
            rows_table.at[step // per_group, step % per_group],
            table_sem,
        ).start()
        return carry

    lax.fori_loop(0, groups * per_group, fetch, 0)

    for p0 in (0, 8):
        for block in range(BLOCKS):
            tap_rows[pl.ds(p0 * BLOCKS + block, 8, stride=BLOCKS), :] = taps[
                p0 : p0 + 8, block * LANES : (block + 1) * LANES
            ]

    lane = lax.broadcasted_iota(jnp.int32, (HERE, LANES), 1)
    row = lax.broadcasted_iota(jnp.int32, (HERE, LANES), 0)
    turn = jnp.zeros((HERE, LANES), jnp.int32)
    for i in range(HERE):
        turn = jnp.where(row == i, delays[i] % LANES, turn)
    index = (lane - turn + LANES) % LANES

    def spread(source, first, chunk):
        values = source[:, pl.ds(pl.multiple_of(chunk * FRAME, FRAME), FRAME)].astype(jnp.float32)
        for block in range(BLOCKS):
            moved = jnp.take_along_axis(
                values[:, block * LANES : (block + 1) * LANES], index, axis=1
            )
            late[pl.ds(first + chunk * BLOCKS + block, HERE, stride=STRIDE), :] = moved

    def run_half(half):
        base = half * HALF

        def filter_block(i, step):
            delay = delays[i]
            part = delay % LANES
            start = i * STRIDE + FIRST + (base + step * TAPS - (TAPS - 1)) * BLOCKS - delay // LANES
            keep = lane >= part
            weight = flags[i].astype(jnp.float32)
            window = []
            for f in range(2 * TAPS - 1):
                here_rows = late[pl.ds(start + f * BLOCKS, BLOCKS), :]
                before = late[pl.ds(start + f * BLOCKS - 1, BLOCKS), :]
                window.append(jnp.where(keep, here_rows, before))
            for s in range(TAPS):
                total = tap_rows[0:BLOCKS, :] * window[s]
                for p in range(1, TAPS):
                    total += tap_rows[p * BLOCKS : (p + 1) * BLOCKS, :] * window[s + p]
                filtered[
                    pl.ds(i * BLOCKS * F_STRIDE + step * TAPS + s, BLOCKS, stride=F_STRIDE), :
                ] = total * weight

        @pl.loop(0, HERE)
        def _(i):
            @pl.loop(0, HALF // TAPS)
            def _(step):
                filter_block(i, step)

        @pl.loop(0, HERE)
        def _(i):
            for block in range(BLOCKS):
                values = filtered[pl.ds((i * BLOCKS + block) * F_STRIDE, HALF), :]
                frames[
                    pl.ds(pl.multiple_of(i * HALF, HALF), HALF),
                    block * LANES : (block + 1) * LANES,
                ] = values.astype(jnp.bfloat16)

    def send_half(half):
        @pl.loop(0, groups)
        def _(group):
            rows = rows_table[group].reshape(per_group * 16, FRAME)

            @pl.loop(0, HERE // 2)
            def _(pair):
                values = frames[pl.ds(pl.multiple_of(pair * 2 * HALF, 2 * HALF), 2 * HALF), :]
                spectra = lax.dot_general(
                    rows, values, (((1,), (1,)), ((), ())), preferred_element_type=jnp.float32
                )
                for dest in range(2 * per_group):
                    for j in range(2):
                        turned[
                            pl.ds(dest * 8 * O_STRIDE + pair * 2 + j, 8, stride=O_STRIDE), :
                        ] = spectra[dest * 8 : (dest + 1) * 8, j * HALF : (j + 1) * HALF]

            def pack(chip, core):
                dest = chip * 2 + core
                for m in range(0, 8, 2):
                    pair_rows = jnp.concatenate(
                        [
                            turned[pl.ds((dest * 8 + m) * O_STRIDE, HERE), :],
                            turned[pl.ds((dest * 8 + m + 1) * O_STRIDE, HERE), :],
                        ],
                        axis=0,
                    )
                    ready[half, group * 2 * per_group + dest, m * 8 : (m + 2) * 8, :] = (
                        pair_rows.astype(jnp.bfloat16)
                    )

            @pl.loop(0, per_group)
            def _(chip):
                pack(chip, 0)
                pack(chip, 1)
                x, y, z = chip_of(group, chip)
                for change in range(2):
                    core = (my_core + change) % 2
                    slot = ready.at[half, (group * per_group + chip) * 2 + core]
                    to_inp = ((x * nz + z) * (ny // 2) + y // 2) * 2 + core

                    def send():
                        pltpu.make_async_remote_copy(
                            src_ref=slot,
                            dst_ref=out.at[half, me],
                            send_sem=send_sem.at[half],
                            recv_sem=recv_sem.at[half],
                            device_id=(y % 2, to_inp),
                            device_id_type=MESH,
                        ).start()

                    if change == 0:
                        own = jnp.logical_and(group == 0, chip == 0)

                        @pl.when(own)
                        def _():
                            pltpu.make_async_copy(
                                slot, out.at[half, me], own_sem.at[half]
                            ).start()

                        pl.when(jnp.logical_not(own))(send)
                    else:
                        send()

    late_load.wait()

    @pl.loop(SPLIT // BLOCKS, S_DEV)
    def _(chunk):
        spread(raw, FIRST, chunk)

    pl.semaphore_wait(barrier, devices - 1)
    rim_copy = pltpu.make_async_remote_copy(
        src_ref=samples.at[:, pl.ds(S_DEV * FRAME - HALO, HALO)],
        dst_ref=rim,
        send_sem=rim_send,
        recv_sem=rim_recv,
        device_id=(1 - tseg, here),
        device_id_type=MESH,
    )
    rim_copy.start()

    run_half(1)
    pltpu.make_async_copy(rows_table, rows_table, table_sem).wait()
    send_half(1)

    early_load.wait()

    @pl.loop(0, SPLIT // BLOCKS)
    def _(chunk):
        spread(raw, FIRST, chunk)

    rim_copy.wait()

    @pl.when(tseg == 0)
    def _():
        rim[...] = jnp.zeros_like(rim)

    @pl.loop(0, HALO_BLOCKS // BLOCKS)
    def _(chunk):
        spread(rim, FIRST - HALO_BLOCKS, chunk)

    run_half(0)
    send_half(0)

    for half in (1, 0):
        own_slot = ready.at[half, my_core]
        pltpu.make_async_copy(own_slot, out.at[half, me], own_sem.at[half]).wait()
        sent = ready.at[half, pl.ds(0, devices - 1)]
        pltpu.make_async_copy(sent, sent, send_sem.at[half]).wait()
        arrived = out.at[half, pl.ds(0, devices - 1)]
        pltpu.make_async_copy(arrived, arrived, recv_sem.at[half]).wait()


def correlate_kernel(segments, scale, spectra, vis_real, vis_imag):
    sources = spectra.shape[1] // segments
    inputs = sources * HERE
    real, imag = [], []
    for half in range(2):
        for segment in range(segments):
            piece = spectra[half, segment * sources : (segment + 1) * sources].astype(jnp.float32)
            real.append(piece[:, :HERE].reshape(inputs, HALF).astype(jnp.bfloat16))
            imag.append(piece[:, HERE:].reshape(inputs, HALF).astype(jnp.bfloat16))
    real = jnp.concatenate(real, axis=1)
    imag = jnp.concatenate(imag, axis=1)

    def product(a, b):
        return lax.dot_general(a, b, (((1,), (1,)), ((), ())), preferred_element_type=jnp.float32)

    vis_real[0] = (product(real, real) + product(imag, imag)) * scale
    vis_imag[0] = (product(real, imag) - product(imag, real)) * scale


def per_device(samples, delays, flags, taps, *, segments, inp):
    nx, nz, ny_hi = SHAPES[inp]
    dims = (nx, 2 * ny_hi, nz)
    devices = segments * inp
    per_group = nx * 2 * ny_hi
    table = jnp.asarray(dft_rows(*dims))
    anywhere = pl.BlockSpec(memory_space=pl.ANY)
    spectra = pl.pallas_call(
        functools.partial(exchange_kernel, dims),
        out_shape=jax.ShapeDtypeStruct((2, devices, ROWS, HALF), jnp.bfloat16),
        in_specs=[
            anywhere,
            pl.BlockSpec(memory_space=pltpu.SMEM),
            pl.BlockSpec(memory_space=pltpu.SMEM),
            pl.BlockSpec(memory_space=pltpu.VMEM),
            anywhere,
        ],
        out_specs=anywhere,
        scratch_shapes=[
            pltpu.VMEM((HERE, S_DEV * FRAME), jnp.bfloat16),
            pltpu.VMEM((HERE, HALO), jnp.bfloat16),
            pltpu.VMEM((nz, per_group, 16, FRAME), jnp.bfloat16),
            pltpu.VMEM((HERE * STRIDE + 8, LANES), jnp.float32),
            pltpu.VMEM((TAPS * BLOCKS, LANES), jnp.float32),
            pltpu.VMEM((HERE * BLOCKS * F_STRIDE, LANES), jnp.float32),
            pltpu.VMEM((HERE * HALF, FRAME), jnp.bfloat16),
            pltpu.VMEM((2 * per_group * 8 * O_STRIDE, LANES), jnp.float32),
            pltpu.VMEM((2, devices, ROWS, HALF), jnp.bfloat16),
            pltpu.SemaphoreType.DMA((2,)),
            pltpu.SemaphoreType.DMA,
            pltpu.SemaphoreType.DMA,
            pltpu.SemaphoreType.DMA,
            pltpu.SemaphoreType.DMA((2,)),
            pltpu.SemaphoreType.DMA((2,)),
            pltpu.SemaphoreType.DMA((2,)),
        ],
        compiler_params=pltpu.CompilerParams(
            collective_id=0, has_side_effects=True, vmem_limit_bytes=48 * 2**20
        ),
        name="filter_and_exchange",
    )(samples, delays, flags, taps, table)
    inputs = inp * HERE
    visibility = jax.ShapeDtypeStruct((CHAN, inputs, inputs), jnp.float32)
    return pl.pallas_call(
        functools.partial(correlate_kernel, segments, 1.0 / (S_DEV * segments)),
        out_shape=(visibility, visibility),
        grid=(CHAN,),
        in_specs=[pl.BlockSpec((2, devices, 2 * HERE, HALF), lambda c: (0, 0, c, 0))],
        out_specs=(
            pl.BlockSpec((1, inputs, inputs), lambda c: (c, 0, 0)),
            pl.BlockSpec((1, inputs, inputs), lambda c: (c, 0, 0)),
        ),
        compiler_params=pltpu.CompilerParams(vmem_limit_bytes=32 * 2**20),
        name="correlate",
    )(spectra)


def solution(mesh):
    segments, inp = mesh.shape["tseg"], mesh.shape["inp"]
    return jax.shard_map(
        functools.partial(per_device, segments=segments, inp=inp),
        mesh=mesh,
        in_specs=(P("inp", "tseg"), P("inp"), P("inp"), P()),
        out_specs=(P(("tseg", "inp"), None, None), P(("tseg", "inp"), None, None)),
        check_vma=False,
    )
```

```python
import functools
import math

import jax
import jax.numpy as jnp
import ml_dtypes
import numpy as np
from jax import lax
from jax.experimental import pallas as pl
from jax.experimental.pallas import tpu as pltpu
from jax.sharding import PartitionSpec as P

MESH = pl.DeviceIdType.MESH
TAPS = 16
FRAME = 1024
HALO = 23552
LANES = 128
BLOCKS = FRAME // LANES
HERE = 8
S_DEV = 256
HALF = 128
CHAN = 4
ROWS = CHAN * 2 * HERE
HALO_BLOCKS = HALO // LANES
FIRST = HALO_BLOCKS + 8
STRIDE = FIRST + S_DEV * BLOCKS + 1
SPLIT = 824
F_STRIDE = HALF + 1
O_STRIDE = HERE + 1
SHAPES = {64: (4, 4, 2), 4: (2, 1, 1)}


def dft_rows(nx, ny, nz):
    count = nx * ny * nz * 2
    inp = count // 2
    k = np.arange(FRAME)[None, :]
    q = np.arange(count * CHAN)[:, None]
    phase = ((q * k) % FRAME).astype(np.float64) * (2.0 * math.pi / FRAME)
    parts = np.stack([np.cos(phase), -np.sin(phase)], axis=1) / math.sqrt(FRAME)
    parts = parts.astype(np.float32).astype(ml_dtypes.bfloat16)
    parts = parts.reshape(2, nx, nz, ny // 2, 2, CHAN * 2, FRAME)
    parts = parts.transpose(1, 3, 0, 2, 4, 5, 6)
    assert inp * 2 == count
    return parts.reshape(nx * ny * nz, 2 * CHAN * 2, FRAME)


class Work:
    def __init__(self, dims, delays, flags, refs):
        self.dims = dims
        self.delays, self.flags = delays, flags
        self.rows_table, self.late, self.tap_rows, self.filtered, self.frames, self.turned = refs
        nx, ny, nz = dims
        self.inp = nx * nz * ny
        self.tseg = lax.axis_index("tseg")
        self.here = lax.axis_index("inp")
        self.me = self.tseg * self.inp + self.here
        self.my_core = self.here % 2
        self.my_y = ((self.here // 2) % (ny // 2)) * 2 + self.tseg
        self.my_z = (self.here // ny) % nz
        self.my_x = self.here // (ny * nz)
        self.lane = lax.broadcasted_iota(jnp.int32, (HERE, LANES), 1)

    def chip_of(self, group, step):
        nx, ny, nz = self.dims
        dx = step % nx
        dy = step // nx
        dz = (group + 2 * nz + 2 * nx + 2 * ny - dx - dy) % nz
        return (self.my_x + dx) % nx, (self.my_y + dy) % ny, (self.my_z + dz) % nz

    def fetch_table(self, table, sem):
        nx, ny, nz = self.dims
        per_group = nx * ny

        @pl.loop(0, nz * per_group)
        def _(step):
            x, y, z = self.chip_of(step // per_group, step % per_group)
            pltpu.make_async_copy(
                table.at[(x * ny + y) * nz + z],
                self.rows_table.at[step // per_group, step % per_group],
                sem,
            ).start()

    def place_taps(self, taps):
        for p0 in (0, 8):
            for block in range(BLOCKS):
                self.tap_rows[pl.ds(p0 * BLOCKS + block, 8, stride=BLOCKS), :] = taps[
                    p0 : p0 + 8, block * LANES : (block + 1) * LANES
                ]

    def spread(self, source, first, chunk_range, unroll):
        row = lax.broadcasted_iota(jnp.int32, (HERE, LANES), 0)
        turn = jnp.zeros((HERE, LANES), jnp.int32)
        for i in range(HERE):
            turn = jnp.where(row == i, self.delays[i] % LANES, turn)
        index = (self.lane - turn + LANES) % LANES

        @pl.loop(*chunk_range, unroll=unroll)
        def _(chunk):
            values = source[:, pl.ds(pl.multiple_of(chunk * FRAME, FRAME), FRAME)].astype(
                jnp.float32
            )
            for block in range(BLOCKS):
                moved = jnp.take_along_axis(
                    values[:, block * LANES : (block + 1) * LANES], index, axis=1
                )
                self.late[pl.ds(first + chunk * BLOCKS + block, HERE, stride=STRIDE), :] = moved

    def run_half(self, half):
        base = half * HALF

        def filter_block(i, step):
            delay = self.delays[i]
            part = delay % LANES
            start = i * STRIDE + FIRST + (base + step * TAPS - (TAPS - 1)) * BLOCKS - delay // LANES
            keep = self.lane >= part
            weight = self.flags[i].astype(jnp.float32)
            window = []
            for f in range(2 * TAPS - 1):
                here_rows = self.late[pl.ds(start + f * BLOCKS, BLOCKS), :]
                before = self.late[pl.ds(start + f * BLOCKS - 1, BLOCKS), :]
                window.append(jnp.where(keep, here_rows, before))
            for s in range(TAPS):
                total = self.tap_rows[0:BLOCKS, :] * window[s]
                for p in range(1, TAPS):
                    total += self.tap_rows[p * BLOCKS : (p + 1) * BLOCKS, :] * window[s + p]
                self.filtered[
                    pl.ds(i * BLOCKS * F_STRIDE + step * TAPS + s, BLOCKS, stride=F_STRIDE), :
                ] = total * weight

        @pl.loop(0, HERE)
        def _(i):
            @pl.loop(0, HALF // TAPS)
            def _(step):
                filter_block(i, step)

        @pl.loop(0, HERE)
        def _(i):
            for block in range(BLOCKS):
                values = self.filtered[pl.ds((i * BLOCKS + block) * F_STRIDE, HALF), :]
                self.frames[
                    pl.ds(pl.multiple_of(i * HALF, HALF), HALF),
                    block * LANES : (block + 1) * LANES,
                ] = values.astype(jnp.bfloat16)

    def transform(self, group):
        nx, ny, nz = self.dims
        per_group = nx * ny
        rows = self.rows_table[group].reshape(per_group * 16, FRAME)

        @pl.loop(0, HERE // 2)
        def _(pair):
            values = self.frames[pl.ds(pl.multiple_of(pair * 2 * HALF, 2 * HALF), 2 * HALF), :]
            spectra = lax.dot_general(
                rows, values, (((1,), (1,)), ((), ())), preferred_element_type=jnp.float32
            )
            for dest in range(2 * per_group):
                for j in range(2):
                    self.turned[
                        pl.ds(dest * 8 * O_STRIDE + pair * 2 + j, 8, stride=O_STRIDE), :
                    ] = spectra[dest * 8 : (dest + 1) * 8, j * HALF : (j + 1) * HALF]

    def pack(self, dest, target):
        for m in range(0, 8, 2):
            pair_rows = jnp.concatenate(
                [
                    self.turned[pl.ds((dest * 8 + m) * O_STRIDE, HERE), :],
                    self.turned[pl.ds((dest * 8 + m + 1) * O_STRIDE, HERE), :],
                ],
                axis=0,
            )
            target[m * 8 : (m + 2) * 8, :] = pair_rows.astype(jnp.bfloat16)

    def start_copies(self, group, chip, source, target, send_sem, recv_sem, own_sem):
        nx, ny, nz = self.dims
        x, y, z = self.chip_of(group, chip)
        for change in range(2):
            core = (self.my_core + change) % 2
            slot = source.at[(group * nx * ny + chip) * 2 + core]
            to_inp = ((x * nz + z) * (ny // 2) + y // 2) * 2 + core

            def send():
                pltpu.make_async_remote_copy(
                    src_ref=slot,
                    dst_ref=target.at[self.me],
                    send_sem=send_sem,
                    recv_sem=recv_sem,
                    device_id=(y % 2, to_inp),
                    device_id_type=MESH,
                ).start()

            if change == 0:
                own = jnp.logical_and(group == 0, chip == 0)

                @pl.when(own)
                def _():
                    pltpu.make_async_copy(slot, target.at[self.me], own_sem).start()

                pl.when(jnp.logical_not(own))(send)
            else:
                send()


def first_kernel(dims, samples, delays, flags, taps, table, ready, raw, *rest):
    refs, (load_sem, table_sem) = rest[:6], rest[6:]
    work = Work(dims, delays, flags, refs)
    nx, ny, nz = dims
    per_group = nx * ny
    part = pl.ds(SPLIT * LANES, (S_DEV * BLOCKS - SPLIT) * LANES)
    load = pltpu.make_async_copy(samples.at[:, part], raw.at[:, part], load_sem)
    load.start()
    work.fetch_table(table, table_sem)
    work.place_taps(taps)
    load.wait()
    work.spread(raw, FIRST, (SPLIT // BLOCKS, S_DEV - 1), 4)
    work.spread(raw, FIRST, (S_DEV - 1, S_DEV), 1)
    work.run_half(1)
    pltpu.make_async_copy(work.rows_table, work.rows_table, table_sem).wait()

    @pl.loop(0, nz)
    def _(group):
        work.transform(group)

        @pl.loop(0, 2 * per_group, unroll=2)
        def _(dest):
            work.pack(dest, ready.at[group * 2 * per_group + dest])


def exchange_kernel(dims, samples, delays, flags, taps, table, first, out, raw, rim, ready, *rest):
    refs, sems = rest[:6], rest[6:]
    load_sem, table_sem, rim_send, rim_recv, send_sem, recv_sem, own_sem = sems
    work = Work(dims, delays, flags, refs)
    nx, ny, nz = dims
    per_group = nx * ny
    inp = nx * ny * nz
    devices = 2 * inp
    barrier = pltpu.get_barrier_semaphore()

    @pl.loop(1, devices)
    def _(step):
        other = (work.me + step) % devices
        pl.semaphore_signal(
            barrier, inc=1, device_id=(other // inp, other % inp), device_id_type=MESH
        )

    part = pl.ds(0, S_DEV // 2 * FRAME)
    load = pltpu.make_async_copy(samples.at[:, part], raw.at[:, part], load_sem)
    load.start()
    work.fetch_table(table, table_sem)
    work.place_taps(taps)
    pl.semaphore_wait(barrier, devices - 1)
    rim_copy = pltpu.make_async_remote_copy(
        src_ref=samples.at[:, pl.ds(S_DEV * FRAME - HALO, HALO)],
        dst_ref=rim,
        send_sem=rim_send,
        recv_sem=rim_recv,
        device_id=(1 - work.tseg, work.here),
        device_id_type=MESH,
    )
    rim_copy.start()

    def start(half, group, chip):
        work.start_copies(
            group,
            chip,
            (ready, first)[half],
            out.at[half],
            send_sem.at[half],
            recv_sem.at[half],
            own_sem.at[half],
        )

    @pl.loop(0, nz)
    def _(group):
        @pl.loop(0, per_group)
        def _(chip):
            start(1, group, chip)

    load.wait()
    work.spread(raw, FIRST, (0, S_DEV // 2), 4)
    rim_copy.wait()

    @pl.when(work.tseg == 0)
    def _():
        rim[...] = jnp.zeros_like(rim)

    work.spread(rim, FIRST - HALO_BLOCKS, (0, 20), 4)
    work.spread(rim, FIRST - HALO_BLOCKS, (20, HALO_BLOCKS // BLOCKS), 1)
    work.run_half(0)
    pltpu.make_async_copy(work.rows_table, work.rows_table, table_sem).wait()

    @pl.loop(0, nz)
    def _(group):
        work.transform(group)

        @pl.loop(0, per_group)
        def _(chip):
            for core in range(2):
                dest = chip * 2 + core
                work.pack(dest, ready.at[group * 2 * per_group + dest])
            start(0, group, chip)

    for half in (1, 0):
        source = (ready, first)[half]
        pltpu.make_async_copy(
            source.at[work.my_core], out.at[half, work.me], own_sem.at[half]
        ).wait()
        sent = source.at[pl.ds(0, devices - 1)]
        pltpu.make_async_copy(sent, sent, send_sem.at[half]).wait()
        arrived = out.at[half, pl.ds(0, devices - 1)]
        pltpu.make_async_copy(arrived, arrived, recv_sem.at[half]).wait()


def correlate_kernel(segments, scale, spectra, vis_real, vis_imag):
    sources = spectra.shape[1] // segments
    inputs = sources * HERE
    real, imag = [], []
    for half in range(2):
        for segment in range(segments):
            piece = spectra[half, segment * sources : (segment + 1) * sources].astype(jnp.float32)
            real.append(piece[:, :HERE].reshape(inputs, HALF).astype(jnp.bfloat16))
            imag.append(piece[:, HERE:].reshape(inputs, HALF).astype(jnp.bfloat16))
    real = jnp.concatenate(real, axis=1)
    imag = jnp.concatenate(imag, axis=1)

    def product(a, b):
        return lax.dot_general(a, b, (((1,), (1,)), ((), ())), preferred_element_type=jnp.float32)

    vis_real[0] = (product(real, real) + product(imag, imag)) * scale
    vis_imag[0] = (product(real, imag) - product(imag, real)) * scale


def per_device(samples, delays, flags, taps, *, segments, inp):
    nx, nz, ny_hi = SHAPES[inp]
    dims = (nx, 2 * ny_hi, nz)
    devices = segments * inp
    per_group = nx * 2 * ny_hi
    table = jnp.asarray(dft_rows(*dims))
    anywhere = pl.BlockSpec(memory_space=pl.ANY)
    in_specs = [
        anywhere,
        pl.BlockSpec(memory_space=pltpu.SMEM),
        pl.BlockSpec(memory_space=pltpu.SMEM),
        pl.BlockSpec(memory_space=pltpu.VMEM),
        anywhere,
    ]
    work_scratch = [
        pltpu.VMEM((nz, per_group, 16, FRAME), jnp.bfloat16),
        pltpu.VMEM((HERE * STRIDE + 8, LANES), jnp.float32),
        pltpu.VMEM((TAPS * BLOCKS, LANES), jnp.float32),
        pltpu.VMEM((HERE * BLOCKS * F_STRIDE, LANES), jnp.float32),
        pltpu.VMEM((HERE * HALF, FRAME), jnp.bfloat16),
        pltpu.VMEM((2 * per_group * 8 * O_STRIDE, LANES), jnp.float32),
    ]
    raw = pltpu.VMEM((HERE, S_DEV * FRAME), jnp.bfloat16)
    dma = pltpu.SemaphoreType.DMA
    first = pl.pallas_call(
        functools.partial(first_kernel, dims),
        out_shape=jax.ShapeDtypeStruct((devices, ROWS, HALF), jnp.bfloat16),
        in_specs=in_specs,
        out_specs=pl.BlockSpec(memory_space=pltpu.VMEM),
        scratch_shapes=[raw, *work_scratch, dma, dma],
        compiler_params=pltpu.CompilerParams(vmem_limit_bytes=60 * 2**20),
        name="filter_first_half",
    )(samples, delays, flags, taps, table)
    spectra = pl.pallas_call(
        functools.partial(exchange_kernel, dims),
        out_shape=jax.ShapeDtypeStruct((2, devices, ROWS, HALF), jnp.bfloat16),
        in_specs=[*in_specs, anywhere],
        out_specs=anywhere,
        scratch_shapes=[
            raw,
            pltpu.VMEM((HERE, HALO), jnp.bfloat16),
            pltpu.VMEM((devices, ROWS, HALF), jnp.bfloat16),
            *work_scratch,
            *[dma] * 4,
            *[dma((2,))] * 3,
        ],
        compiler_params=pltpu.CompilerParams(
            collective_id=0, has_side_effects=True, vmem_limit_bytes=60 * 2**20
        ),
        name="exchange",
    )(samples, delays, flags, taps, table, first)
    inputs = inp * HERE
    visibility = jax.ShapeDtypeStruct((CHAN, inputs, inputs), jnp.float32)
    return pl.pallas_call(
        functools.partial(correlate_kernel, segments, 1.0 / (S_DEV * segments)),
        out_shape=(visibility, visibility),
        grid=(CHAN,),
        in_specs=[pl.BlockSpec((2, devices, 2 * HERE, HALF), lambda c: (0, 0, c, 0))],
        out_specs=(
            pl.BlockSpec((1, inputs, inputs), lambda c: (c, 0, 0)),
            pl.BlockSpec((1, inputs, inputs), lambda c: (c, 0, 0)),
        ),
        compiler_params=pltpu.CompilerParams(vmem_limit_bytes=60 * 2**20),
        name="correlate",
    )(spectra)


def solution(mesh):
    segments, inp = mesh.shape["tseg"], mesh.shape["inp"]
    return jax.shard_map(
        functools.partial(per_device, segments=segments, inp=inp),
        mesh=mesh,
        in_specs=(P("inp", "tseg"), P("inp"), P("inp"), P()),
        out_specs=(P(("tseg", "inp"), None, None), P(("tseg", "inp"), None, None)),
        check_vma=False,
    )
```

```python
import functools
import math

import jax
import jax.numpy as jnp
import ml_dtypes
import numpy as np
from jax import lax
from jax.experimental import pallas as pl
from jax.experimental.pallas import tpu as pltpu
from jax.sharding import PartitionSpec as P

MESH = pl.DeviceIdType.MESH
TAPS = 16
FRAME = 1024
HALO = 23552
LANES = 128
BLOCKS = FRAME // LANES
HERE = 8
S_DEV = 256
HALF = 128
CHAN = 4
ROWS = CHAN * 2 * HERE
HALO_BLOCKS = HALO // LANES
FIRST = HALO_BLOCKS + 8
STRIDE = FIRST + S_DEV * BLOCKS + 1
SPLIT = 824
F_STRIDE = HALF + 1
O_STRIDE = HERE + 1
SHAPES = {64: (4, 4, 2), 4: (2, 1, 1)}


def dft_rows(nx, ny, nz):
    count = nx * ny * nz * 2
    inp = count // 2
    k = np.arange(FRAME)[None, :]
    q = np.arange(count * CHAN)[:, None]
    phase = ((q * k) % FRAME).astype(np.float64) * (2.0 * math.pi / FRAME)
    parts = np.stack([np.cos(phase), -np.sin(phase)], axis=1) / math.sqrt(FRAME)
    parts = parts.astype(np.float32).astype(ml_dtypes.bfloat16)
    parts = parts.reshape(2, nx, nz, ny // 2, 2, CHAN * 2, FRAME)
    parts = parts.transpose(1, 3, 0, 2, 4, 5, 6)
    assert inp * 2 == count
    return parts.reshape(nx * ny * nz, 2 * CHAN * 2, FRAME)


class Work:
    def __init__(self, dims, delays, flags, refs):
        self.dims = dims
        self.delays, self.flags = delays, flags
        self.rows_table, self.late, self.tap_rows, self.filtered, self.frames, self.turned = refs
        nx, ny, nz = dims
        self.inp = nx * nz * ny
        self.tseg = lax.axis_index("tseg")
        self.here = lax.axis_index("inp")
        self.me = self.tseg * self.inp + self.here
        self.my_core = self.here % 2
        self.my_y = ((self.here // 2) % (ny // 2)) * 2 + self.tseg
        self.my_z = (self.here // ny) % nz
        self.my_x = self.here // (ny * nz)
        self.lane = lax.broadcasted_iota(jnp.int32, (HERE, LANES), 1)

    def chip_of(self, group, step):
        nx, ny, nz = self.dims
        dx = step % nx
        dy = step // nx
        dz = (group + 2 * nz + 2 * nx + 2 * ny - dx - dy) % nz
        return (self.my_x + dx) % nx, (self.my_y + dy) % ny, (self.my_z + dz) % nz

    def fetch_table(self, table, sem):
        nx, ny, nz = self.dims
        per_group = nx * ny

        @pl.loop(0, nz * per_group)
        def _(step):
            x, y, z = self.chip_of(step // per_group, step % per_group)
            pltpu.make_async_copy(
                table.at[(x * ny + y) * nz + z],
                self.rows_table.at[step // per_group, step % per_group],
                sem,
            ).start()

    def place_taps(self, taps):
        for p0 in (0, 8):
            for block in range(BLOCKS):
                self.tap_rows[pl.ds(p0 * BLOCKS + block, 8, stride=BLOCKS), :] = taps[
                    p0 : p0 + 8, block * LANES : (block + 1) * LANES
                ]

    def spread(self, source, first, chunk_range, unroll):
        row = lax.broadcasted_iota(jnp.int32, (HERE, LANES), 0)
        turn = jnp.zeros((HERE, LANES), jnp.int32)
        for i in range(HERE):
            turn = jnp.where(row == i, self.delays[i] % LANES, turn)
        index = (self.lane - turn + LANES) % LANES

        @pl.loop(*chunk_range, unroll=unroll)
        def _(chunk):
            values = source[:, pl.ds(pl.multiple_of(chunk * FRAME, FRAME), FRAME)].astype(
                jnp.float32
            )
            for block in range(BLOCKS):
                moved = jnp.take_along_axis(
                    values[:, block * LANES : (block + 1) * LANES], index, axis=1
                )
                self.late[pl.ds(first + chunk * BLOCKS + block, HERE, stride=STRIDE), :] = moved

    def run_half(self, half):
        base = half * HALF

        def filter_block(i, step):
            delay = self.delays[i]
            part = delay % LANES
            start = i * STRIDE + FIRST + (base + step * TAPS - (TAPS - 1)) * BLOCKS - delay // LANES
            keep = self.lane >= part
            weight = self.flags[i].astype(jnp.float32)
            window = []
            for f in range(2 * TAPS - 1):
                here_rows = self.late[pl.ds(start + f * BLOCKS, BLOCKS), :]
                before = self.late[pl.ds(start + f * BLOCKS - 1, BLOCKS), :]
                window.append(jnp.where(keep, here_rows, before))
            for s in range(TAPS):
                total = self.tap_rows[0:BLOCKS, :] * window[s]
                for p in range(1, TAPS):
                    total += self.tap_rows[p * BLOCKS : (p + 1) * BLOCKS, :] * window[s + p]
                self.filtered[
                    pl.ds(i * BLOCKS * F_STRIDE + step * TAPS + s, BLOCKS, stride=F_STRIDE), :
                ] = total * weight

        @pl.loop(0, HERE)
        def _(i):
            @pl.loop(0, HALF // TAPS)
            def _(step):
                filter_block(i, step)

        @pl.loop(0, HERE)
        def _(i):
            for block in range(BLOCKS):
                values = self.filtered[pl.ds((i * BLOCKS + block) * F_STRIDE, HALF), :]
                self.frames[
                    pl.ds(pl.multiple_of(i * HALF, HALF), HALF),
                    block * LANES : (block + 1) * LANES,
                ] = values.astype(jnp.bfloat16)

    def transform(self, group):
        nx, ny, nz = self.dims
        per_group = nx * ny
        rows = self.rows_table[group].reshape(per_group * 16, FRAME)

        @pl.loop(0, HERE // 2)
        def _(pair):
            values = self.frames[pl.ds(pl.multiple_of(pair * 2 * HALF, 2 * HALF), 2 * HALF), :]
            spectra = lax.dot_general(
                rows, values, (((1,), (1,)), ((), ())), preferred_element_type=jnp.float32
            )
            for dest in range(2 * per_group):
                for j in range(2):
                    self.turned[
                        pl.ds(dest * 8 * O_STRIDE + pair * 2 + j, 8, stride=O_STRIDE), :
                    ] = spectra[dest * 8 : (dest + 1) * 8, j * HALF : (j + 1) * HALF]

    def pack(self, dest, target):
        for m in range(0, 8, 2):
            pair_rows = jnp.concatenate(
                [
                    self.turned[pl.ds((dest * 8 + m) * O_STRIDE, HERE), :],
                    self.turned[pl.ds((dest * 8 + m + 1) * O_STRIDE, HERE), :],
                ],
                axis=0,
            )
            target[m * 8 : (m + 2) * 8, :] = pair_rows.astype(jnp.bfloat16)

    def start_copies(self, group, chip, source, target, send_sem, recv_sem, own_sem):
        nx, ny, nz = self.dims
        x, y, z = self.chip_of(group, chip)
        for change in range(2):
            core = (self.my_core + change) % 2
            slot = source.at[(group * nx * ny + chip) * 2 + core]
            to_inp = ((x * nz + z) * (ny // 2) + y // 2) * 2 + core

            def send():
                pltpu.make_async_remote_copy(
                    src_ref=slot,
                    dst_ref=target.at[self.me],
                    send_sem=send_sem,
                    recv_sem=recv_sem,
                    device_id=(y % 2, to_inp),
                    device_id_type=MESH,
                ).start()

            if change == 0:
                own = jnp.logical_and(group == 0, chip == 0)

                @pl.when(own)
                def _():
                    pltpu.make_async_copy(slot, target.at[self.me], own_sem).start()

                pl.when(jnp.logical_not(own))(send)
            else:
                send()


def filter_kernel(dims, samples, delays, flags, taps, frames, raw, late, tap_rows, filtered, load_sem):
    work = Work(dims, delays, flags, (None, late, tap_rows, filtered, frames, None))
    part = pl.ds(SPLIT * LANES, (S_DEV * BLOCKS - SPLIT) * LANES)
    load = pltpu.make_async_copy(samples.at[:, part], raw.at[:, part], load_sem)
    load.start()
    work.place_taps(taps)
    load.wait()
    work.spread(raw, FIRST, (SPLIT // BLOCKS, S_DEV - 1), 4)
    work.spread(raw, FIRST, (S_DEV - 1, S_DEV), 1)
    work.run_half(1)


def transform_kernel(dims, frames, table, ready, rows_table, turned, table_sem):
    work = Work(dims, None, None, (rows_table, None, None, None, frames, turned))
    nx, ny, nz = dims
    per_group = nx * ny
    work.fetch_table(table, table_sem)
    pltpu.make_async_copy(rows_table, rows_table, table_sem).wait()

    @pl.loop(0, nz)
    def _(group):
        work.transform(group)

        @pl.loop(0, 2 * per_group, unroll=2)
        def _(dest):
            work.pack(dest, ready.at[group * 2 * per_group + dest])


def exchange_kernel(dims, samples, delays, flags, taps, table, first, out, raw, rim, ready, *rest):
    refs, sems = rest[:6], rest[6:]
    load_sem, table_sem, rim_send, rim_recv, send_sem, recv_sem, own_sem = sems
    work = Work(dims, delays, flags, refs)
    nx, ny, nz = dims
    per_group = nx * ny
    inp = nx * ny * nz
    devices = 2 * inp
    barrier = pltpu.get_barrier_semaphore()

    @pl.loop(1, devices)
    def _(step):
        other = (work.me + step) % devices
        pl.semaphore_signal(
            barrier, inc=1, device_id=(other // inp, other % inp), device_id_type=MESH
        )

    part = pl.ds(0, S_DEV // 2 * FRAME)
    load = pltpu.make_async_copy(samples.at[:, part], raw.at[:, part], load_sem)
    load.start()
    work.fetch_table(table, table_sem)
    work.place_taps(taps)
    pl.semaphore_wait(barrier, devices - 1)
    rim_copy = pltpu.make_async_remote_copy(
        src_ref=samples.at[:, pl.ds(S_DEV * FRAME - HALO, HALO)],
        dst_ref=rim,
        send_sem=rim_send,
        recv_sem=rim_recv,
        device_id=(1 - work.tseg, work.here),
        device_id_type=MESH,
    )
    rim_copy.start()

    def start(half, group, chip):
        work.start_copies(
            group,
            chip,
            (ready, first)[half],
            out.at[half],
            send_sem.at[half],
            recv_sem.at[half],
            own_sem.at[half],
        )

    @pl.loop(0, nz)
    def _(group):
        @pl.loop(0, per_group)
        def _(chip):
            start(1, group, chip)

    load.wait()
    work.spread(raw, FIRST, (0, S_DEV // 2), 4)
    rim_copy.wait()

    @pl.when(work.tseg == 0)
    def _():
        rim[...] = jnp.zeros_like(rim)

    work.spread(rim, FIRST - HALO_BLOCKS, (0, 20), 4)
    work.spread(rim, FIRST - HALO_BLOCKS, (20, HALO_BLOCKS // BLOCKS), 1)
    work.run_half(0)
    pltpu.make_async_copy(work.rows_table, work.rows_table, table_sem).wait()

    @pl.loop(0, nz)
    def _(group):
        work.transform(group)

        @pl.loop(0, per_group)
        def _(chip):
            for core in range(2):
                dest = chip * 2 + core
                work.pack(dest, ready.at[group * 2 * per_group + dest])
            start(0, group, chip)

    for half in (1, 0):
        source = (ready, first)[half]
        pltpu.make_async_copy(
            source.at[work.my_core], out.at[half, work.me], own_sem.at[half]
        ).wait()
        sent = source.at[pl.ds(0, devices - 1)]
        pltpu.make_async_copy(sent, sent, send_sem.at[half]).wait()
        arrived = out.at[half, pl.ds(0, devices - 1)]
        pltpu.make_async_copy(arrived, arrived, recv_sem.at[half]).wait()


def correlate_kernel(segments, scale, spectra, vis_real, vis_imag):
    sources = spectra.shape[1] // segments
    inputs = sources * HERE
    real, imag = [], []
    for half in range(2):
        for segment in range(segments):
            piece = spectra[half, segment * sources : (segment + 1) * sources].astype(jnp.float32)
            real.append(piece[:, :HERE].reshape(inputs, HALF).astype(jnp.bfloat16))
            imag.append(piece[:, HERE:].reshape(inputs, HALF).astype(jnp.bfloat16))
    real = jnp.concatenate(real, axis=1)
    imag = jnp.concatenate(imag, axis=1)

    def product(a, b):
        return lax.dot_general(a, b, (((1,), (1,)), ((), ())), preferred_element_type=jnp.float32)

    middle = inputs // 2
    low, high = slice(0, middle), slice(middle, inputs)
    for rows, columns in ((low, low), (high, high), (low, high)):
        block = product(real[rows], real[columns]) + product(imag[rows], imag[columns])
        vis_real[0, rows, columns] = block * scale
        if rows != columns:
            vis_real[0, columns, rows] = block.T * scale
    cross = product(real, imag)
    vis_imag[0] = (cross - cross.T) * scale


def per_device(samples, delays, flags, taps, *, segments, inp):
    nx, nz, ny_hi = SHAPES[inp]
    dims = (nx, 2 * ny_hi, nz)
    devices = segments * inp
    per_group = nx * 2 * ny_hi
    table = jnp.asarray(dft_rows(*dims))
    anywhere = pl.BlockSpec(memory_space=pl.ANY)
    in_specs = [
        anywhere,
        pl.BlockSpec(memory_space=pltpu.SMEM),
        pl.BlockSpec(memory_space=pltpu.SMEM),
        pl.BlockSpec(memory_space=pltpu.VMEM),
        anywhere,
    ]
    work_scratch = [
        pltpu.VMEM((nz, per_group, 16, FRAME), jnp.bfloat16),
        pltpu.VMEM((HERE * STRIDE + 8, LANES), jnp.float32),
        pltpu.VMEM((TAPS * BLOCKS, LANES), jnp.float32),
        pltpu.VMEM((HERE * BLOCKS * F_STRIDE, LANES), jnp.float32),
        pltpu.VMEM((HERE * HALF, FRAME), jnp.bfloat16),
        pltpu.VMEM((2 * per_group * 8 * O_STRIDE, LANES), jnp.float32),
    ]
    raw = pltpu.VMEM((HERE, S_DEV * FRAME), jnp.bfloat16)
    dma = pltpu.SemaphoreType.DMA
    rows_table, late, tap_rows, filtered, frames, turned = work_scratch
    grant = pltpu.CompilerParams(vmem_limit_bytes=60 * 2**20)
    first_frames = pl.pallas_call(
        functools.partial(filter_kernel, dims),
        out_shape=jax.ShapeDtypeStruct(frames.shape, frames.dtype),
        in_specs=in_specs[:4],
        out_specs=pl.BlockSpec(memory_space=pltpu.VMEM),
        scratch_shapes=[raw, late, tap_rows, filtered, dma],
        compiler_params=grant,
        name="filter_first_half",
    )(samples, delays, flags, taps)
    first = pl.pallas_call(
        functools.partial(transform_kernel, dims),
        out_shape=jax.ShapeDtypeStruct((devices, ROWS, HALF), jnp.bfloat16),
        in_specs=[pl.BlockSpec(memory_space=pltpu.VMEM), anywhere],
        out_specs=pl.BlockSpec(memory_space=pltpu.VMEM),
        scratch_shapes=[rows_table, turned, dma],
        compiler_params=grant,
        name="transform_first_half",
    )(first_frames, table)
    spectra = pl.pallas_call(
        functools.partial(exchange_kernel, dims),
        out_shape=jax.ShapeDtypeStruct((2, devices, ROWS, HALF), jnp.bfloat16),
        in_specs=[*in_specs, anywhere],
        out_specs=anywhere,
        scratch_shapes=[
            raw,
            pltpu.VMEM((HERE, HALO), jnp.bfloat16),
            pltpu.VMEM((devices, ROWS, HALF), jnp.bfloat16),
            *work_scratch,
            *[dma] * 4,
            *[dma((2,))] * 3,
        ],
        compiler_params=pltpu.CompilerParams(
            collective_id=0, has_side_effects=True, vmem_limit_bytes=60 * 2**20
        ),
        name="exchange",
    )(samples, delays, flags, taps, table, first)
    inputs = inp * HERE
    visibility = jax.ShapeDtypeStruct((CHAN, inputs, inputs), jnp.float32)
    return pl.pallas_call(
        functools.partial(correlate_kernel, segments, 1.0 / (S_DEV * segments)),
        out_shape=(visibility, visibility),
        grid=(CHAN,),
        in_specs=[pl.BlockSpec((2, devices, 2 * HERE, HALF), lambda c: (0, 0, c, 0))],
        out_specs=(
            pl.BlockSpec((1, inputs, inputs), lambda c: (c, 0, 0)),
            pl.BlockSpec((1, inputs, inputs), lambda c: (c, 0, 0)),
        ),
        compiler_params=pltpu.CompilerParams(vmem_limit_bytes=60 * 2**20),
        name="correlate",
    )(spectra)


def solution(mesh):
    segments, inp = mesh.shape["tseg"], mesh.shape["inp"]
    return jax.shard_map(
        functools.partial(per_device, segments=segments, inp=inp),
        mesh=mesh,
        in_specs=(P("inp", "tseg"), P("inp"), P("inp"), P()),
        out_specs=(P(("tseg", "inp"), None, None), P(("tseg", "inp"), None, None)),
        check_vma=False,
    )
```

```python
import functools
import math

import jax
import jax.numpy as jnp
import ml_dtypes
import numpy as np
from jax import lax
from jax.experimental import pallas as pl
from jax.experimental.pallas import tpu as pltpu
from jax.sharding import PartitionSpec as P

MESH = pl.DeviceIdType.MESH
TAPS = 16
FRAME = 1024
HALO = 23552
LANES = 128
BLOCKS = FRAME // LANES
HERE = 8
S_DEV = 256
HALF = 128
CHAN = 4
ROWS = CHAN * 2 * HERE
FIRST = HALO // FRAME + 1
RUN = FIRST + S_DEV + 1
WINDOW = HALF + TAPS
SPLIT = 103
O_STRIDE = HERE + 1
SHAPES = {64: (4, 4, 2), 4: (2, 1, 1)}


def dft_rows(nx, ny, nz):
    count = nx * ny * nz * 2
    inp = count // 2
    k = np.arange(FRAME)[None, :]
    q = np.arange(count * CHAN)[:, None]
    phase = ((q * k) % FRAME).astype(np.float64) * (2.0 * math.pi / FRAME)
    parts = np.stack([np.cos(phase), -np.sin(phase)], axis=1) / math.sqrt(FRAME)
    parts = parts.astype(np.float32).astype(ml_dtypes.bfloat16)
    parts = parts.reshape(2, nx, nz, ny // 2, 2, CHAN * 2, FRAME)
    parts = parts.transpose(1, 3, 0, 2, 4, 5, 6)
    assert inp * 2 == count
    return parts.reshape(nx * ny * nz, 2 * CHAN * 2, FRAME)


class Work:
    def __init__(self, dims, delays, flags, refs):
        self.dims = dims
        self.delays, self.flags = delays, flags
        self.rows_table, self.runs, self.tap_rows, self.delayed, self.frames, self.turned = refs
        nx, ny, nz = dims
        self.inp = nx * nz * ny
        self.tseg = lax.axis_index("tseg")
        self.here = lax.axis_index("inp")
        self.me = self.tseg * self.inp + self.here
        self.my_core = self.here % 2
        self.my_y = ((self.here // 2) % (ny // 2)) * 2 + self.tseg
        self.my_z = (self.here // ny) % nz
        self.my_x = self.here // (ny * nz)
        self.lane = lax.broadcasted_iota(jnp.int32, (HERE, LANES), 1)

    def chip_of(self, group, step):
        nx, ny, nz = self.dims
        dx = step % nx
        dy = step // nx
        dz = (group + 2 * nz + 2 * nx + 2 * ny - dx - dy) % nz
        return (self.my_x + dx) % nx, (self.my_y + dy) % ny, (self.my_z + dz) % nz

    def fetch_table(self, table, sem):
        nx, ny, nz = self.dims
        per_group = nx * ny

        @pl.loop(0, nz * per_group)
        def _(step):
            x, y, z = self.chip_of(step // per_group, step % per_group)
            pltpu.make_async_copy(
                table.at[(x * ny + y) * nz + z],
                self.rows_table.at[step // per_group, step % per_group],
                sem,
            ).start()

    def place_taps(self, taps):
        for block in range(BLOCKS):
            for p in range(TAPS):
                self.tap_rows[pl.ds((block * TAPS + p) * 8, 8), :] = jnp.broadcast_to(
                    taps[p : p + 1, block * LANES : (block + 1) * LANES], (8, LANES)
                )

    def spread(self, source, first, frame_range, unroll):
        row = lax.broadcasted_iota(jnp.int32, (HERE, LANES), 0)
        turn = jnp.zeros((HERE, LANES), jnp.int32)
        for i in range(HERE):
            turn = jnp.where(row == i, self.delays[i] % LANES, turn)
        index = (self.lane - turn + LANES) % LANES

        @pl.loop(*frame_range, unroll=unroll)
        def _(frame):
            values = source[:, pl.ds(pl.multiple_of(frame * FRAME, FRAME), FRAME)].astype(
                jnp.float32
            )
            for block in range(BLOCKS):
                moved = jnp.take_along_axis(
                    values[:, block * LANES : (block + 1) * LANES], index, axis=1
                )
                self.runs[pl.ds(block * HERE * RUN + first + frame, HERE, stride=RUN), :] = moved

    def run_half(self, half):
        base = half * HALF - (TAPS - 1)

        @pl.loop(0, HERE * BLOCKS)
        def _(run):
            i = run // BLOCKS
            block = run % BLOCKS
            delay = self.delays[i]
            keep = self.lane >= delay % LANES
            weight = self.flags[i].astype(jnp.float32)

            def start(back):
                moved = block - delay // LANES - back + 9 * BLOCKS
                return (moved % BLOCKS * HERE + i) * RUN + moved // BLOCKS - 9 + FIRST + base

            now, before = start(0), start(1)
            for f in range(0, WINDOW, 8):
                self.delayed[pl.ds(pl.multiple_of(run * WINDOW, 8) + f, 8), :] = jnp.where(
                    keep, self.runs[pl.ds(now + f, 8), :], self.runs[pl.ds(before + f, 8), :]
                )
            tap = [self.tap_rows[pl.ds((block * TAPS + p) * 8, 8), :] for p in range(TAPS)]
            total = {}
            for f in range(HALF + 8):
                values = self.delayed[pl.ds(run * WINDOW + f, 8), :]
                for p in (f % 8 + 8, f % 8):
                    s = f - p
                    if 0 <= s < HALF:
                        total[s] = tap[p] * values if p == 0 else total[s] + tap[p] * values
                if f % 16 == 15 and f > 16:
                    pair = [total.pop(f - 31), total.pop(f - 23)]
                    self.frames[
                        pl.ds(pl.multiple_of(i * HALF, HALF) + f - 31, 16),
                        pl.ds(pl.multiple_of(block * LANES, LANES), LANES),
                    ] = (jnp.concatenate(pair, axis=0) * weight).astype(jnp.bfloat16)
            pair = [total.pop(HALF - 16), total.pop(HALF - 8)]
            self.frames[
                pl.ds(pl.multiple_of(i * HALF, HALF) + HALF - 16, 16),
                pl.ds(pl.multiple_of(block * LANES, LANES), LANES),
            ] = (jnp.concatenate(pair, axis=0) * weight).astype(jnp.bfloat16)
            assert not total

    def transform(self, group):
        nx, ny, nz = self.dims
        per_group = nx * ny
        rows = self.rows_table[group].reshape(per_group * 16, FRAME)

        for pair in range(HERE // 2):
            values = self.frames[pair * 2 * HALF : (pair + 1) * 2 * HALF, :]
            spectra = lax.dot_general(
                rows, values, (((1,), (1,)), ((), ())), preferred_element_type=jnp.float32
            )
            for dest in range(2 * per_group):
                for j in range(2):
                    self.turned[
                        pl.ds(dest * 8 * O_STRIDE + pair * 2 + j, 8, stride=O_STRIDE), :
                    ] = spectra[dest * 8 : (dest + 1) * 8, j * HALF : (j + 1) * HALF]

    def pack(self, dest, target):
        for m in range(0, 8, 2):
            pair_rows = jnp.concatenate(
                [
                    self.turned[pl.ds((dest * 8 + m) * O_STRIDE, HERE), :],
                    self.turned[pl.ds((dest * 8 + m + 1) * O_STRIDE, HERE), :],
                ],
                axis=0,
            )
            target[m * 8 : (m + 2) * 8, :] = pair_rows.astype(jnp.bfloat16)

    def start_copies(self, group, chip, source, target, send_sem, recv_sem, own_sem):
        nx, ny, nz = self.dims
        x, y, z = self.chip_of(group, chip)
        for change in range(2):
            core = (self.my_core + change) % 2
            slot = source.at[(group * nx * ny + chip) * 2 + core]
            to_inp = ((x * nz + z) * (ny // 2) + y // 2) * 2 + core

            def send():
                pltpu.make_async_remote_copy(
                    src_ref=slot,
                    dst_ref=target.at[self.me],
                    send_sem=send_sem,
                    recv_sem=recv_sem,
                    device_id=(y % 2, to_inp),
                    device_id_type=MESH,
                ).start()

            if change == 0:
                own = jnp.logical_and(group == 0, chip == 0)

                @pl.when(own)
                def _():
                    pltpu.make_async_copy(slot, target.at[self.me], own_sem).start()

                pl.when(jnp.logical_not(own))(send)
            else:
                send()


def first_kernel(dims, samples, delays, flags, taps, table, ready, raw, *rest):
    refs, (load_sem, table_sem) = rest[:6], rest[6:]
    work = Work(dims, delays, flags, refs)
    nx, ny, nz = dims
    per_group = nx * ny
    part = pl.ds(SPLIT * FRAME, (S_DEV - SPLIT) * FRAME)
    load = pltpu.make_async_copy(samples.at[:, part], raw.at[:, part], load_sem)
    load.start()
    work.fetch_table(table, table_sem)
    work.place_taps(taps)
    load.wait()
    work.spread(raw, FIRST, (SPLIT, S_DEV - 1), 4)
    work.spread(raw, FIRST, (S_DEV - 1, S_DEV), 1)
    work.run_half(1)
    pltpu.make_async_copy(work.rows_table, work.rows_table, table_sem).wait()

    @pl.loop(0, nz)
    def _(group):
        work.transform(group)

        @pl.loop(0, 2 * per_group, unroll=8)
        def _(dest):
            work.pack(dest, ready.at[group * 2 * per_group + dest])


def exchange_kernel(dims, samples, delays, flags, taps, table, first, out, raw, rim, ready, *rest):
    refs, sems = rest[:6], rest[6:]
    load_sem, table_sem, rim_send, rim_recv, send_sem, recv_sem, own_sem = sems
    work = Work(dims, delays, flags, refs)
    nx, ny, nz = dims
    per_group = nx * ny
    inp = nx * ny * nz
    devices = 2 * inp
    barrier = pltpu.get_barrier_semaphore()

    @pl.loop(1, devices)
    def _(step):
        other = (work.me + step) % devices
        pl.semaphore_signal(
            barrier, inc=1, device_id=(other // inp, other % inp), device_id_type=MESH
        )

    part = pl.ds(0, S_DEV // 2 * FRAME)
    load = pltpu.make_async_copy(samples.at[:, part], raw.at[:, part], load_sem)
    load.start()
    work.fetch_table(table, table_sem)
    work.place_taps(taps)
    pl.semaphore_wait(barrier, devices - 1)
    rim_copy = pltpu.make_async_remote_copy(
        src_ref=samples.at[:, pl.ds(S_DEV * FRAME - HALO, HALO)],
        dst_ref=rim,
        send_sem=rim_send,
        recv_sem=rim_recv,
        device_id=(1 - work.tseg, work.here),
        device_id_type=MESH,
    )
    rim_copy.start()

    def start(half, group, chip):
        work.start_copies(
            group,
            chip,
            (ready, first)[half],
            out.at[half],
            send_sem.at[half],
            recv_sem.at[half],
            own_sem.at[half],
        )

    @pl.loop(0, nz)
    def _(group):
        @pl.loop(0, per_group)
        def _(chip):
            start(1, group, chip)

    load.wait()
    work.spread(raw, FIRST, (0, S_DEV // 2), 4)
    rim_copy.wait()

    @pl.when(work.tseg == 0)
    def _():
        rim[...] = jnp.zeros_like(rim)

    work.spread(rim, 1, (0, 20), 4)
    work.spread(rim, 1, (20, HALO // FRAME), 1)
    work.run_half(0)
    pltpu.make_async_copy(work.rows_table, work.rows_table, table_sem).wait()

    @pl.loop(0, nz)
    def _(group):
        work.transform(group)

        @pl.loop(0, per_group, step=4)
        def _(chips):
            for dest in range(8):
                dest = chips * 2 + dest
                work.pack(dest, ready.at[group * 2 * per_group + dest])

            @pl.loop(0, 4)
            def _(chip):
                start(0, group, chips + chip)

    for half in (1, 0):
        source = (ready, first)[half]
        pltpu.make_async_copy(
            source.at[work.my_core], out.at[half, work.me], own_sem.at[half]
        ).wait()
        sent = source.at[pl.ds(0, devices - 1)]
        pltpu.make_async_copy(sent, sent, send_sem.at[half]).wait()
        arrived = out.at[half, pl.ds(0, devices - 1)]
        pltpu.make_async_copy(arrived, arrived, recv_sem.at[half]).wait()


def correlate_kernel(segments, scale, spectra, vis_real, vis_imag):
    sources = spectra.shape[1] // segments
    inputs = sources * HERE
    real, imag = [], []
    for half in range(2):
        for segment in range(segments):
            piece = spectra[half, segment * sources : (segment + 1) * sources].astype(jnp.float32)
            real.append(piece[:, :HERE].reshape(inputs, HALF).astype(jnp.bfloat16))
            imag.append(piece[:, HERE:].reshape(inputs, HALF).astype(jnp.bfloat16))
    real = jnp.concatenate(real, axis=1)
    imag = jnp.concatenate(imag, axis=1)

    def product(a, b):
        return lax.dot_general(a, b, (((1,), (1,)), ((), ())), preferred_element_type=jnp.float32)

    middle = inputs // 2
    low, high = slice(0, middle), slice(middle, inputs)
    for rows, columns in ((low, low), (high, high), (low, high)):
        block = product(real[rows], real[columns]) + product(imag[rows], imag[columns])
        vis_real[0, rows, columns] = block * scale
        if rows != columns:
            vis_real[0, columns, rows] = block.T * scale
    cross = product(real, imag)
    vis_imag[0] = (cross - cross.T) * scale


def per_device(samples, delays, flags, taps, *, segments, inp):
    nx, nz, ny_hi = SHAPES[inp]
    dims = (nx, 2 * ny_hi, nz)
    devices = segments * inp
    per_group = nx * 2 * ny_hi
    table = jnp.asarray(dft_rows(*dims))
    anywhere = pl.BlockSpec(memory_space=pl.ANY)
    in_specs = [
        anywhere,
        pl.BlockSpec(memory_space=pltpu.SMEM),
        pl.BlockSpec(memory_space=pltpu.SMEM),
        pl.BlockSpec(memory_space=pltpu.VMEM),
        anywhere,
    ]
    work_scratch = [
        pltpu.VMEM((nz, per_group, 16, FRAME), jnp.bfloat16),
        pltpu.VMEM((BLOCKS * HERE * RUN + 8, LANES), jnp.float32),
        pltpu.VMEM((BLOCKS * TAPS * 8, LANES), jnp.float32),
        pltpu.VMEM((HERE * BLOCKS * WINDOW, LANES), jnp.float32),
        pltpu.VMEM((HERE * HALF, FRAME), jnp.bfloat16),
        pltpu.VMEM((2 * per_group * 8 * O_STRIDE, LANES), jnp.float32),
    ]
    raw = pltpu.VMEM((HERE, S_DEV * FRAME), jnp.bfloat16)
    dma = pltpu.SemaphoreType.DMA
    first = pl.pallas_call(
        functools.partial(first_kernel, dims),
        out_shape=jax.ShapeDtypeStruct((devices, ROWS, HALF), jnp.bfloat16),
        in_specs=in_specs,
        out_specs=pl.BlockSpec(memory_space=pltpu.VMEM),
        scratch_shapes=[raw, *work_scratch, dma, dma],
        compiler_params=pltpu.CompilerParams(vmem_limit_bytes=60 * 2**20),
        name="filter_first_half",
    )(samples, delays, flags, taps, table)
    spectra = pl.pallas_call(
        functools.partial(exchange_kernel, dims),
        out_shape=jax.ShapeDtypeStruct((2, devices, ROWS, HALF), jnp.bfloat16),
        in_specs=[*in_specs, anywhere],
        out_specs=anywhere,
        scratch_shapes=[
            raw,
            pltpu.VMEM((HERE, HALO), jnp.bfloat16),
            pltpu.VMEM((devices, ROWS, HALF), jnp.bfloat16),
            *work_scratch,
            *[dma] * 4,
            *[dma((2,))] * 3,
        ],
        compiler_params=pltpu.CompilerParams(
            collective_id=0, has_side_effects=True, vmem_limit_bytes=60 * 2**20
        ),
        name="exchange",
    )(samples, delays, flags, taps, table, first)
    inputs = inp * HERE
    visibility = jax.ShapeDtypeStruct((CHAN, inputs, inputs), jnp.float32)
    return pl.pallas_call(
        functools.partial(correlate_kernel, segments, 1.0 / (S_DEV * segments)),
        out_shape=(visibility, visibility),
        grid=(CHAN,),
        in_specs=[pl.BlockSpec((2, devices, 2 * HERE, HALF), lambda c: (0, 0, c, 0))],
        out_specs=(
            pl.BlockSpec((1, inputs, inputs), lambda c: (c, 0, 0)),
            pl.BlockSpec((1, inputs, inputs), lambda c: (c, 0, 0)),
        ),
        compiler_params=pltpu.CompilerParams(vmem_limit_bytes=60 * 2**20),
        name="correlate",
    )(spectra)


def solution(mesh):
    segments, inp = mesh.shape["tseg"], mesh.shape["inp"]
    return jax.shard_map(
        functools.partial(per_device, segments=segments, inp=inp),
        mesh=mesh,
        in_specs=(P("inp", "tseg"), P("inp"), P("inp"), P()),
        out_specs=(P(("tseg", "inp"), None, None), P(("tseg", "inp"), None, None)),
        check_vma=False,
    )
```

```python
import functools
import math

import jax
import jax.numpy as jnp
import ml_dtypes
import numpy as np
from jax import lax
from jax.experimental import pallas as pl
from jax.experimental.pallas import tpu as pltpu
from jax.sharding import PartitionSpec as P

MESH = pl.DeviceIdType.MESH
TAPS = 16
FRAME = 1024
HALO = 23552
LANES = 128
BLOCKS = FRAME // LANES
HERE = 8
S_DEV = 256
HALF = 128
CHAN = 4
ROWS = CHAN * 2 * HERE
FIRST = HALO // FRAME + 1
RUN = FIRST + S_DEV + 1
WINDOW = HALF + TAPS
SPLIT = 103
O_STRIDE = HERE + 1
SHAPES = {64: (4, 4, 2), 4: (2, 1, 1)}


def dft_rows(nx, ny, nz):
    count = nx * ny * nz * 2
    inp = count // 2
    k = np.arange(FRAME)[None, :]
    q = np.arange(count * CHAN)[:, None]
    phase = ((q * k) % FRAME).astype(np.float64) * (2.0 * math.pi / FRAME)
    parts = np.stack([np.cos(phase), -np.sin(phase)], axis=1) / math.sqrt(FRAME)
    parts = parts.astype(np.float32).astype(ml_dtypes.bfloat16)
    parts = parts.reshape(2, nx, nz, ny // 2, 2, CHAN * 2, FRAME)
    parts = parts.transpose(1, 3, 0, 2, 4, 5, 6)
    assert inp * 2 == count
    return parts.reshape(nx * ny * nz, 2 * CHAN * 2, FRAME)


class Work:
    def __init__(self, dims, delays, flags, refs):
        self.dims = dims
        self.delays, self.flags = delays, flags
        self.rows_table, self.runs, self.tap_rows, self.delayed, self.frames, self.turned = refs
        nx, ny, nz = dims
        self.inp = nx * nz * ny
        self.tseg = lax.axis_index("tseg")
        self.here = lax.axis_index("inp")
        self.me = self.tseg * self.inp + self.here
        self.my_core = self.here % 2
        self.my_y = ((self.here // 2) % (ny // 2)) * 2 + self.tseg
        self.my_z = (self.here // ny) % nz
        self.my_x = self.here // (ny * nz)
        self.lane = lax.broadcasted_iota(jnp.int32, (HERE, LANES), 1)

    def offset(self, group, step):
        nx, ny, nz = self.dims
        dx = step % nx
        dy = step // nx
        dz = (group + 2 * nz + 2 * nx + 2 * ny - dx - dy) % nz
        return dx, dy, dz

    def chip_at(self, dx, dy, dz):
        nx, ny, nz = self.dims
        return (self.my_x + dx) % nx, (self.my_y + dy) % ny, (self.my_z + dz) % nz

    def chip_of(self, group, step):
        return self.chip_at(*self.offset(group, step))

    def device(self, chip, core):
        nx, ny, nz = self.dims
        x, y, z = chip
        return y % 2, ((x * nz + z) * (ny // 2) + y // 2) * 2 + core

    def tied(self, group, step):
        dx, dy, dz = self.offset(group, step)
        return jnp.logical_or(jnp.logical_or(dx == 2, dy == 2), dz == 2)

    def fetch_table(self, table, sem):
        nx, ny, nz = self.dims
        per_group = nx * ny

        @pl.loop(0, nz * per_group)
        def _(step):
            x, y, z = self.chip_of(step // per_group, step % per_group)
            pltpu.make_async_copy(
                table.at[(x * ny + y) * nz + z],
                self.rows_table.at[step // per_group, step % per_group],
                sem,
            ).start()

    def place_taps(self, taps):
        for block in range(BLOCKS):
            for p in range(TAPS):
                self.tap_rows[pl.ds((block * TAPS + p) * 8, 8), :] = jnp.broadcast_to(
                    taps[p : p + 1, block * LANES : (block + 1) * LANES], (8, LANES)
                )

    def spread(self, source, first, frame_range, unroll):
        row = lax.broadcasted_iota(jnp.int32, (HERE, LANES), 0)
        turn = jnp.zeros((HERE, LANES), jnp.int32)
        for i in range(HERE):
            turn = jnp.where(row == i, self.delays[i] % LANES, turn)
        index = (self.lane - turn + LANES) % LANES

        @pl.loop(*frame_range, unroll=unroll)
        def _(frame):
            values = source[:, pl.ds(pl.multiple_of(frame * FRAME, FRAME), FRAME)].astype(
                jnp.float32
            )
            for block in range(BLOCKS):
                moved = jnp.take_along_axis(
                    values[:, block * LANES : (block + 1) * LANES], index, axis=1
                )
                self.runs[pl.ds(block * HERE * RUN + first + frame, HERE, stride=RUN), :] = moved

    def run_half(self, half, each=None):
        base = half * HALF - (TAPS - 1)

        @pl.loop(0, HERE * BLOCKS)
        def _(run):
            i = run // BLOCKS
            block = run % BLOCKS
            delay = self.delays[i]
            keep = self.lane >= delay % LANES
            weight = self.flags[i].astype(jnp.float32)

            def start(back):
                moved = block - delay // LANES - back + 9 * BLOCKS
                return (moved % BLOCKS * HERE + i) * RUN + moved // BLOCKS - 9 + FIRST + base

            now, before = start(0), start(1)
            for f in range(0, WINDOW, 8):
                self.delayed[pl.ds(pl.multiple_of(run * WINDOW, 8) + f, 8), :] = jnp.where(
                    keep, self.runs[pl.ds(now + f, 8), :], self.runs[pl.ds(before + f, 8), :]
                )
            tap = [self.tap_rows[pl.ds((block * TAPS + p) * 8, 8), :] for p in range(TAPS)]
            total = [None] * (HALF // 8)
            for f in range(HALF + 8):
                values = self.delayed[pl.ds(run * WINDOW + f, 8), :]
                for p in (f % 8 + 8, f % 8):
                    s = (f - p) // 8
                    if 0 <= s < HALF // 8:
                        term = tap[p] * values
                        total[s] = term if p == 0 else total[s] + term
            frame = jnp.concatenate(total, axis=0) * weight
            self.frames[
                pl.ds(pl.multiple_of(block * LANES, LANES), LANES),
                pl.ds(pl.multiple_of(i * HALF, HALF), HALF),
            ] = frame.T.astype(jnp.bfloat16)
            if each is not None:
                each(run)

    def transform(self, group):
        nx, ny, nz = self.dims
        per_group = nx * ny
        rows = self.rows_table[group].reshape(per_group * 16, FRAME)

        for pair in range(HERE // 2):
            values = self.frames[:, pair * 2 * HALF : (pair + 1) * 2 * HALF]
            spectra = jnp.dot(rows, values, preferred_element_type=jnp.float32)
            for dest in range(2 * per_group):
                for j in range(2):
                    self.turned[
                        pl.ds(dest * 8 * O_STRIDE + pair * 2 + j, 8, stride=O_STRIDE), :
                    ] = spectra[dest * 8 : (dest + 1) * 8, j * HALF : (j + 1) * HALF]

    def pack(self, dest, target):
        for m in range(0, 8, 2):
            pair_rows = jnp.concatenate(
                [
                    self.turned[pl.ds((dest * 8 + m) * O_STRIDE, HERE), :],
                    self.turned[pl.ds((dest * 8 + m + 1) * O_STRIDE, HERE), :],
                ],
                axis=0,
            )
            target[m * 8 : (m + 2) * 8, :] = pair_rows.astype(jnp.bfloat16)

    def send(self, source, target, device, send_sem, recv_sem):
        pltpu.make_async_remote_copy(
            src_ref=source,
            dst_ref=target,
            send_sem=send_sem,
            recv_sem=recv_sem,
            device_id=device,
            device_id_type=MESH,
        ).start()

    def pass_by(self, group, step, source, relay, send_sem, relay_sem):
        dx, dy, dz = self.offset(group, step)
        chip = self.chip_at(*[jnp.where(d == 2, 3, 0) for d in (dx, dy, dz)])
        slot = group * self.dims[0] * self.dims[1] + step
        self.send(
            source.at[slot * 2 + 1 - self.my_core],
            relay.at[slot],
            self.device(chip, self.my_core),
            send_sem,
            relay_sem.at[slot],
        )

    def pass_on(self, group, step, relay, relay_sem, target, send_sem, recv_sem):
        dx, dy, dz = self.offset(group, step)
        slot = group * self.dims[0] * self.dims[1] + step
        message = relay.at[slot]
        pltpu.make_async_copy(message, message, relay_sem.at[slot]).wait()
        origin_y, origin_inp = self.device(
            self.chip_at(*[jnp.where(d == 2, 1, 0) for d in (dx, dy, dz)]), self.my_core
        )
        chip = self.chip_at(*[jnp.where(d == 2, 3, d) for d in (dx, dy, dz)])
        self.send(
            message,
            target.at[origin_y * self.inp + origin_inp],
            self.device(chip, 1 - self.my_core),
            send_sem,
            recv_sem,
        )

    def send_direct(self, group, step, change, source, target, send_sem, recv_sem):
        core = (self.my_core + change) % 2
        slot = (group * self.dims[0] * self.dims[1] + step) * 2 + core
        chip = self.chip_of(group, step)
        self.send(
            source.at[slot], target.at[self.me], self.device(chip, core), send_sem, recv_sem
        )


def first_kernel(dims, samples, delays, flags, taps, table, ready, raw, *rest):
    refs, (load_sem, table_sem) = rest[:6], rest[6:]
    work = Work(dims, delays, flags, refs)
    nx, ny, nz = dims
    per_group = nx * ny
    part = pl.ds(SPLIT * FRAME, (S_DEV - SPLIT) * FRAME)
    load = pltpu.make_async_copy(samples.at[:, part], raw.at[:, part], load_sem)
    load.start()
    work.fetch_table(table, table_sem)
    work.place_taps(taps)
    load.wait()
    work.spread(raw, FIRST, (SPLIT, S_DEV - 1), 4)
    work.spread(raw, FIRST, (S_DEV - 1, S_DEV), 1)
    work.run_half(1)
    pltpu.make_async_copy(work.rows_table, work.rows_table, table_sem).wait()

    @pl.loop(0, nz)
    def _(group):
        work.transform(group)

        @pl.loop(0, 2 * per_group, unroll=8)
        def _(dest):
            work.pack(dest, ready.at[group * 2 * per_group + dest])


def exchange_kernel(dims, samples, delays, flags, taps, table, first, out, raw, rim, ready, relay, *rest):
    refs, sems = rest[:6], rest[6:]
    load_sem, table_sem, rim_send, rim_recv = sems[:4]
    send_sem, recv_sem, own_sem, relay_send, relay_sem = sems[4:]
    work = Work(dims, delays, flags, refs)
    nx, ny, nz = dims
    per_group = nx * ny
    inp = nx * ny * nz
    devices = 2 * inp
    ties = inp - (nx - 1) * (ny - 1) * (nz - 1)
    barrier = pltpu.get_barrier_semaphore()

    @pl.loop(1, devices)
    def _(step):
        other = (work.me + step) % devices
        pl.semaphore_signal(
            barrier, inc=1, device_id=(other // inp, other % inp), device_id_type=MESH
        )

    part = pl.ds(0, S_DEV // 2 * FRAME)
    load = pltpu.make_async_copy(samples.at[:, part], raw.at[:, part], load_sem)
    load.start()
    work.fetch_table(table, table_sem)
    work.place_taps(taps)
    pl.semaphore_wait(barrier, devices - 1)
    rim_copy = pltpu.make_async_remote_copy(
        src_ref=samples.at[:, pl.ds(S_DEV * FRAME - HALO, HALO)],
        dst_ref=rim,
        send_sem=rim_send,
        recv_sem=rim_recv,
        device_id=(1 - work.tseg, work.here),
        device_id_type=MESH,
    )
    rim_copy.start()

    def source(half):
        return (ready, first)[half]

    def pass_by(half, group, step):
        @pl.when(work.tied(group, step))
        def _():
            work.pass_by(
                group, step, source(half), relay.at[half], send_sem.at[half], relay_sem.at[half]
            )

    def send_rest(half, group, step):
        common = (source(half), out.at[half], send_sem.at[half], recv_sem.at[half])

        @pl.when(group + step > 0)
        def _():
            work.send_direct(group, step, 0, *common)

        @pl.when(group + step == 0)
        def _():
            pltpu.make_async_copy(
                source(half).at[work.my_core], out.at[half, work.me], own_sem.at[half]
            ).start()

        @pl.when(jnp.logical_not(work.tied(group, step)))
        def _():
            work.send_direct(group, step, 1, *common)

    def pass_on(half, slot):
        group, step = slot // per_group, slot % per_group

        @pl.when(work.tied(group, step))
        def _():
            work.pass_on(
                group,
                step,
                relay.at[half],
                relay_sem.at[half],
                out.at[half],
                relay_send.at[half],
                recv_sem.at[half],
            )

    @pl.loop(0, nz * per_group)
    def _(slot):
        pass_by(1, slot // per_group, slot % per_group)

    @pl.loop(0, nz * per_group)
    def _(slot):
        send_rest(1, slot // per_group, slot % per_group)

    load.wait()
    work.spread(raw, FIRST, (0, S_DEV // 2), 4)
    rim_copy.wait()

    @pl.when(work.tseg == 0)
    def _():
        rim[...] = jnp.zeros_like(rim)

    work.spread(rim, 1, (0, 20), 4)
    work.spread(rim, 1, (20, HALO // FRAME), 1)
    work.run_half(0, lambda slot: pass_on(1, slot))
    pltpu.make_async_copy(work.rows_table, work.rows_table, table_sem).wait()

    @pl.loop(0, nz)
    def _(group):
        work.transform(group)

        @pl.loop(0, per_group, step=4)
        def _(chips):
            for dest in range(8):
                dest = chips * 2 + dest
                work.pack(dest, ready.at[group * 2 * per_group + dest])

            @pl.loop(0, 4)
            def _(chip):
                pass_by(0, group, chips + chip)
                send_rest(0, group, chips + chip)

    @pl.loop(0, nz * per_group)
    def _(slot):
        pass_on(0, slot)

    for half in (1, 0):
        pltpu.make_async_copy(
            source(half).at[work.my_core], out.at[half, work.me], own_sem.at[half]
        ).wait()
        sent = source(half).at[pl.ds(0, devices - 1)]
        pltpu.make_async_copy(sent, sent, send_sem.at[half]).wait()
        passed = relay.at[half, pl.ds(0, ties)]
        pltpu.make_async_copy(passed, passed, relay_send.at[half]).wait()
        arrived = out.at[half, pl.ds(0, devices - 1)]
        pltpu.make_async_copy(arrived, arrived, recv_sem.at[half]).wait()


def correlate_kernel(segments, scale, spectra, vis_real, vis_imag):
    sources = spectra.shape[1] // segments
    inputs = sources * HERE
    real, imag = [], []
    for half in range(2):
        for segment in range(segments):
            piece = spectra[half, segment * sources : (segment + 1) * sources].astype(jnp.float32)
            real.append(piece[:, :HERE].reshape(inputs, HALF).astype(jnp.bfloat16))
            imag.append(piece[:, HERE:].reshape(inputs, HALF).astype(jnp.bfloat16))
    real = jnp.concatenate(real, axis=1)
    imag = jnp.concatenate(imag, axis=1)

    def product(a, b):
        return lax.dot_general(a, b, (((1,), (1,)), ((), ())), preferred_element_type=jnp.float32)

    middle = inputs // 2
    low, high = slice(0, middle), slice(middle, inputs)
    for rows, columns in ((low, low), (high, high), (low, high)):
        block = product(real[rows], real[columns]) + product(imag[rows], imag[columns])
        vis_real[0, rows, columns] = block * scale
        if rows != columns:
            vis_real[0, columns, rows] = block.T * scale
    cross = product(real, imag)
    vis_imag[0] = (cross - cross.T) * scale


def per_device(samples, delays, flags, taps, *, segments, inp):
    nx, nz, ny_hi = SHAPES[inp]
    dims = (nx, 2 * ny_hi, nz)
    devices = segments * inp
    per_group = nx * 2 * ny_hi
    table = jnp.asarray(dft_rows(*dims))
    anywhere = pl.BlockSpec(memory_space=pl.ANY)
    in_specs = [
        anywhere,
        pl.BlockSpec(memory_space=pltpu.SMEM),
        pl.BlockSpec(memory_space=pltpu.SMEM),
        pl.BlockSpec(memory_space=pltpu.VMEM),
        anywhere,
    ]
    work_scratch = [
        pltpu.VMEM((nz, per_group, 16, FRAME), jnp.bfloat16),
        pltpu.VMEM((BLOCKS * HERE * RUN + 8, LANES), jnp.float32),
        pltpu.VMEM((BLOCKS * TAPS * 8, LANES), jnp.float32),
        pltpu.VMEM((HERE * BLOCKS * WINDOW, LANES), jnp.float32),
        pltpu.VMEM((FRAME, HERE * HALF), jnp.bfloat16),
        pltpu.VMEM((2 * per_group * 8 * O_STRIDE, LANES), jnp.float32),
    ]
    raw = pltpu.VMEM((HERE, S_DEV * FRAME), jnp.bfloat16)
    dma = pltpu.SemaphoreType.DMA
    first = pl.pallas_call(
        functools.partial(first_kernel, dims),
        out_shape=jax.ShapeDtypeStruct((devices, ROWS, HALF), jnp.bfloat16),
        in_specs=in_specs,
        out_specs=pl.BlockSpec(memory_space=pltpu.VMEM),
        scratch_shapes=[raw, *work_scratch, dma, dma],
        compiler_params=pltpu.CompilerParams(vmem_limit_bytes=60 * 2**20),
        name="filter_first_half",
    )(samples, delays, flags, taps, table)
    spectra = pl.pallas_call(
        functools.partial(exchange_kernel, dims),
        out_shape=jax.ShapeDtypeStruct((2, devices, ROWS, HALF), jnp.bfloat16),
        in_specs=[*in_specs, anywhere],
        out_specs=anywhere,
        scratch_shapes=[
            raw,
            pltpu.VMEM((HERE, HALO), jnp.bfloat16),
            pltpu.VMEM((devices, ROWS, HALF), jnp.bfloat16),
            pltpu.VMEM((2, nz * per_group, ROWS, HALF), jnp.bfloat16),
            *work_scratch,
            *[dma] * 4,
            *[dma((2,))] * 4,
            dma((2, nz * per_group)),
        ],
        compiler_params=pltpu.CompilerParams(
            collective_id=0, has_side_effects=True, vmem_limit_bytes=60 * 2**20
        ),
        name="exchange",
    )(samples, delays, flags, taps, table, first)
    inputs = inp * HERE
    visibility = jax.ShapeDtypeStruct((CHAN, inputs, inputs), jnp.float32)
    return pl.pallas_call(
        functools.partial(correlate_kernel, segments, 1.0 / (S_DEV * segments)),
        out_shape=(visibility, visibility),
        grid=(CHAN,),
        in_specs=[pl.BlockSpec((2, devices, 2 * HERE, HALF), lambda c: (0, 0, c, 0))],
        out_specs=(
            pl.BlockSpec((1, inputs, inputs), lambda c: (c, 0, 0)),
            pl.BlockSpec((1, inputs, inputs), lambda c: (c, 0, 0)),
        ),
        compiler_params=pltpu.CompilerParams(vmem_limit_bytes=60 * 2**20),
        name="correlate",
    )(spectra)


def solution(mesh):
    segments, inp = mesh.shape["tseg"], mesh.shape["inp"]
    return jax.shard_map(
        functools.partial(per_device, segments=segments, inp=inp),
        mesh=mesh,
        in_specs=(P("inp", "tseg"), P("inp"), P("inp"), P()),
        out_specs=(P(("tseg", "inp"), None, None), P(("tseg", "inp"), None, None)),
        check_vma=False,
    )
```

```python
import functools
import math

import jax
import jax.numpy as jnp
import ml_dtypes
import numpy as np
from jax import lax
from jax.experimental import pallas as pl
from jax.experimental.pallas import tpu as pltpu
from jax.sharding import PartitionSpec as P

MESH = pl.DeviceIdType.MESH
TAPS = 16
FRAME = 1024
HALO = 23552
LANES = 128
BLOCKS = FRAME // LANES
HERE = 8
S_DEV = 256
HALF = 128
CHAN = 4
ROWS = CHAN * 2 * HERE
FIRST = HALO // FRAME + 1
RUN = FIRST + S_DEV + 1
WINDOW = HALF + TAPS
SPLIT = 103
O_STRIDE = HERE + 1
SHAPES = {64: (4, 4, 2), 4: (2, 1, 1)}


def dft_rows(nx, ny, nz):
    count = nx * ny * nz * 2
    inp = count // 2
    k = np.arange(FRAME)[None, :]
    q = np.arange(count * CHAN)[:, None]
    phase = ((q * k) % FRAME).astype(np.float64) * (2.0 * math.pi / FRAME)
    parts = np.stack([np.cos(phase), -np.sin(phase)], axis=1) / math.sqrt(FRAME)
    parts = parts.astype(np.float32).astype(ml_dtypes.bfloat16)
    parts = parts.reshape(2, nx, nz, ny // 2, 2, CHAN * 2, FRAME)
    parts = parts.transpose(1, 3, 0, 2, 4, 5, 6)
    assert inp * 2 == count
    return parts.reshape(nx * ny * nz, 2 * CHAN * 2, FRAME)


class Work:
    def __init__(self, dims, delays, flags, refs):
        self.dims = dims
        self.delays, self.flags = delays, flags
        self.rows_table, self.runs, self.tap_rows, self.delayed, self.frames, self.turned = refs
        nx, ny, nz = dims
        self.inp = nx * nz * ny
        self.tseg = lax.axis_index("tseg")
        self.here = lax.axis_index("inp")
        self.me = self.tseg * self.inp + self.here
        self.my_core = self.here % 2
        self.my_y = ((self.here // 2) % (ny // 2)) * 2 + self.tseg
        self.my_z = (self.here // ny) % nz
        self.my_x = self.here // (ny * nz)
        self.lane = lax.broadcasted_iota(jnp.int32, (HERE, LANES), 1)

    def offset(self, group, step):
        nx, ny, nz = self.dims
        dx = step % nx
        dy = step // nx
        dz = (group + 2 * nz + 2 * nx + 2 * ny - dx - dy) % nz
        return dx, dy, dz

    def chip_at(self, dx, dy, dz):
        nx, ny, nz = self.dims
        return (self.my_x + dx) % nx, (self.my_y + dy) % ny, (self.my_z + dz) % nz

    def chip_of(self, group, step):
        return self.chip_at(*self.offset(group, step))

    def device(self, chip, core):
        nx, ny, nz = self.dims
        x, y, z = chip
        return y % 2, ((x * nz + z) * (ny // 2) + y // 2) * 2 + core

    def tied(self, group, step):
        dx, dy, dz = self.offset(group, step)
        return jnp.logical_or(jnp.logical_or(dx == 2, dy == 2), dz == 2)

    def fetch_table(self, table, sem):
        nx, ny, nz = self.dims
        per_group = nx * ny

        @pl.loop(0, nz * per_group)
        def _(step):
            x, y, z = self.chip_of(step // per_group, step % per_group)
            pltpu.make_async_copy(
                table.at[(x * ny + y) * nz + z],
                self.rows_table.at[step // per_group, step % per_group],
                sem,
            ).start()

    def place_taps(self, taps):
        for block in range(BLOCKS):
            for p in range(TAPS):
                self.tap_rows[pl.ds((block * TAPS + p) * 8, 8), :] = jnp.broadcast_to(
                    taps[p : p + 1, block * LANES : (block + 1) * LANES], (8, LANES)
                )

    def spread(self, source, first, frame_range, unroll):
        row = lax.broadcasted_iota(jnp.int32, (HERE, LANES), 0)
        turn = jnp.zeros((HERE, LANES), jnp.int32)
        for i in range(HERE):
            turn = jnp.where(row == i, self.delays[i] % LANES, turn)
        index = (self.lane - turn + LANES) % LANES

        @pl.loop(*frame_range, unroll=unroll)
        def _(frame):
            values = source[:, pl.ds(pl.multiple_of(frame * FRAME, FRAME), FRAME)].astype(
                jnp.float32
            )
            for block in range(BLOCKS):
                moved = jnp.take_along_axis(
                    values[:, block * LANES : (block + 1) * LANES], index, axis=1
                )
                self.runs[pl.ds(block * HERE * RUN + first + frame, HERE, stride=RUN), :] = moved

    def run_half(self, half):
        base = half * HALF - (TAPS - 1)

        @pl.loop(0, HERE * BLOCKS)
        def _(run):
            i = run // BLOCKS
            block = run % BLOCKS
            delay = self.delays[i]
            keep = self.lane >= delay % LANES
            weight = self.flags[i].astype(jnp.float32)

            def start(back):
                moved = block - delay // LANES - back + 9 * BLOCKS
                return (moved % BLOCKS * HERE + i) * RUN + moved // BLOCKS - 9 + FIRST + base

            now, before = start(0), start(1)
            for f in range(0, WINDOW, 8):
                self.delayed[pl.ds(pl.multiple_of(run * WINDOW, 8) + f, 8), :] = jnp.where(
                    keep, self.runs[pl.ds(now + f, 8), :], self.runs[pl.ds(before + f, 8), :]
                )
            tap = [self.tap_rows[pl.ds((block * TAPS + p) * 8, 8), :] for p in range(TAPS)]
            total = {}
            for f in range(HALF + 8):
                values = self.delayed[pl.ds(run * WINDOW + f, 8), :]
                for p in (f % 8 + 8, f % 8):
                    s = f - p
                    if 0 <= s < HALF:
                        total[s] = tap[p] * values if p == 0 else total[s] + tap[p] * values
                if f % 16 == 15 and f > 16:
                    pair = [total.pop(f - 31), total.pop(f - 23)]
                    self.frames[
                        pl.ds(pl.multiple_of(i * HALF, HALF) + f - 31, 16),
                        pl.ds(pl.multiple_of(block * LANES, LANES), LANES),
                    ] = (jnp.concatenate(pair, axis=0) * weight).astype(jnp.bfloat16)
            pair = [total.pop(HALF - 16), total.pop(HALF - 8)]
            self.frames[
                pl.ds(pl.multiple_of(i * HALF, HALF) + HALF - 16, 16),
                pl.ds(pl.multiple_of(block * LANES, LANES), LANES),
            ] = (jnp.concatenate(pair, axis=0) * weight).astype(jnp.bfloat16)
            assert not total

    def transform(self, group):
        nx, ny, nz = self.dims
        per_group = nx * ny
        rows = self.rows_table[group].reshape(per_group * 16, FRAME)

        for pair in range(HERE // 2):
            values = self.frames[pair * 2 * HALF : (pair + 1) * 2 * HALF, :]
            spectra = lax.dot_general(
                rows, values, (((1,), (1,)), ((), ())), preferred_element_type=jnp.float32
            )
            for dest in range(2 * per_group):
                for j in range(2):
                    self.turned[
                        pl.ds(dest * 8 * O_STRIDE + pair * 2 + j, 8, stride=O_STRIDE), :
                    ] = spectra[dest * 8 : (dest + 1) * 8, j * HALF : (j + 1) * HALF]

    def pack(self, dest, target):
        for m in range(0, 8, 2):
            pair_rows = jnp.concatenate(
                [
                    self.turned[pl.ds((dest * 8 + m) * O_STRIDE, HERE), :],
                    self.turned[pl.ds((dest * 8 + m + 1) * O_STRIDE, HERE), :],
                ],
                axis=0,
            )
            target[m * 8 : (m + 2) * 8, :] = pair_rows.astype(jnp.bfloat16)

    def send(self, source, target, device, send_sem, recv_sem):
        pltpu.make_async_remote_copy(
            src_ref=source,
            dst_ref=target,
            send_sem=send_sem,
            recv_sem=recv_sem,
            device_id=device,
            device_id_type=MESH,
        ).start()

    def pass_by(self, group, step, change, source, relay, send_sem, relay_sem):
        way = (1, 3)[change]
        chip = self.chip_at(*[jnp.where(d == 2, way, 0) for d in self.offset(group, step)])
        slot = (group * self.dims[0] * self.dims[1] + step) * 2
        self.send(
            source.at[slot + (self.my_core + change) % 2],
            relay.at[slot + change],
            self.device(chip, self.my_core),
            send_sem,
            relay_sem.at[slot + change],
        )

    def pass_on(self, group, step, change, relay, relay_sem, target, send_sem, recv_sem):
        way = (1, 3)[change]
        offset = self.offset(group, step)
        slot = (group * self.dims[0] * self.dims[1] + step) * 2 + change
        message = relay.at[slot]
        pltpu.make_async_copy(message, message, relay_sem.at[slot]).wait()
        origin_y, origin_inp = self.device(
            self.chip_at(*[jnp.where(d == 2, 4 - way, 0) for d in offset]), self.my_core
        )
        chip = self.chip_at(*[jnp.where(d == 2, way, d) for d in offset])
        self.send(
            message,
            target.at[origin_y * self.inp + origin_inp],
            self.device(chip, (self.my_core + change) % 2),
            send_sem,
            recv_sem,
        )

    def send_direct(self, group, step, change, source, target, send_sem, recv_sem):
        core = (self.my_core + change) % 2
        slot = (group * self.dims[0] * self.dims[1] + step) * 2 + core
        chip = self.chip_of(group, step)
        self.send(
            source.at[slot], target.at[self.me], self.device(chip, core), send_sem, recv_sem
        )


def exchange_kernel(dims, samples, delays, flags, taps, table, out, raw, rim, ready, *rest):
    relay, refs, sems = rest[0], rest[1:7], rest[7:]
    load_sem, table_sem, rim_send, rim_recv, send_sem, recv_sem, own_sem = sems[:7]
    relay_send, relay_sem = sems[7:]
    work = Work(dims, delays, flags, refs)
    nx, ny, nz = dims
    per_group = nx * ny
    inp = nx * ny * nz
    devices = 2 * inp
    ties = 2 * (inp - (nx - 1) * (ny - 1) * (nz - 1))

    def load(first, count, sem):
        part = pl.ds(first * FRAME, count * FRAME)
        copy = pltpu.make_async_copy(samples.at[:, part], raw.at[:, part], sem)
        copy.start()
        return copy

    late_load = load(SPLIT, S_DEV - SPLIT, load_sem.at[0])
    early_load = load(0, SPLIT, load_sem.at[1])
    barrier = pltpu.get_barrier_semaphore()

    @pl.loop(1, devices)
    def _(step):
        other = (work.me + step) % devices
        pl.semaphore_signal(
            barrier, inc=1, device_id=(other // inp, other % inp), device_id_type=MESH
        )

    work.fetch_table(table, table_sem)
    work.place_taps(taps)

    def pass_by(half, group, step):
        @pl.when(work.tied(group, step))
        def _():
            for change in range(2):
                work.pass_by(
                    group,
                    step,
                    change,
                    ready.at[half],
                    relay.at[half],
                    send_sem.at[half],
                    relay_sem.at[half],
                )

    def pass_on(half, group, step):
        @pl.when(work.tied(group, step))
        def _():
            for change in range(2):
                work.pass_on(
                    group,
                    step,
                    change,
                    relay.at[half],
                    relay_sem.at[half],
                    out.at[half],
                    relay_send.at[half],
                    recv_sem.at[half],
                )

    def send_direct(half, group, step):
        common = (ready.at[half], out.at[half], send_sem.at[half], recv_sem.at[half])

        @pl.when(group + step > 0)
        def _():
            work.send_direct(group, step, 0, *common)

        @pl.when(group + step == 0)
        def _():
            pltpu.make_async_copy(
                ready.at[half, work.my_core], out.at[half, work.me], own_sem.at[half]
            ).start()

        work.send_direct(group, step, 1, *common)

    def transform_half(half):
        @pl.loop(0, nz)
        def _(group):
            work.transform(group)

            @pl.loop(0, per_group, step=4)
            def _(chips):
                for dest in range(8):
                    dest = chips * 2 + dest
                    work.pack(dest, ready.at[half, group * 2 * per_group + dest])

                @pl.loop(0, 4)
                def _(chip):
                    pass_by(half, group, chips + chip)

                @pl.loop(0, 4)
                def _(chip):
                    step = chips + chip

                    @pl.when(jnp.logical_not(work.tied(group, step)))
                    def _():
                        send_direct(half, group, step)

            if half == 0:

                @pl.loop(0, per_group)
                def _(step):
                    pass_on(1, group, step)

    late_load.wait()
    work.spread(raw, FIRST, (SPLIT, S_DEV - 1), 4)
    work.spread(raw, FIRST, (S_DEV - 1, S_DEV), 1)
    pl.semaphore_wait(barrier, devices - 1)
    rim_copy = pltpu.make_async_remote_copy(
        src_ref=samples.at[:, pl.ds(S_DEV * FRAME - HALO, HALO)],
        dst_ref=rim,
        send_sem=rim_send,
        recv_sem=rim_recv,
        device_id=(1 - work.tseg, work.here),
        device_id_type=MESH,
    )
    rim_copy.start()
    work.run_half(1)
    pltpu.make_async_copy(work.rows_table, work.rows_table, table_sem).wait()
    transform_half(1)

    early_load.wait()
    work.spread(raw, FIRST, (0, SPLIT - 3), 4)
    work.spread(raw, FIRST, (SPLIT - 3, SPLIT), 1)
    rim_copy.wait()

    @pl.when(work.tseg == 0)
    def _():
        rim[...] = jnp.zeros_like(rim)

    work.spread(rim, 1, (0, 20), 4)
    work.spread(rim, 1, (20, HALO // FRAME), 1)
    work.run_half(0)
    transform_half(0)

    @pl.loop(0, nz)
    def _(group):
        @pl.loop(0, per_group)
        def _(step):
            pass_on(0, group, step)

    for half in (1, 0):
        pltpu.make_async_copy(
            ready.at[half, work.my_core], out.at[half, work.me], own_sem.at[half]
        ).wait()
        sent = ready.at[half, pl.ds(0, devices - 1)]
        pltpu.make_async_copy(sent, sent, send_sem.at[half]).wait()
        passed = relay.at[half, pl.ds(0, ties)]
        pltpu.make_async_copy(passed, passed, relay_send.at[half]).wait()
        arrived = out.at[half, pl.ds(0, devices - 1)]
        pltpu.make_async_copy(arrived, arrived, recv_sem.at[half]).wait()


def correlate_kernel(segments, scale, spectra, vis_real, vis_imag):
    sources = spectra.shape[1] // segments
    inputs = sources * HERE
    real, imag = [], []
    for half in range(2):
        for segment in range(segments):
            piece = spectra[half, segment * sources : (segment + 1) * sources].astype(jnp.float32)
            real.append(piece[:, :HERE].reshape(inputs, HALF).astype(jnp.bfloat16))
            imag.append(piece[:, HERE:].reshape(inputs, HALF).astype(jnp.bfloat16))
    real = jnp.concatenate(real, axis=1)
    imag = jnp.concatenate(imag, axis=1)

    def product(a, b):
        return lax.dot_general(a, b, (((1,), (1,)), ((), ())), preferred_element_type=jnp.float32)

    middle = inputs // 2
    low, high = slice(0, middle), slice(middle, inputs)
    for rows, columns in ((low, low), (high, high), (low, high)):
        block = product(real[rows], real[columns]) + product(imag[rows], imag[columns])
        vis_real[0, rows, columns] = block * scale
        if rows != columns:
            vis_real[0, columns, rows] = block.T * scale
    cross = product(real, imag)
    vis_imag[0] = (cross - cross.T) * scale


def per_device(samples, delays, flags, taps, *, segments, inp):
    nx, nz, ny_hi = SHAPES[inp]
    dims = (nx, 2 * ny_hi, nz)
    devices = segments * inp
    per_group = nx * 2 * ny_hi
    table = jnp.asarray(dft_rows(*dims))
    anywhere = pl.BlockSpec(memory_space=pl.ANY)
    in_specs = [
        anywhere,
        pl.BlockSpec(memory_space=pltpu.SMEM),
        pl.BlockSpec(memory_space=pltpu.SMEM),
        pl.BlockSpec(memory_space=pltpu.VMEM),
        anywhere,
    ]
    work_scratch = [
        pltpu.VMEM((nz, per_group, 16, FRAME), jnp.bfloat16),
        pltpu.VMEM((BLOCKS * HERE * RUN + 8, LANES), jnp.float32),
        pltpu.VMEM((BLOCKS * TAPS * 8, LANES), jnp.float32),
        pltpu.VMEM((HERE * BLOCKS * WINDOW, LANES), jnp.float32),
        pltpu.VMEM((HERE * HALF, FRAME), jnp.bfloat16),
        pltpu.VMEM((2 * per_group * 8 * O_STRIDE, LANES), jnp.float32),
    ]
    raw = pltpu.VMEM((HERE, S_DEV * FRAME), jnp.bfloat16)
    dma = pltpu.SemaphoreType.DMA
    spectra = pl.pallas_call(
        functools.partial(exchange_kernel, dims),
        out_shape=jax.ShapeDtypeStruct((2, devices, ROWS, HALF), jnp.bfloat16),
        in_specs=in_specs,
        out_specs=anywhere,
        scratch_shapes=[
            raw,
            pltpu.VMEM((HERE, HALO), jnp.bfloat16),
            pltpu.VMEM((2, devices, ROWS, HALF), jnp.bfloat16),
            pltpu.VMEM((2, devices, ROWS, HALF), jnp.bfloat16),
            *work_scratch,
            dma((2,)),
            *[dma] * 3,
            *[dma((2,))] * 4,
            dma((2, devices)),
        ],
        compiler_params=pltpu.CompilerParams(
            collective_id=0, has_side_effects=True, vmem_limit_bytes=60 * 2**20
        ),
        name="exchange",
    )(samples, delays, flags, taps, table)
    inputs = inp * HERE
    visibility = jax.ShapeDtypeStruct((CHAN, inputs, inputs), jnp.float32)
    return pl.pallas_call(
        functools.partial(correlate_kernel, segments, 1.0 / (S_DEV * segments)),
        out_shape=(visibility, visibility),
        grid=(CHAN,),
        in_specs=[pl.BlockSpec((2, devices, 2 * HERE, HALF), lambda c: (0, 0, c, 0))],
        out_specs=(
            pl.BlockSpec((1, inputs, inputs), lambda c: (c, 0, 0)),
            pl.BlockSpec((1, inputs, inputs), lambda c: (c, 0, 0)),
        ),
        compiler_params=pltpu.CompilerParams(vmem_limit_bytes=60 * 2**20),
        name="correlate",
    )(spectra)


def solution(mesh):
    segments, inp = mesh.shape["tseg"], mesh.shape["inp"]
    return jax.shard_map(
        functools.partial(per_device, segments=segments, inp=inp),
        mesh=mesh,
        in_specs=(P("inp", "tseg"), P("inp"), P("inp"), P()),
        out_specs=(P(("tseg", "inp"), None, None), P(("tseg", "inp"), None, None)),
        check_vma=False,
    )
```

```python
import functools
import math

import jax
import jax.numpy as jnp
import ml_dtypes
import numpy as np
from jax import lax
from jax.experimental import pallas as pl
from jax.experimental.pallas import tpu as pltpu
from jax.sharding import PartitionSpec as P

MESH = pl.DeviceIdType.MESH
TAPS = 16
FRAME = 1024
HALO = 23552
LANES = 128
BLOCKS = FRAME // LANES
HERE = 8
S_DEV = 256
HALF = 128
CHAN = 4
ROWS = CHAN * 2 * HERE
FIRST = HALO // FRAME + 1
RUN = FIRST + S_DEV + 1
WINDOW = HALF + TAPS
SPLIT = 103
O_STRIDE = HERE + 1
SHAPES = {64: (4, 4, 2), 4: (2, 1, 1)}


def dft_rows(nx, ny, nz):
    count = nx * ny * nz * 2
    inp = count // 2
    k = np.arange(FRAME)[None, :]
    q = np.arange(count * CHAN)[:, None]
    phase = ((q * k) % FRAME).astype(np.float64) * (2.0 * math.pi / FRAME)
    parts = np.stack([np.cos(phase), -np.sin(phase)], axis=1) / math.sqrt(FRAME)
    parts = parts.astype(np.float32).astype(ml_dtypes.bfloat16)
    parts = parts.reshape(2, nx, nz, ny // 2, 2, CHAN * 2, FRAME)
    parts = parts.transpose(1, 3, 0, 2, 4, 5, 6)
    assert inp * 2 == count
    return parts.reshape(nx * ny * nz, 2 * CHAN * 2, FRAME)


class Work:
    def __init__(self, dims, delays, flags, refs):
        self.dims = dims
        self.delays, self.flags = delays, flags
        self.rows_table, self.runs, self.tap_rows, self.delayed, self.frames, self.turned = refs
        nx, ny, nz = dims
        self.inp = nx * nz * ny
        self.tseg = lax.axis_index("tseg")
        self.here = lax.axis_index("inp")
        self.me = self.tseg * self.inp + self.here
        self.my_core = self.here % 2
        self.my_y = ((self.here // 2) % (ny // 2)) * 2 + self.tseg
        self.my_z = (self.here // ny) % nz
        self.my_x = self.here // (ny * nz)
        self.lane = lax.broadcasted_iota(jnp.int32, (HERE, LANES), 1)

    def offset(self, group, step):
        nx, ny, nz = self.dims
        dx = step % nx
        return dx, (dx + step // nx) % ny, (dx + group) % nz

    def chip_at(self, dx, dy, dz):
        nx, ny, nz = self.dims
        return (self.my_x + dx) % nx, (self.my_y + dy) % ny, (self.my_z + dz) % nz

    def chip_of(self, group, step):
        return self.chip_at(*self.offset(group, step))

    def device(self, chip, core):
        nx, ny, nz = self.dims
        x, y, z = chip
        return y % 2, ((x * nz + z) * (ny // 2) + y // 2) * 2 + core

    def tied(self, group, step):
        dx, dy, dz = self.offset(group, step)
        return jnp.logical_or(jnp.logical_or(dx == 2, dy == 2), dz == 2)

    def fetch_table(self, table, sem):
        nx, ny, nz = self.dims
        per_group = nx * ny

        @pl.loop(0, nz * per_group)
        def _(step):
            x, y, z = self.chip_of(step // per_group, step % per_group)
            pltpu.make_async_copy(
                table.at[(x * ny + y) * nz + z],
                self.rows_table.at[step // per_group, step % per_group],
                sem,
            ).start()

    def place_taps(self, taps):
        for block in range(BLOCKS):
            for p in range(TAPS):
                self.tap_rows[pl.ds((block * TAPS + p) * 8, 8), :] = jnp.broadcast_to(
                    taps[p : p + 1, block * LANES : (block + 1) * LANES], (8, LANES)
                )

    def spread(self, source, first, frame_range, unroll):
        row = lax.broadcasted_iota(jnp.int32, (HERE, LANES), 0)
        turn = jnp.zeros((HERE, LANES), jnp.int32)
        for i in range(HERE):
            turn = jnp.where(row == i, self.delays[i] % LANES, turn)
        index = (self.lane - turn + LANES) % LANES

        @pl.loop(*frame_range, unroll=unroll)
        def _(frame):
            values = source[:, pl.ds(pl.multiple_of(frame * FRAME, FRAME), FRAME)].astype(
                jnp.float32
            )
            for block in range(BLOCKS):
                moved = jnp.take_along_axis(
                    values[:, block * LANES : (block + 1) * LANES], index, axis=1
                )
                self.runs[pl.ds(block * HERE * RUN + first + frame, HERE, stride=RUN), :] = moved

    def run_half(self, half):
        base = half * HALF - (TAPS - 1)

        @pl.loop(0, HERE * BLOCKS)
        def _(run):
            i = run // BLOCKS
            block = run % BLOCKS
            delay = self.delays[i]
            keep = self.lane >= delay % LANES
            weight = self.flags[i].astype(jnp.float32)

            def start(back):
                moved = block - delay // LANES - back + 9 * BLOCKS
                return (moved % BLOCKS * HERE + i) * RUN + moved // BLOCKS - 9 + FIRST + base

            now, before = start(0), start(1)
            for f in range(0, WINDOW, 8):
                self.delayed[pl.ds(pl.multiple_of(run * WINDOW, 8) + f, 8), :] = jnp.where(
                    keep, self.runs[pl.ds(now + f, 8), :], self.runs[pl.ds(before + f, 8), :]
                )
            tap = [self.tap_rows[pl.ds((block * TAPS + p) * 8, 8), :] for p in range(TAPS)]
            total = {}
            for f in range(HALF + 8):
                values = self.delayed[pl.ds(run * WINDOW + f, 8), :]
                for p in (f % 8 + 8, f % 8):
                    s = f - p
                    if 0 <= s < HALF:
                        total[s] = tap[p] * values if p == 0 else total[s] + tap[p] * values
                if f % 16 == 15 and f > 16:
                    pair = [total.pop(f - 31), total.pop(f - 23)]
                    self.frames[
                        pl.ds(pl.multiple_of(i * HALF, HALF) + f - 31, 16),
                        pl.ds(pl.multiple_of(block * LANES, LANES), LANES),
                    ] = (jnp.concatenate(pair, axis=0) * weight).astype(jnp.bfloat16)
            pair = [total.pop(HALF - 16), total.pop(HALF - 8)]
            self.frames[
                pl.ds(pl.multiple_of(i * HALF, HALF) + HALF - 16, 16),
                pl.ds(pl.multiple_of(block * LANES, LANES), LANES),
            ] = (jnp.concatenate(pair, axis=0) * weight).astype(jnp.bfloat16)
            assert not total

    def transform(self, group):
        nx, ny, nz = self.dims
        per_group = nx * ny
        rows = self.rows_table[group].reshape(per_group * 16, FRAME)

        for pair in range(HERE // 2):
            values = self.frames[pair * 2 * HALF : (pair + 1) * 2 * HALF, :]
            spectra = lax.dot_general(
                rows, values, (((1,), (1,)), ((), ())), preferred_element_type=jnp.float32
            )
            for dest in range(2 * per_group):
                for j in range(2):
                    self.turned[
                        pl.ds(dest * 8 * O_STRIDE + pair * 2 + j, 8, stride=O_STRIDE), :
                    ] = spectra[dest * 8 : (dest + 1) * 8, j * HALF : (j + 1) * HALF]

    def pack(self, dest, target):
        for m in range(0, 8, 2):
            pair_rows = jnp.concatenate(
                [
                    self.turned[pl.ds((dest * 8 + m) * O_STRIDE, HERE), :],
                    self.turned[pl.ds((dest * 8 + m + 1) * O_STRIDE, HERE), :],
                ],
                axis=0,
            )
            target[m * 8 : (m + 2) * 8, :] = pair_rows.astype(jnp.bfloat16)

    def send(self, source, target, device, send_sem, recv_sem):
        pltpu.make_async_remote_copy(
            src_ref=source,
            dst_ref=target,
            send_sem=send_sem,
            recv_sem=recv_sem,
            device_id=device,
            device_id_type=MESH,
        ).start()

    def pass_by(self, group, step, change, source, relay, send_sem, relay_sem):
        way = (1, 3)[change]
        chip = self.chip_at(*[jnp.where(d == 2, way, 0) for d in self.offset(group, step)])
        slot = (group * self.dims[0] * self.dims[1] + step) * 2
        self.send(
            source.at[slot + (self.my_core + change) % 2],
            relay.at[slot + change],
            self.device(chip, self.my_core),
            send_sem,
            relay_sem.at[slot + change],
        )

    def pass_on(self, group, step, change, relay, relay_sem, target, send_sem, recv_sem):
        way = (1, 3)[change]
        offset = self.offset(group, step)
        slot = (group * self.dims[0] * self.dims[1] + step) * 2 + change
        message = relay.at[slot]
        pltpu.make_async_copy(message, message, relay_sem.at[slot]).wait()
        origin_y, origin_inp = self.device(
            self.chip_at(*[jnp.where(d == 2, 4 - way, 0) for d in offset]), self.my_core
        )
        chip = self.chip_at(*[jnp.where(d == 2, way, d) for d in offset])
        self.send(
            message,
            target.at[origin_y * self.inp + origin_inp],
            self.device(chip, (self.my_core + change) % 2),
            send_sem,
            recv_sem,
        )

    def send_direct(self, group, step, change, source, target, send_sem, recv_sem):
        core = (self.my_core + change) % 2
        slot = (group * self.dims[0] * self.dims[1] + step) * 2 + core
        chip = self.chip_of(group, step)
        self.send(
            source.at[slot], target.at[self.me], self.device(chip, core), send_sem, recv_sem
        )


def exchange_kernel(dims, samples, delays, flags, taps, table, out, raw, rim, ready, *rest):
    relay, refs, sems = rest[0], rest[1:7], rest[7:]
    load_sem, table_sem, rim_send, rim_recv, send_sem, recv_sem, own_sem = sems[:7]
    relay_send, relay_sem = sems[7:]
    work = Work(dims, delays, flags, refs)
    nx, ny, nz = dims
    per_group = nx * ny
    inp = nx * ny * nz
    devices = 2 * inp
    ties = 2 * (inp - (nx - 1) * (ny - 1) * (nz - 1))

    def load(first, count, sem):
        part = pl.ds(first * FRAME, count * FRAME)
        copy = pltpu.make_async_copy(samples.at[:, part], raw.at[:, part], sem)
        copy.start()
        return copy

    late_load = load(SPLIT, S_DEV - SPLIT, load_sem.at[0])
    early_load = load(0, SPLIT, load_sem.at[1])
    barrier = pltpu.get_barrier_semaphore()

    @pl.loop(1, devices)
    def _(step):
        other = (work.me + step) % devices
        pl.semaphore_signal(
            barrier, inc=1, device_id=(other // inp, other % inp), device_id_type=MESH
        )

    work.fetch_table(table, table_sem)
    work.place_taps(taps)

    def pass_by(half, group, step):
        @pl.when(work.tied(group, step))
        def _():
            for change in range(2):
                work.pass_by(
                    group,
                    step,
                    change,
                    ready.at[half],
                    relay.at[half],
                    send_sem.at[half],
                    relay_sem.at[half],
                )

    def pass_on(half, group, step):
        @pl.when(work.tied(group, step))
        def _():
            for change in range(2):
                work.pass_on(
                    group,
                    step,
                    change,
                    relay.at[half],
                    relay_sem.at[half],
                    out.at[half],
                    relay_send.at[half],
                    recv_sem.at[half],
                )

    def send_direct(half, group, step):
        common = (ready.at[half], out.at[half], send_sem.at[half], recv_sem.at[half])

        @pl.when(group + step > 0)
        def _():
            work.send_direct(group, step, 0, *common)

        @pl.when(group + step == 0)
        def _():
            pltpu.make_async_copy(
                ready.at[half, work.my_core], out.at[half, work.me], own_sem.at[half]
            ).start()

        work.send_direct(group, step, 1, *common)

    def transform_half(half):
        @pl.loop(0, nz)
        def _(group):
            work.transform(group)

            @pl.loop(0, per_group, step=4)
            def _(chips):
                for dest in range(8):
                    dest = chips * 2 + dest
                    work.pack(dest, ready.at[half, group * 2 * per_group + dest])

                @pl.loop(0, 4)
                def _(chip):
                    pass_by(half, group, chips + chip)

                @pl.loop(0, 4)
                def _(chip):
                    step = chips + chip

                    @pl.when(jnp.logical_not(work.tied(group, step)))
                    def _():
                        send_direct(half, group, step)

            if half == 0:

                @pl.loop(0, per_group)
                def _(step):
                    pass_on(1, group, step)

    late_load.wait()
    work.spread(raw, FIRST, (SPLIT, S_DEV - 1), 4)
    work.spread(raw, FIRST, (S_DEV - 1, S_DEV), 1)
    pl.semaphore_wait(barrier, devices - 1)
    rim_copy = pltpu.make_async_remote_copy(
        src_ref=samples.at[:, pl.ds(S_DEV * FRAME - HALO, HALO)],
        dst_ref=rim,
        send_sem=rim_send,
        recv_sem=rim_recv,
        device_id=(1 - work.tseg, work.here),
        device_id_type=MESH,
    )
    rim_copy.start()
    work.run_half(1)
    pltpu.make_async_copy(work.rows_table, work.rows_table, table_sem).wait()
    transform_half(1)

    early_load.wait()
    work.spread(raw, FIRST, (0, SPLIT - 3), 4)
    work.spread(raw, FIRST, (SPLIT - 3, SPLIT), 1)
    rim_copy.wait()

    @pl.when(work.tseg == 0)
    def _():
        rim[...] = jnp.zeros_like(rim)

    work.spread(rim, 1, (0, 20), 4)
    work.spread(rim, 1, (20, HALO // FRAME), 1)
    work.run_half(0)
    transform_half(0)

    @pl.loop(0, nz)
    def _(group):
        @pl.loop(0, per_group)
        def _(step):
            pass_on(0, group, step)

    for half in (1, 0):
        pltpu.make_async_copy(
            ready.at[half, work.my_core], out.at[half, work.me], own_sem.at[half]
        ).wait()
        sent = ready.at[half, pl.ds(0, devices - 1)]
        pltpu.make_async_copy(sent, sent, send_sem.at[half]).wait()
        passed = relay.at[half, pl.ds(0, ties)]
        pltpu.make_async_copy(passed, passed, relay_send.at[half]).wait()
        arrived = out.at[half, pl.ds(0, devices - 1)]
        pltpu.make_async_copy(arrived, arrived, recv_sem.at[half]).wait()


def correlate_kernel(segments, scale, spectra, vis_real, vis_imag):
    sources = spectra.shape[1] // segments
    inputs = sources * HERE
    real, imag = [], []
    for half in range(2):
        for segment in range(segments):
            piece = spectra[half, segment * sources : (segment + 1) * sources].astype(jnp.float32)
            real.append(piece[:, :HERE].reshape(inputs, HALF).astype(jnp.bfloat16))
            imag.append(piece[:, HERE:].reshape(inputs, HALF).astype(jnp.bfloat16))
    real = jnp.concatenate(real, axis=1)
    imag = jnp.concatenate(imag, axis=1)

    def product(a, b):
        return lax.dot_general(a, b, (((1,), (1,)), ((), ())), preferred_element_type=jnp.float32)

    middle = inputs // 2
    low, high = slice(0, middle), slice(middle, inputs)
    for rows, columns in ((low, low), (high, high), (low, high)):
        block = product(real[rows], real[columns]) + product(imag[rows], imag[columns])
        vis_real[0, rows, columns] = block * scale
        if rows != columns:
            vis_real[0, columns, rows] = block.T * scale
    cross = product(real, imag)
    vis_imag[0] = (cross - cross.T) * scale


def per_device(samples, delays, flags, taps, *, segments, inp):
    nx, nz, ny_hi = SHAPES[inp]
    dims = (nx, 2 * ny_hi, nz)
    devices = segments * inp
    per_group = nx * 2 * ny_hi
    table = jnp.asarray(dft_rows(*dims))
    anywhere = pl.BlockSpec(memory_space=pl.ANY)
    in_specs = [
        anywhere,
        pl.BlockSpec(memory_space=pltpu.SMEM),
        pl.BlockSpec(memory_space=pltpu.SMEM),
        pl.BlockSpec(memory_space=pltpu.VMEM),
        anywhere,
    ]
    work_scratch = [
        pltpu.VMEM((nz, per_group, 16, FRAME), jnp.bfloat16),
        pltpu.VMEM((BLOCKS * HERE * RUN + 8, LANES), jnp.float32),
        pltpu.VMEM((BLOCKS * TAPS * 8, LANES), jnp.float32),
        pltpu.VMEM((HERE * BLOCKS * WINDOW, LANES), jnp.float32),
        pltpu.VMEM((HERE * HALF, FRAME), jnp.bfloat16),
        pltpu.VMEM((2 * per_group * 8 * O_STRIDE, LANES), jnp.float32),
    ]
    raw = pltpu.VMEM((HERE, S_DEV * FRAME), jnp.bfloat16)
    dma = pltpu.SemaphoreType.DMA
    spectra = pl.pallas_call(
        functools.partial(exchange_kernel, dims),
        out_shape=jax.ShapeDtypeStruct((2, devices, ROWS, HALF), jnp.bfloat16),
        in_specs=in_specs,
        out_specs=anywhere,
        scratch_shapes=[
            raw,
            pltpu.VMEM((HERE, HALO), jnp.bfloat16),
            pltpu.VMEM((2, devices, ROWS, HALF), jnp.bfloat16),
            pltpu.VMEM((2, devices, ROWS, HALF), jnp.bfloat16),
            *work_scratch,
            dma((2,)),
            *[dma] * 3,
            *[dma((2,))] * 4,
            dma((2, devices)),
        ],
        compiler_params=pltpu.CompilerParams(
            collective_id=0, has_side_effects=True, vmem_limit_bytes=60 * 2**20
        ),
        name="exchange",
    )(samples, delays, flags, taps, table)
    inputs = inp * HERE
    visibility = jax.ShapeDtypeStruct((CHAN, inputs, inputs), jnp.float32)
    return pl.pallas_call(
        functools.partial(correlate_kernel, segments, 1.0 / (S_DEV * segments)),
        out_shape=(visibility, visibility),
        grid=(CHAN,),
        in_specs=[pl.BlockSpec((2, devices, 2 * HERE, HALF), lambda c: (0, 0, c, 0))],
        out_specs=(
            pl.BlockSpec((1, inputs, inputs), lambda c: (c, 0, 0)),
            pl.BlockSpec((1, inputs, inputs), lambda c: (c, 0, 0)),
        ),
        compiler_params=pltpu.CompilerParams(vmem_limit_bytes=60 * 2**20),
        name="correlate",
    )(spectra)


def solution(mesh):
    segments, inp = mesh.shape["tseg"], mesh.shape["inp"]
    return jax.shard_map(
        functools.partial(per_device, segments=segments, inp=inp),
        mesh=mesh,
        in_specs=(P("inp", "tseg"), P("inp"), P("inp"), P()),
        out_specs=(P(("tseg", "inp"), None, None), P(("tseg", "inp"), None, None)),
        check_vma=False,
    )
```

```python
import functools
import math

import jax
import jax.numpy as jnp
import ml_dtypes
import numpy as np
from jax import lax
from jax.experimental import pallas as pl
from jax.experimental.pallas import tpu as pltpu
from jax.sharding import PartitionSpec as P

MESH = pl.DeviceIdType.MESH
TAPS = 16
FRAME = 1024
HALO = 23552
LANES = 128
BLOCKS = FRAME // LANES
HERE = 8
S_DEV = 256
HALF = 128
CHAN = 4
ROWS = CHAN * 2 * HERE
FIRST = HALO // FRAME + 1
RUN = FIRST + S_DEV + 1
WINDOW = HALF + TAPS
SPLIT = 103
O_STRIDE = HERE + 1
AT_ONCE = 5
SHAPES = {64: (4, 4, 2), 4: (2, 1, 1)}


def dft_rows(nx, ny, nz):
    count = nx * ny * nz * 2
    inp = count // 2
    k = np.arange(FRAME)[None, :]
    q = np.arange(count * CHAN)[:, None]
    phase = ((q * k) % FRAME).astype(np.float64) * (2.0 * math.pi / FRAME)
    parts = np.stack([np.cos(phase), -np.sin(phase)], axis=1) / math.sqrt(FRAME)
    parts = parts.astype(np.float32).astype(ml_dtypes.bfloat16)
    parts = parts.reshape(2, nx, nz, ny // 2, 2, CHAN * 2, FRAME)
    parts = parts.transpose(1, 3, 0, 2, 4, 5, 6)
    assert inp * 2 == count
    return parts.reshape(nx * ny * nz, 2 * CHAN * 2, FRAME)


class Work:
    def __init__(self, dims, delays, flags, refs):
        self.dims = dims
        self.delays, self.flags = delays, flags
        self.rows_table, self.runs, self.tap_rows, self.delayed, self.frames, self.turned = refs
        nx, ny, nz = dims
        self.inp = nx * nz * ny
        self.tseg = lax.axis_index("tseg")
        self.here = lax.axis_index("inp")
        self.me = self.tseg * self.inp + self.here
        self.my_core = self.here % 2
        self.my_y = ((self.here // 2) % (ny // 2)) * 2 + self.tseg
        self.my_z = (self.here // ny) % nz
        self.my_x = self.here // (ny * nz)
        self.lane = lax.broadcasted_iota(jnp.int32, (HERE, LANES), 1)

    def offset(self, group, step):
        nx, ny, nz = self.dims
        dx = step % nx
        dy = step // nx
        dz = (group + 2 * nz + 2 * nx + 2 * ny - dx - dy) % nz
        return dx, dy, dz

    def chip_at(self, dx, dy, dz):
        nx, ny, nz = self.dims
        return (self.my_x + dx) % nx, (self.my_y + dy) % ny, (self.my_z + dz) % nz

    def chip_of(self, group, step):
        return self.chip_at(*self.offset(group, step))

    def device(self, chip, core):
        nx, ny, nz = self.dims
        x, y, z = chip
        return y % 2, ((x * nz + z) * (ny // 2) + y // 2) * 2 + core

    def fetch_table(self, table, sem):
        nx, ny, nz = self.dims
        per_group = nx * ny

        @pl.loop(0, nz * per_group)
        def _(step):
            x, y, z = self.chip_of(step // per_group, step % per_group)
            pltpu.make_async_copy(
                table.at[(x * ny + y) * nz + z],
                self.rows_table.at[step // per_group, step % per_group],
                sem,
            ).start()

    def place_taps(self, taps):
        for block in range(BLOCKS):
            for p in range(TAPS):
                self.tap_rows[pl.ds((block * TAPS + p) * 8, 8), :] = jnp.broadcast_to(
                    taps[p : p + 1, block * LANES : (block + 1) * LANES], (8, LANES)
                )

    def spread(self, source, first, frame_range, unroll, each=None):
        row = lax.broadcasted_iota(jnp.int32, (HERE, LANES), 0)
        turn = jnp.zeros((HERE, LANES), jnp.int32)
        for i in range(HERE):
            turn = jnp.where(row == i, self.delays[i] % LANES, turn)
        index = (self.lane - turn + LANES) % LANES

        @pl.loop(*frame_range, step=unroll)
        def _(start):
            for frame in range(unroll):
                frame = start + frame
                values = source[:, pl.ds(pl.multiple_of(frame * FRAME, FRAME), FRAME)].astype(
                    jnp.float32
                )
                for block in range(BLOCKS):
                    moved = jnp.take_along_axis(
                        values[:, block * LANES : (block + 1) * LANES], index, axis=1
                    )
                    self.runs[pl.ds(block * HERE * RUN + first + frame, HERE, stride=RUN), :] = (
                        moved
                    )
            if each is not None:
                each(start // unroll)

    def run_half(self, half, each=None):
        base = half * HALF - (TAPS - 1)

        @pl.loop(0, HERE * BLOCKS)
        def _(run):
            i = run // BLOCKS
            block = run % BLOCKS
            delay = self.delays[i]
            keep = self.lane >= delay % LANES
            weight = self.flags[i].astype(jnp.float32)

            def start(back):
                moved = block - delay // LANES - back + 9 * BLOCKS
                return (moved % BLOCKS * HERE + i) * RUN + moved // BLOCKS - 9 + FIRST + base

            now, before = start(0), start(1)
            for f in range(0, WINDOW, 8):
                self.delayed[pl.ds(pl.multiple_of(run * WINDOW, 8) + f, 8), :] = jnp.where(
                    keep, self.runs[pl.ds(now + f, 8), :], self.runs[pl.ds(before + f, 8), :]
                )
            tap = [self.tap_rows[pl.ds((block * TAPS + p) * 8, 8), :] for p in range(TAPS)]
            total = {}
            for f in range(HALF + 8):
                values = self.delayed[pl.ds(run * WINDOW + f, 8), :]
                for p in (f % 8 + 8, f % 8):
                    s = f - p
                    if 0 <= s < HALF:
                        total[s] = tap[p] * values if p == 0 else total[s] + tap[p] * values
                if f % 16 == 15 and f > 16:
                    pair = [total.pop(f - 31), total.pop(f - 23)]
                    self.frames[
                        pl.ds(pl.multiple_of(i * HALF, HALF) + f - 31, 16),
                        pl.ds(pl.multiple_of(block * LANES, LANES), LANES),
                    ] = (jnp.concatenate(pair, axis=0) * weight).astype(jnp.bfloat16)
            pair = [total.pop(HALF - 16), total.pop(HALF - 8)]
            self.frames[
                pl.ds(pl.multiple_of(i * HALF, HALF) + HALF - 16, 16),
                pl.ds(pl.multiple_of(block * LANES, LANES), LANES),
            ] = (jnp.concatenate(pair, axis=0) * weight).astype(jnp.bfloat16)
            assert not total
            if each is not None:
                each(run)

    def transform(self, group):
        nx, ny, nz = self.dims
        per_group = nx * ny
        rows = self.rows_table[group].reshape(per_group * 16, FRAME)

        for pair in range(HERE // 2):
            values = self.frames[pair * 2 * HALF : (pair + 1) * 2 * HALF, :]
            spectra = lax.dot_general(
                rows, values, (((1,), (1,)), ((), ())), preferred_element_type=jnp.float32
            )
            for dest in range(2 * per_group):
                for j in range(2):
                    self.turned[
                        pl.ds(dest * 8 * O_STRIDE + pair * 2 + j, 8, stride=O_STRIDE), :
                    ] = spectra[dest * 8 : (dest + 1) * 8, j * HALF : (j + 1) * HALF]

    def pack(self, dest, target):
        for m in range(0, 8, 2):
            pair_rows = jnp.concatenate(
                [
                    self.turned[pl.ds((dest * 8 + m) * O_STRIDE, HERE), :],
                    self.turned[pl.ds((dest * 8 + m + 1) * O_STRIDE, HERE), :],
                ],
                axis=0,
            )
            target[m * 8 : (m + 2) * 8, :] = pair_rows.astype(jnp.bfloat16)

    def send(self, source, target, device, send_sem, recv_sem):
        pltpu.make_async_remote_copy(
            src_ref=source,
            dst_ref=target,
            send_sem=send_sem,
            recv_sem=recv_sem,
            device_id=device,
            device_id_type=MESH,
        ).start()

    def send_direct(self, group, step, change, source, target, send_sem, recv_sem):
        core = (self.my_core + change) % 2
        slot = (group * self.dims[0] * self.dims[1] + step) * 2 + core
        chip = self.chip_of(group, step)
        self.send(
            source.at[slot], target.at[self.me], self.device(chip, core), send_sem, recv_sem
        )


def exchange_kernel(dims, samples, delays, flags, taps, table, out, raw, rim, ready, *rest):
    refs, sems = rest[:6], rest[6:]
    load_sem, table_sem, rim_send, rim_recv, send_sem, recv_sem, own_sem = sems
    work = Work(dims, delays, flags, refs)
    nx, ny, nz = dims
    per_group = nx * ny
    inp = nx * ny * nz
    devices = 2 * inp

    def load(first, count, sem):
        part = pl.ds(first * FRAME, count * FRAME)
        copy = pltpu.make_async_copy(samples.at[:, part], raw.at[:, part], sem)
        copy.start()
        return copy

    late_load = load(SPLIT, S_DEV - SPLIT, load_sem.at[0])
    early_load = load(0, SPLIT, load_sem.at[1])
    barrier = pltpu.get_barrier_semaphore()

    @pl.loop(1, devices)
    def _(step):
        other = (work.me + step) % devices
        pl.semaphore_signal(
            barrier, inc=1, device_id=(other // inp, other % inp), device_id_type=MESH
        )

    work.fetch_table(table, table_sem)
    work.place_taps(taps)

    def send_direct(half, group, step):
        common = (ready.at[half], out.at[half], send_sem.at[half], recv_sem.at[half])

        @pl.when(group + step > 0)
        def _():
            work.send_direct(group, step, 0, *common)

        @pl.when(group + step == 0)
        def _():
            pltpu.make_async_copy(
                ready.at[half, work.my_core], out.at[half, work.me], own_sem.at[half]
            ).start()

        work.send_direct(group, step, 1, *common)

    def send_chip(half, slot):
        send_direct(half, slot // per_group, slot % per_group)

    def send_later(order):
        later = per_group - AT_ONCE
        send_direct(1, order // later, AT_ONCE + order % later)

    def transform_half(half, each_group, each_step):
        @pl.loop(0, nz)
        def _(group):
            work.transform(group)

            @pl.loop(0, per_group, step=4)
            def _(chips):
                for dest in range(8):
                    dest = chips * 2 + dest
                    work.pack(dest, ready.at[half, group * 2 * per_group + dest])
                if each_step is not None:
                    each_step(group * 4 + chips // 4)

            if each_group is not None:
                each_group(group)

    def some_now(group):
        @pl.loop(0, AT_ONCE)
        def _(step):
            send_direct(1, group, step)

    def in_spread(step):
        @pl.when(step % 3 == 0)
        def _():
            send_later(step // 3)

    def in_filter(run):
        @pl.when(run % 3 == 0)
        def _():
            send_later(9 + run // 3)

    def in_transform(step):
        @pl.when(step < 13)
        def _():
            send_later(31 + step)

    late_load.wait()
    work.spread(raw, FIRST, (SPLIT, S_DEV - 1), 4)
    work.spread(raw, FIRST, (S_DEV - 1, S_DEV), 1)
    pl.semaphore_wait(barrier, devices - 1)
    rim_copy = pltpu.make_async_remote_copy(
        src_ref=samples.at[:, pl.ds(S_DEV * FRAME - HALO, HALO)],
        dst_ref=rim,
        send_sem=rim_send,
        recv_sem=rim_recv,
        device_id=(1 - work.tseg, work.here),
        device_id_type=MESH,
    )
    rim_copy.start()
    work.run_half(1)
    pltpu.make_async_copy(work.rows_table, work.rows_table, table_sem).wait()
    transform_half(1, some_now, None)

    early_load.wait()
    work.spread(raw, FIRST, (0, SPLIT - 3), 4, in_spread)
    work.spread(raw, FIRST, (SPLIT - 3, SPLIT), 1)
    rim_copy.wait()

    @pl.when(work.tseg == 0)
    def _():
        rim[...] = jnp.zeros_like(rim)

    work.spread(rim, 1, (0, 20), 4)
    work.spread(rim, 1, (20, HALO // FRAME), 1)
    work.run_half(0, in_filter)
    transform_half(0, None, in_transform)

    @pl.loop(0, nz * per_group)
    def _(slot):
        send_chip(0, slot)

    for half in (1, 0):
        pltpu.make_async_copy(
            ready.at[half, work.my_core], out.at[half, work.me], own_sem.at[half]
        ).wait()
        sent = ready.at[half, pl.ds(0, devices - 1)]
        pltpu.make_async_copy(sent, sent, send_sem.at[half]).wait()
        arrived = out.at[half, pl.ds(0, devices - 1)]
        pltpu.make_async_copy(arrived, arrived, recv_sem.at[half]).wait()


def correlate_kernel(segments, scale, spectra, vis_real, vis_imag):
    sources = spectra.shape[1] // segments
    inputs = sources * HERE
    real, imag = [], []
    for half in range(2):
        for segment in range(segments):
            piece = spectra[half, segment * sources : (segment + 1) * sources].astype(jnp.float32)
            real.append(piece[:, :HERE].reshape(inputs, HALF).astype(jnp.bfloat16))
            imag.append(piece[:, HERE:].reshape(inputs, HALF).astype(jnp.bfloat16))
    real = jnp.concatenate(real, axis=1)
    imag = jnp.concatenate(imag, axis=1)

    def product(a, b):
        return lax.dot_general(a, b, (((1,), (1,)), ((), ())), preferred_element_type=jnp.float32)

    middle = inputs // 2
    low, high = slice(0, middle), slice(middle, inputs)
    for rows, columns in ((low, low), (high, high), (low, high)):
        block = product(real[rows], real[columns]) + product(imag[rows], imag[columns])
        vis_real[0, rows, columns] = block * scale
        if rows != columns:
            vis_real[0, columns, rows] = block.T * scale
    cross = product(real, imag)
    vis_imag[0] = (cross - cross.T) * scale


def per_device(samples, delays, flags, taps, *, segments, inp):
    nx, nz, ny_hi = SHAPES[inp]
    dims = (nx, 2 * ny_hi, nz)
    devices = segments * inp
    per_group = nx * 2 * ny_hi
    table = jnp.asarray(dft_rows(*dims))
    anywhere = pl.BlockSpec(memory_space=pl.ANY)
    in_specs = [
        anywhere,
        pl.BlockSpec(memory_space=pltpu.SMEM),
        pl.BlockSpec(memory_space=pltpu.SMEM),
        pl.BlockSpec(memory_space=pltpu.VMEM),
        anywhere,
    ]
    work_scratch = [
        pltpu.VMEM((nz, per_group, 16, FRAME), jnp.bfloat16),
        pltpu.VMEM((BLOCKS * HERE * RUN + 8, LANES), jnp.float32),
        pltpu.VMEM((BLOCKS * TAPS * 8, LANES), jnp.float32),
        pltpu.VMEM((HERE * BLOCKS * WINDOW, LANES), jnp.float32),
        pltpu.VMEM((HERE * HALF, FRAME), jnp.bfloat16),
        pltpu.VMEM((2 * per_group * 8 * O_STRIDE, LANES), jnp.float32),
    ]
    raw = pltpu.VMEM((HERE, S_DEV * FRAME), jnp.bfloat16)
    dma = pltpu.SemaphoreType.DMA
    spectra = pl.pallas_call(
        functools.partial(exchange_kernel, dims),
        out_shape=jax.ShapeDtypeStruct((2, devices, ROWS, HALF), jnp.bfloat16),
        in_specs=in_specs,
        out_specs=anywhere,
        scratch_shapes=[
            raw,
            pltpu.VMEM((HERE, HALO), jnp.bfloat16),
            pltpu.VMEM((2, devices, ROWS, HALF), jnp.bfloat16),
            *work_scratch,
            dma((2,)),
            *[dma] * 3,
            *[dma((2,))] * 3,
        ],
        compiler_params=pltpu.CompilerParams(
            collective_id=0, has_side_effects=True, vmem_limit_bytes=60 * 2**20
        ),
        name="exchange",
    )(samples, delays, flags, taps, table)
    inputs = inp * HERE
    visibility = jax.ShapeDtypeStruct((CHAN, inputs, inputs), jnp.float32)
    return pl.pallas_call(
        functools.partial(correlate_kernel, segments, 1.0 / (S_DEV * segments)),
        out_shape=(visibility, visibility),
        grid=(CHAN,),
        in_specs=[pl.BlockSpec((2, devices, 2 * HERE, HALF), lambda c: (0, 0, c, 0))],
        out_specs=(
            pl.BlockSpec((1, inputs, inputs), lambda c: (c, 0, 0)),
            pl.BlockSpec((1, inputs, inputs), lambda c: (c, 0, 0)),
        ),
        compiler_params=pltpu.CompilerParams(vmem_limit_bytes=60 * 2**20),
        name="correlate",
    )(spectra)


def solution(mesh):
    segments, inp = mesh.shape["tseg"], mesh.shape["inp"]
    return jax.shard_map(
        functools.partial(per_device, segments=segments, inp=inp),
        mesh=mesh,
        in_specs=(P("inp", "tseg"), P("inp"), P("inp"), P()),
        out_specs=(P(("tseg", "inp"), None, None), P(("tseg", "inp"), None, None)),
        check_vma=False,
    )
```

```python
import functools
import math

import jax
import jax.numpy as jnp
import ml_dtypes
import numpy as np
from jax import lax
from jax.experimental import pallas as pl
from jax.experimental.pallas import tpu as pltpu
from jax.sharding import PartitionSpec as P

MESH = pl.DeviceIdType.MESH
TAPS = 16
FRAME = 1024
HALO = 23552
LANES = 128
BLOCKS = FRAME // LANES
HERE = 8
S_DEV = 256
HALF = 128
CHAN = 4
ROWS = CHAN * 2 * HERE
FIRST = HALO // FRAME + 1
RUN = FIRST + S_DEV + 1
WINDOW = HALF + TAPS
SPLIT = 103
O_STRIDE = HERE + 1
WINDOW_CHIPS = 8
AT_ONCE = 5
SHAPES = {64: (4, 4, 2), 4: (2, 1, 1)}


def dft_rows(nx, ny, nz):
    count = nx * ny * nz * 2
    inp = count // 2
    k = np.arange(FRAME)[None, :]
    q = np.arange(count * CHAN)[:, None]
    phase = ((q * k) % FRAME).astype(np.float64) * (2.0 * math.pi / FRAME)
    parts = np.stack([np.cos(phase), -np.sin(phase)], axis=1) / math.sqrt(FRAME)
    parts = parts.astype(np.float32).astype(ml_dtypes.bfloat16)
    parts = parts.reshape(2, nx, nz, ny // 2, 2, CHAN * 2, FRAME)
    parts = parts.transpose(1, 3, 0, 2, 4, 5, 6)
    assert inp * 2 == count
    return parts.reshape(nx * ny * nz, 2 * CHAN * 2, FRAME)


class Work:
    def __init__(self, dims, delays, flags, refs):
        self.dims = dims
        self.delays, self.flags = delays, flags
        self.rows_table, self.runs, self.tap_rows, self.delayed, self.frames, self.turned = refs
        nx, ny, nz = dims
        self.inp = nx * nz * ny
        self.tseg = lax.axis_index("tseg")
        self.here = lax.axis_index("inp")
        self.me = self.tseg * self.inp + self.here
        self.my_core = self.here % 2
        self.my_y = ((self.here // 2) % (ny // 2)) * 2 + self.tseg
        self.my_z = (self.here // ny) % nz
        self.my_x = self.here // (ny * nz)
        self.lane = lax.broadcasted_iota(jnp.int32, (HERE, LANES), 1)

    def offset(self, group, step):
        nx, ny, nz = self.dims
        dx = step % nx
        return dx, (dx + step // nx) % ny, (dx + group) % nz

    def chip_at(self, dx, dy, dz):
        nx, ny, nz = self.dims
        return (self.my_x + dx) % nx, (self.my_y + dy) % ny, (self.my_z + dz) % nz

    def chip_of(self, group, step):
        return self.chip_at(*self.offset(group, step))

    def device(self, chip, core):
        nx, ny, nz = self.dims
        x, y, z = chip
        return y % 2, ((x * nz + z) * (ny // 2) + y // 2) * 2 + core

    def fetch_table(self, table, sem):
        nx, ny, nz = self.dims
        per_group = nx * ny

        @pl.loop(0, nz * per_group)
        def _(step):
            x, y, z = self.chip_of(step // per_group, step % per_group)
            pltpu.make_async_copy(
                table.at[(x * ny + y) * nz + z],
                self.rows_table.at[step // per_group, step % per_group],
                sem,
            ).start()

    def place_taps(self, taps):
        for block in range(BLOCKS):
            for p in range(TAPS):
                self.tap_rows[pl.ds((block * TAPS + p) * 8, 8), :] = jnp.broadcast_to(
                    taps[p : p + 1, block * LANES : (block + 1) * LANES], (8, LANES)
                )

    def spread(self, source, first, frame_range, unroll, each=None):
        row = lax.broadcasted_iota(jnp.int32, (HERE, LANES), 0)
        turn = jnp.zeros((HERE, LANES), jnp.int32)
        for i in range(HERE):
            turn = jnp.where(row == i, self.delays[i] % LANES, turn)
        index = (self.lane - turn + LANES) % LANES

        @pl.loop(*frame_range, step=unroll)
        def _(start):
            for frame in range(unroll):
                frame = start + frame
                values = source[:, pl.ds(pl.multiple_of(frame * FRAME, FRAME), FRAME)].astype(
                    jnp.float32
                )
                for block in range(BLOCKS):
                    moved = jnp.take_along_axis(
                        values[:, block * LANES : (block + 1) * LANES], index, axis=1
                    )
                    self.runs[pl.ds(block * HERE * RUN + first + frame, HERE, stride=RUN), :] = (
                        moved
                    )
            if each is not None:
                each(start // unroll)

    def run_half(self, half, each=None):
        base = half * HALF - (TAPS - 1)

        @pl.loop(0, HERE * BLOCKS)
        def _(run):
            i = run // BLOCKS
            block = run % BLOCKS
            delay = self.delays[i]
            keep = self.lane >= delay % LANES
            weight = self.flags[i].astype(jnp.float32)

            def start(back):
                moved = block - delay // LANES - back + 9 * BLOCKS
                return (moved % BLOCKS * HERE + i) * RUN + moved // BLOCKS - 9 + FIRST + base

            now, before = start(0), start(1)
            for f in range(0, WINDOW, 8):
                self.delayed[pl.ds(pl.multiple_of(run * WINDOW, 8) + f, 8), :] = jnp.where(
                    keep, self.runs[pl.ds(now + f, 8), :], self.runs[pl.ds(before + f, 8), :]
                )
            tap = [self.tap_rows[pl.ds((block * TAPS + p) * 8, 8), :] for p in range(TAPS)]
            total = {}
            for f in range(HALF + 8):
                values = self.delayed[pl.ds(run * WINDOW + f, 8), :]
                for p in (f % 8 + 8, f % 8):
                    s = f - p
                    if 0 <= s < HALF:
                        total[s] = tap[p] * values if p == 0 else total[s] + tap[p] * values
                if f % 16 == 15 and f > 16:
                    pair = [total.pop(f - 31), total.pop(f - 23)]
                    self.frames[
                        pl.ds(pl.multiple_of(i * HALF, HALF) + f - 31, 16),
                        pl.ds(pl.multiple_of(block * LANES, LANES), LANES),
                    ] = (jnp.concatenate(pair, axis=0) * weight).astype(jnp.bfloat16)
            pair = [total.pop(HALF - 16), total.pop(HALF - 8)]
            self.frames[
                pl.ds(pl.multiple_of(i * HALF, HALF) + HALF - 16, 16),
                pl.ds(pl.multiple_of(block * LANES, LANES), LANES),
            ] = (jnp.concatenate(pair, axis=0) * weight).astype(jnp.bfloat16)
            assert not total
            if each is not None:
                each(run)

    def transform(self, group):
        nx, ny, nz = self.dims
        per_group = nx * ny
        rows = self.rows_table[group].reshape(per_group * 16, FRAME)

        for pair in range(HERE // 2):
            values = self.frames[pair * 2 * HALF : (pair + 1) * 2 * HALF, :]
            spectra = lax.dot_general(
                rows, values, (((1,), (1,)), ((), ())), preferred_element_type=jnp.float32
            )
            for dest in range(2 * per_group):
                for j in range(2):
                    self.turned[
                        pl.ds(dest * 8 * O_STRIDE + pair * 2 + j, 8, stride=O_STRIDE), :
                    ] = spectra[dest * 8 : (dest + 1) * 8, j * HALF : (j + 1) * HALF]

    def pack(self, dest, target):
        for m in range(0, 8, 2):
            pair_rows = jnp.concatenate(
                [
                    self.turned[pl.ds((dest * 8 + m) * O_STRIDE, HERE), :],
                    self.turned[pl.ds((dest * 8 + m + 1) * O_STRIDE, HERE), :],
                ],
                axis=0,
            )
            target[m * 8 : (m + 2) * 8, :] = pair_rows.astype(jnp.bfloat16)

    def send(self, source, target, device, send_sem, recv_sem):
        pltpu.make_async_remote_copy(
            src_ref=source,
            dst_ref=target,
            send_sem=send_sem,
            recv_sem=recv_sem,
            device_id=device,
            device_id_type=MESH,
        ).start()

    def send_direct(self, group, step, change, source, target, send_sem, recv_sem):
        core = (self.my_core + change) % 2
        slot = (group * self.dims[0] * self.dims[1] + step) * 2 + core
        chip = self.chip_of(group, step)
        self.send(
            source.at[slot], target.at[self.me], self.device(chip, core), send_sem, recv_sem
        )


def exchange_kernel(dims, samples, delays, flags, taps, table, out, raw, rim, ready, *rest):
    refs, sems = rest[:6], rest[6:]
    load_sem, table_sem, rim_send, rim_recv, send_sem, recv_sem, own_sem = sems
    work = Work(dims, delays, flags, refs)
    nx, ny, nz = dims
    per_group = nx * ny
    inp = nx * ny * nz
    devices = 2 * inp

    def load(first, count, sem):
        part = pl.ds(first * FRAME, count * FRAME)
        copy = pltpu.make_async_copy(samples.at[:, part], raw.at[:, part], sem)
        copy.start()
        return copy

    late_load = load(SPLIT, S_DEV - SPLIT, load_sem.at[0])
    early_load = load(0, SPLIT, load_sem.at[1])
    barrier = pltpu.get_barrier_semaphore()

    @pl.loop(1, devices)
    def _(step):
        other = (work.me + step) % devices
        pl.semaphore_signal(
            barrier, inc=1, device_id=(other // inp, other % inp), device_id_type=MESH
        )

    work.fetch_table(table, table_sem)
    work.place_taps(taps)

    def send_direct(half, group, step):
        slot = group * per_group + step
        common = (ready.at[half], out.at[half], send_sem.at[half, slot], recv_sem.at[half])

        @pl.when(group + step > 0)
        def _():
            work.send_direct(group, step, 0, *common)

        @pl.when(group + step == 0)
        def _():
            pltpu.make_async_copy(
                ready.at[half, work.my_core], out.at[half, work.me], own_sem.at[half]
            ).start()

        work.send_direct(group, step, 1, *common)

    def send_chip(half, slot):
        send_direct(half, slot // per_group, slot % per_group)

    def send_later(order):
        later = per_group - AT_ONCE
        send_direct(1, order // later, AT_ONCE + order % later)

    def transform_half(half, each_group, each_step):
        @pl.loop(0, nz)
        def _(group):
            work.transform(group)

            @pl.loop(0, per_group, step=4)
            def _(chips):
                for dest in range(8):
                    dest = chips * 2 + dest
                    work.pack(dest, ready.at[half, group * 2 * per_group + dest])
                if each_step is not None:
                    each_step(group * 4 + chips // 4)

            if each_group is not None:
                each_group(group)

    def some_now(group):
        @pl.loop(0, AT_ONCE)
        def _(step):
            send_direct(1, group, step)

    def in_spread(step):
        @pl.when(step % 3 == 0)
        def _():
            send_later(step // 3)

    def in_filter(run):
        @pl.when(run % 3 == 0)
        def _():
            send_later(9 + run // 3)

    def in_transform(step):
        @pl.when(step < 13)
        def _():
            send_later(31 + step)

    late_load.wait()
    work.spread(raw, FIRST, (SPLIT, S_DEV - 1), 4)
    work.spread(raw, FIRST, (S_DEV - 1, S_DEV), 1)
    pl.semaphore_wait(barrier, devices - 1)
    rim_copy = pltpu.make_async_remote_copy(
        src_ref=samples.at[:, pl.ds(S_DEV * FRAME - HALO, HALO)],
        dst_ref=rim,
        send_sem=rim_send,
        recv_sem=rim_recv,
        device_id=(1 - work.tseg, work.here),
        device_id_type=MESH,
    )
    rim_copy.start()
    work.run_half(1)
    pltpu.make_async_copy(work.rows_table, work.rows_table, table_sem).wait()
    transform_half(1, some_now, None)

    early_load.wait()
    work.spread(raw, FIRST, (0, SPLIT - 3), 4, in_spread)
    work.spread(raw, FIRST, (SPLIT - 3, SPLIT), 1)
    rim_copy.wait()

    @pl.when(work.tseg == 0)
    def _():
        rim[...] = jnp.zeros_like(rim)

    work.spread(rim, 1, (0, 20), 4)
    work.spread(rim, 1, (20, HALO // FRAME), 1)
    work.run_half(0, in_filter)
    transform_half(0, None, in_transform)

    def left(half, slot):
        pair = ready.at[half, pl.ds(slot * 2, 2)]

        @pl.when(slot == 0)
        def _():
            pltpu.make_async_copy(pair.at[0], pair.at[0], send_sem.at[half, slot]).wait()

        @pl.when(slot > 0)
        def _():
            pltpu.make_async_copy(pair, pair, send_sem.at[half, slot]).wait()

    @pl.loop(0, WINDOW_CHIPS)
    def _(slot):
        send_chip(0, slot)

    @pl.loop(WINDOW_CHIPS, nz * per_group)
    def _(slot):
        left(0, slot - WINDOW_CHIPS)
        send_chip(0, slot)

    @pl.loop(nz * per_group - WINDOW_CHIPS, nz * per_group)
    def _(slot):
        left(0, slot)

    @pl.loop(0, nz * per_group)
    def _(slot):
        left(1, slot)

    for half in (1, 0):
        pltpu.make_async_copy(
            ready.at[half, work.my_core], out.at[half, work.me], own_sem.at[half]
        ).wait()
        arrived = out.at[half, pl.ds(0, devices - 1)]
        pltpu.make_async_copy(arrived, arrived, recv_sem.at[half]).wait()


def correlate_kernel(segments, scale, spectra, vis_real, vis_imag):
    sources = spectra.shape[1] // segments
    inputs = sources * HERE
    real, imag = [], []
    for half in range(2):
        for segment in range(segments):
            piece = spectra[half, segment * sources : (segment + 1) * sources].astype(jnp.float32)
            real.append(piece[:, :HERE].reshape(inputs, HALF).astype(jnp.bfloat16))
            imag.append(piece[:, HERE:].reshape(inputs, HALF).astype(jnp.bfloat16))
    plain = jnp.concatenate([*real, *imag], axis=1)
    crossed = jnp.concatenate([*imag, *[-part for part in real]], axis=1)

    def product(a, b):
        return (
            lax.dot_general(a, b, (((1,), (1,)), ((), ())), preferred_element_type=jnp.float32)
            * scale
        )

    middle = inputs // 2
    low, high = slice(0, middle), slice(middle, inputs)
    for rows, columns in ((low, high), (low, low), (high, high)):
        block_real = product(plain[rows], plain[columns])
        block_imag = product(plain[rows], crossed[columns])
        vis_real[0, rows, columns] = block_real
        vis_imag[0, rows, columns] = block_imag
        if rows != columns:
            vis_real[0, columns, rows] = block_real.T
            vis_imag[0, columns, rows] = -block_imag.T


def per_device(samples, delays, flags, taps, *, segments, inp):
    nx, nz, ny_hi = SHAPES[inp]
    dims = (nx, 2 * ny_hi, nz)
    devices = segments * inp
    per_group = nx * 2 * ny_hi
    table = jnp.asarray(dft_rows(*dims))
    anywhere = pl.BlockSpec(memory_space=pl.ANY)
    in_specs = [
        anywhere,
        pl.BlockSpec(memory_space=pltpu.SMEM),
        pl.BlockSpec(memory_space=pltpu.SMEM),
        pl.BlockSpec(memory_space=pltpu.VMEM),
        anywhere,
    ]
    work_scratch = [
        pltpu.VMEM((nz, per_group, 16, FRAME), jnp.bfloat16),
        pltpu.VMEM((BLOCKS * HERE * RUN + 8, LANES), jnp.float32),
        pltpu.VMEM((BLOCKS * TAPS * 8, LANES), jnp.float32),
        pltpu.VMEM((HERE * BLOCKS * WINDOW, LANES), jnp.float32),
        pltpu.VMEM((HERE * HALF, FRAME), jnp.bfloat16),
        pltpu.VMEM((2 * per_group * 8 * O_STRIDE, LANES), jnp.float32),
    ]
    raw = pltpu.VMEM((HERE, S_DEV * FRAME), jnp.bfloat16)
    dma = pltpu.SemaphoreType.DMA
    spectra = pl.pallas_call(
        functools.partial(exchange_kernel, dims),
        out_shape=jax.ShapeDtypeStruct((2, devices, ROWS, HALF), jnp.bfloat16),
        in_specs=in_specs,
        out_specs=anywhere,
        scratch_shapes=[
            raw,
            pltpu.VMEM((HERE, HALO), jnp.bfloat16),
            pltpu.VMEM((2, devices, ROWS, HALF), jnp.bfloat16),
            *work_scratch,
            dma((2,)),
            *[dma] * 3,
            dma((2, nz * per_group)),
            *[dma((2,))] * 2,
        ],
        compiler_params=pltpu.CompilerParams(
            collective_id=0, has_side_effects=True, vmem_limit_bytes=60 * 2**20
        ),
        name="exchange",
    )(samples, delays, flags, taps, table)
    inputs = inp * HERE
    visibility = jax.ShapeDtypeStruct((CHAN, inputs, inputs), jnp.float32)
    return pl.pallas_call(
        functools.partial(correlate_kernel, segments, 1.0 / (S_DEV * segments)),
        out_shape=(visibility, visibility),
        grid=(CHAN,),
        in_specs=[pl.BlockSpec((2, devices, 2 * HERE, HALF), lambda c: (0, 0, c, 0))],
        out_specs=(
            pl.BlockSpec((1, inputs, inputs), lambda c: (c, 0, 0)),
            pl.BlockSpec((1, inputs, inputs), lambda c: (c, 0, 0)),
        ),
        compiler_params=pltpu.CompilerParams(vmem_limit_bytes=60 * 2**20),
        name="correlate",
    )(spectra)


def solution(mesh):
    segments, inp = mesh.shape["tseg"], mesh.shape["inp"]
    return jax.shard_map(
        functools.partial(per_device, segments=segments, inp=inp),
        mesh=mesh,
        in_specs=(P("inp", "tseg"), P("inp"), P("inp"), P()),
        out_specs=(P(("tseg", "inp"), None, None), P(("tseg", "inp"), None, None)),
        check_vma=False,
    )
```

```python
import functools
import math

import jax
import jax.numpy as jnp
import ml_dtypes
import numpy as np
from jax import lax
from jax.experimental import pallas as pl
from jax.experimental.pallas import tpu as pltpu
from jax.sharding import PartitionSpec as P

MESH = pl.DeviceIdType.MESH
TAPS = 16
FRAME = 1024
HALO = 23552
LANES = 128
BLOCKS = FRAME // LANES
HERE = 8
S_DEV = 256
HALF = 128
CHAN = 4
ROWS = CHAN * 2 * HERE
FIRST = HALO // FRAME + 1
RUN = FIRST + S_DEV + 1
WINDOW = HALF + TAPS
SPLIT = 103
O_STRIDE = HERE + 1
PIECES = ((103, 40), (143, 40), (183, 40), (223, 33))
GREET_FIRST = 37
GREET_STEP = 3
AT_ONCE = 5
SHAPES = {64: (4, 4, 2), 4: (2, 1, 1)}


def dft_rows(nx, ny, nz):
    count = nx * ny * nz * 2
    inp = count // 2
    k = np.arange(FRAME)[None, :]
    q = np.arange(count * CHAN)[:, None]
    phase = ((q * k) % FRAME).astype(np.float64) * (2.0 * math.pi / FRAME)
    parts = np.stack([np.cos(phase), -np.sin(phase)], axis=1) / math.sqrt(FRAME)
    parts = parts.astype(np.float32).astype(ml_dtypes.bfloat16)
    parts = parts.reshape(2, nx, nz, ny // 2, 2, CHAN * 2, FRAME)
    parts = parts.transpose(1, 3, 0, 2, 4, 5, 6)
    assert inp * 2 == count
    return parts.reshape(nx * ny * nz, 2 * CHAN * 2, FRAME)


def rem(a, b):
    return lax.rem(a, jnp.int32(b))


def div(a, b):
    return lax.div(a, jnp.int32(b))


class Work:
    def __init__(self, dims, delays, flags, refs):
        self.dims = dims
        self.delays, self.flags = delays, flags
        self.rows_table, self.runs, self.tap_rows, self.delayed, self.frames, self.turned = refs
        nx, ny, nz = dims
        self.inp = nx * nz * ny
        self.tseg = lax.axis_index("tseg")
        self.here = lax.axis_index("inp")
        self.me = self.tseg * self.inp + self.here
        self.my_core = rem(self.here, 2)
        self.my_y = rem(div(self.here, 2), ny // 2) * 2 + self.tseg
        self.my_z = rem(div(self.here, ny), nz)
        self.my_x = div(self.here, ny * nz)
        self.sign = 1 - 2 * self.my_core
        self.lane = lax.broadcasted_iota(jnp.int32, (HERE, LANES), 1)

    def chip_of(self, group, step):
        nx, ny, nz = self.dims
        dx = rem(step, nx)
        dy = div(step, nx)
        dz = group + 2 * nz - dx - dy
        return (
            rem(self.my_x + nx + self.sign * dx, nx),
            rem(self.my_y + ny + self.sign * dy, ny),
            rem(self.my_z + 4 * nz + self.sign * dz, nz),
        )

    def device(self, chip, core):
        nx, ny, nz = self.dims
        x, y, z = chip
        return rem(y, 2), ((x * nz + z) * (ny // 2) + div(y, 2)) * 2 + core

    def place_taps(self, taps):
        for block in range(BLOCKS):
            for p in range(TAPS):
                self.tap_rows[pl.ds((block * TAPS + p) * 8, 8), :] = jnp.broadcast_to(
                    taps[p : p + 1, block * LANES : (block + 1) * LANES], (8, LANES)
                )

    def spread(self, source, first, frame_range, unroll, each=None):
        row = lax.broadcasted_iota(jnp.int32, (HERE, LANES), 0)
        turn = jnp.zeros((HERE, LANES), jnp.int32)
        for i in range(HERE):
            turn = jnp.where(row == i, self.delays[i] % LANES, turn)
        index = (self.lane - turn + LANES) % LANES

        @pl.loop(*frame_range, step=unroll)
        def _(start):
            for frame in range(unroll):
                frame = start + frame
                values = source[:, pl.ds(pl.multiple_of(frame * FRAME, FRAME), FRAME)].astype(
                    jnp.float32
                )
                for block in range(BLOCKS):
                    moved = jnp.take_along_axis(
                        values[:, block * LANES : (block + 1) * LANES], index, axis=1
                    )
                    self.runs[pl.ds(block * HERE * RUN + first + frame, HERE, stride=RUN), :] = (
                        moved
                    )
            if each is not None:
                each(div(start - frame_range[0], unroll))

    def run_half(self, half, each=None):
        base = half * HALF - (TAPS - 1)

        @pl.loop(0, HERE * BLOCKS)
        def _(run):
            i = div(run, BLOCKS)
            block = rem(run, BLOCKS)
            delay = self.delays[i]
            keep = self.lane >= delay % LANES
            weight = self.flags[i].astype(jnp.float32)

            def start(back):
                moved = block - delay // LANES - back + 9 * BLOCKS
                return (moved % BLOCKS * HERE + i) * RUN + moved // BLOCKS - 9 + FIRST + base

            now, before = start(0), start(1)
            for f in range(0, WINDOW, 8):
                self.delayed[pl.ds(pl.multiple_of(run * WINDOW, 8) + f, 8), :] = jnp.where(
                    keep, self.runs[pl.ds(now + f, 8), :], self.runs[pl.ds(before + f, 8), :]
                )
            tap = [self.tap_rows[pl.ds((block * TAPS + p) * 8, 8), :] for p in range(TAPS)]
            total = {}
            for f in range(HALF + 8):
                values = self.delayed[pl.ds(run * WINDOW + f, 8), :]
                for p in (f % 8 + 8, f % 8):
                    s = f - p
                    if 0 <= s < HALF:
                        total[s] = tap[p] * values if p == 0 else total[s] + tap[p] * values
                if f % 16 == 15 and f > 16:
                    pair = [total.pop(f - 31), total.pop(f - 23)]
                    self.frames[
                        pl.ds(pl.multiple_of(i * HALF, HALF) + f - 31, 16),
                        pl.ds(pl.multiple_of(block * LANES, LANES), LANES),
                    ] = (jnp.concatenate(pair, axis=0) * weight).astype(jnp.bfloat16)
            pair = [total.pop(HALF - 16), total.pop(HALF - 8)]
            self.frames[
                pl.ds(pl.multiple_of(i * HALF, HALF) + HALF - 16, 16),
                pl.ds(pl.multiple_of(block * LANES, LANES), LANES),
            ] = (jnp.concatenate(pair, axis=0) * weight).astype(jnp.bfloat16)
            assert not total
            if each is not None:
                each(run)

    def transform(self, group):
        nx, ny, nz = self.dims
        per_group = nx * ny
        chips = [self.chip_of(group, jnp.int32(step)) for step in range(per_group)]
        rows = jnp.concatenate(
            [self.rows_table[(x * ny + y) * nz + z] for x, y, z in chips], axis=0
        )

        for pair in range(HERE // 2):
            values = self.frames[pair * 2 * HALF : (pair + 1) * 2 * HALF, :]
            spectra = lax.dot_general(
                rows, values, (((1,), (1,)), ((), ())), preferred_element_type=jnp.float32
            )
            for dest in range(2 * per_group):
                for j in range(2):
                    self.turned[
                        pl.ds(dest * 8 * O_STRIDE + pair * 2 + j, 8, stride=O_STRIDE), :
                    ] = spectra[dest * 8 : (dest + 1) * 8, j * HALF : (j + 1) * HALF]

    def pack(self, dest, target):
        for m in range(0, 8, 2):
            pair_rows = jnp.concatenate(
                [
                    self.turned[pl.ds((dest * 8 + m) * O_STRIDE, HERE), :],
                    self.turned[pl.ds((dest * 8 + m + 1) * O_STRIDE, HERE), :],
                ],
                axis=0,
            )
            target[m * 8 : (m + 2) * 8, :] = pair_rows.astype(jnp.bfloat16)

    def send(self, source, target, device, send_sem, recv_sem):
        pltpu.make_async_remote_copy(
            src_ref=source,
            dst_ref=target,
            send_sem=send_sem,
            recv_sem=recv_sem,
            device_id=device,
            device_id_type=MESH,
        ).start()

    def send_direct(self, group, step, change, source, target, send_sem, recv_sem):
        core = self.my_core if change == 0 else 1 - self.my_core
        slot = (group * self.dims[0] * self.dims[1] + step) * 2 + core
        chip = self.chip_of(group, step)
        self.send(
            source.at[slot], target.at[self.me], self.device(chip, core), send_sem, recv_sem
        )


def exchange_kernel(dims, samples, delays, flags, taps, table, out, raw, rim, ready, *rest):
    refs, sems = rest[:6], rest[6:]
    load_sem, table_sem, rim_send, rim_recv, send_sem, recv_sem, own_sem = sems
    work = Work(dims, delays, flags, refs)
    nx, ny, nz = dims
    per_group = nx * ny
    inp = nx * ny * nz
    devices = 2 * inp

    def load(first, count, sem):
        part = pl.ds(first * FRAME, count * FRAME)
        copy = pltpu.make_async_copy(samples.at[:, part], raw.at[:, part], sem)
        copy.start()
        return copy

    late_loads = [
        load(first, count, load_sem.at[piece]) for piece, (first, count) in enumerate(PIECES)
    ]
    fetch = pltpu.make_async_copy(table, work.rows_table, table_sem)
    fetch.start()
    early_load = load(0, SPLIT, load_sem.at[len(PIECES)])
    barrier = pltpu.get_barrier_semaphore()

    def greet(step):
        other = rem(work.me + step, devices)
        pl.semaphore_signal(
            barrier, inc=1, device_id=(div(other, inp), rem(other, inp)), device_id_type=MESH
        )

    @pl.loop(1, 1 + GREET_FIRST)
    def _(step):
        greet(step)

    work.place_taps(taps)

    def send_direct(half, group, step):
        common = (ready.at[half], out.at[half], send_sem.at[half], recv_sem.at[half])

        @pl.when(group + step > 0)
        def _():
            work.send_direct(group, step, 0, *common)

        @pl.when(group + step == 0)
        def _():
            pltpu.make_async_copy(
                ready.at[half, work.my_core], out.at[half, work.me], own_sem.at[half]
            ).start()

        work.send_direct(group, step, 1, *common)

    def send_chip(half, slot):
        send_direct(half, div(slot, per_group), rem(slot, per_group))

    def send_later(order):
        later = per_group - AT_ONCE
        send_direct(1, div(order, later), AT_ONCE + rem(order, later))

    def transform_half(half, each_group, each_step):
        @pl.loop(0, nz)
        def _(group):
            work.transform(group)

            @pl.loop(0, per_group, step=4)
            def _(chips):
                for dest in range(8):
                    dest = chips * 2 + dest
                    work.pack(dest, ready.at[half, group * 2 * per_group + dest])
                if each_step is not None:
                    each_step(group * 4 + div(chips, 4))

            if each_group is not None:
                each_group(group)

    def some_now(group):
        @pl.loop(0, AT_ONCE)
        def _(step):
            send_direct(1, group, step)

    def in_spread(step):
        @pl.when(rem(step, 3) == 0)
        def _():
            send_later(div(step, 3))

    def in_filter(run):
        @pl.when(rem(run, 3) == 0)
        def _():
            send_later(9 + div(run, 3))

    def in_transform(step):
        @pl.when(step < 13)
        def _():
            send_later(31 + step)

    greeted = 1 + GREET_FIRST
    for piece, (first, count) in enumerate(PIECES):
        late_loads[piece].wait()
        whole = count // 4 * 4

        def in_late(step, begin=greeted):
            for k in range(GREET_STEP):
                greet(begin + step * GREET_STEP + k)

        greeting = greeted < devices
        work.spread(raw, FIRST, (first, first + whole), 4, in_late if greeting else None)
        if greeting:
            greeted += whole // 4 * GREET_STEP
        if whole < count:
            work.spread(raw, FIRST, (first + whole, first + count), 1)
    assert greeted == devices
    pl.semaphore_wait(barrier, devices - 1)
    rim_copy = pltpu.make_async_remote_copy(
        src_ref=samples.at[:, pl.ds(S_DEV * FRAME - HALO, HALO)],
        dst_ref=rim,
        send_sem=rim_send,
        recv_sem=rim_recv,
        device_id=(1 - work.tseg, work.here),
        device_id_type=MESH,
    )
    rim_copy.start()
    work.run_half(1)
    fetch.wait()
    transform_half(1, some_now, None)

    early_load.wait()
    work.spread(raw, FIRST, (0, SPLIT - 3), 4, in_spread)
    work.spread(raw, FIRST, (SPLIT - 3, SPLIT), 1)
    rim_copy.wait()

    @pl.when(work.tseg == 0)
    def _():
        rim[...] = jnp.zeros_like(rim)

    work.spread(rim, 1, (0, 20), 4)
    work.spread(rim, 1, (20, HALO // FRAME), 1)
    work.run_half(0, in_filter)
    transform_half(0, None, in_transform)

    @pl.loop(0, nz * per_group)
    def _(slot):
        send_chip(0, slot)

    for half in (1, 0):
        pltpu.make_async_copy(
            ready.at[half, work.my_core], out.at[half, work.me], own_sem.at[half]
        ).wait()
        sent = ready.at[half, pl.ds(0, devices - 1)]
        pltpu.make_async_copy(sent, sent, send_sem.at[half]).wait()
        arrived = out.at[half, pl.ds(0, devices - 1)]
        pltpu.make_async_copy(arrived, arrived, recv_sem.at[half]).wait()


def correlate_kernel(segments, scale, source, vis_real, vis_imag, loaded, sem):
    channel = pl.program_id(0)

    def load(c, half):
        rows = pl.ds(pl.multiple_of(c * 2 * HERE, 2 * HERE), 2 * HERE)
        return pltpu.make_async_copy(
            source.at[half, :, rows, :], loaded.at[c, half], sem.at[c, half]
        )

    @pl.when(channel == 0)
    def _():
        for c in range(CHAN):
            for half in range(2):
                load(c, half).start()

    for half in range(2):
        load(channel, half).wait()
    spectra = loaded.at[channel]
    sources = spectra.shape[1] // segments
    inputs = sources * HERE
    real, imag = [], []
    for half in range(2):
        for segment in range(segments):
            piece = spectra[half, segment * sources : (segment + 1) * sources].astype(jnp.float32)
            real.append(piece[:, :HERE].reshape(inputs, HALF).astype(jnp.bfloat16))
            imag.append(piece[:, HERE:].reshape(inputs, HALF).astype(jnp.bfloat16))
    real = jnp.concatenate(real, axis=1)
    imag = jnp.concatenate(imag, axis=1)

    def product(a, b):
        return lax.dot_general(a, b, (((1,), (1,)), ((), ())), preferred_element_type=jnp.float32)

    middle = inputs // 2
    low, high = slice(0, middle), slice(middle, inputs)
    for rows, columns in ((low, low), (high, high), (low, high)):
        block = product(real[rows], real[columns]) + product(imag[rows], imag[columns])
        vis_real[0, rows, columns] = block * scale
        if rows != columns:
            vis_real[0, columns, rows] = block.T * scale
    cross = product(real, imag)
    vis_imag[0] = (cross - cross.T) * scale


def per_device(samples, delays, flags, taps, *, segments, inp):
    nx, nz, ny_hi = SHAPES[inp]
    dims = (nx, 2 * ny_hi, nz)
    devices = segments * inp
    per_group = nx * 2 * ny_hi
    table = jnp.asarray(dft_rows(*dims))
    anywhere = pl.BlockSpec(memory_space=pl.ANY)
    in_specs = [
        anywhere,
        pl.BlockSpec(memory_space=pltpu.SMEM),
        pl.BlockSpec(memory_space=pltpu.SMEM),
        pl.BlockSpec(memory_space=pltpu.VMEM),
        anywhere,
    ]
    work_scratch = [
        pltpu.VMEM((nz * per_group, 16, FRAME), jnp.bfloat16),
        pltpu.VMEM((BLOCKS * HERE * RUN + 8, LANES), jnp.float32),
        pltpu.VMEM((BLOCKS * TAPS * 8, LANES), jnp.float32),
        pltpu.VMEM((HERE * BLOCKS * WINDOW, LANES), jnp.float32),
        pltpu.VMEM((HERE * HALF, FRAME), jnp.bfloat16),
        pltpu.VMEM((2 * per_group * 8 * O_STRIDE, LANES), jnp.float32),
    ]
    raw = pltpu.VMEM((HERE, S_DEV * FRAME), jnp.bfloat16)
    dma = pltpu.SemaphoreType.DMA
    spectra = pl.pallas_call(
        functools.partial(exchange_kernel, dims),
        out_shape=jax.ShapeDtypeStruct((2, devices, ROWS, HALF), jnp.bfloat16),
        in_specs=in_specs,
        out_specs=anywhere,
        scratch_shapes=[
            raw,
            pltpu.VMEM((HERE, HALO), jnp.bfloat16),
            pltpu.VMEM((2, devices, ROWS, HALF), jnp.bfloat16),
            *work_scratch,
            dma((len(PIECES) + 1,)),
            *[dma] * 3,
            *[dma((2,))] * 3,
        ],
        compiler_params=pltpu.CompilerParams(
            collective_id=0, has_side_effects=True, vmem_limit_bytes=60 * 2**20
        ),
        name="exchange",
    )(samples, delays, flags, taps, table)
    inputs = inp * HERE
    visibility = jax.ShapeDtypeStruct((CHAN, inputs, inputs), jnp.float32)
    return pl.pallas_call(
        functools.partial(correlate_kernel, segments, 1.0 / (S_DEV * segments)),
        out_shape=(visibility, visibility),
        grid=(CHAN,),
        in_specs=[anywhere],
        out_specs=(
            pl.BlockSpec((1, inputs, inputs), lambda c: (c, 0, 0)),
            pl.BlockSpec((1, inputs, inputs), lambda c: (c, 0, 0)),
        ),
        scratch_shapes=[
            pltpu.VMEM((CHAN, 2, devices, 2 * HERE, HALF), jnp.bfloat16),
            dma((CHAN, 2)),
        ],
        compiler_params=pltpu.CompilerParams(vmem_limit_bytes=60 * 2**20),
        name="correlate",
    )(spectra)


def solution(mesh):
    segments, inp = mesh.shape["tseg"], mesh.shape["inp"]
    return jax.shard_map(
        functools.partial(per_device, segments=segments, inp=inp),
        mesh=mesh,
        in_specs=(P("inp", "tseg"), P("inp"), P("inp"), P()),
        out_specs=(P(("tseg", "inp"), None, None), P(("tseg", "inp"), None, None)),
        check_vma=False,
    )
```

```python
import functools
import math

import jax
import jax.numpy as jnp
import ml_dtypes
import numpy as np
from jax import lax
from jax.experimental import pallas as pl
from jax.experimental.pallas import tpu as pltpu
from jax.sharding import PartitionSpec as P

MESH = pl.DeviceIdType.MESH
TAPS = 16
FRAME = 1024
HALO = 23552
LANES = 128
BLOCKS = FRAME // LANES
HERE = 8
S_DEV = 256
HALF = 128
CHAN = 4
ROWS = CHAN * 2 * HERE
FIRST = HALO // FRAME + 1
RUN = FIRST + S_DEV + 1
WINDOW = HALF + TAPS
SPLIT = 103
O_STRIDE = HERE + 1
PIECES = ((103, 40), (143, 40), (183, 40), (223, 33))
GREET_FIRST = 37
GREET_STEP = 3
BEHIND = 32
AT_ONCE = 5
SHAPES = {64: (4, 4, 2), 4: (2, 1, 1)}


def dft_rows(nx, ny, nz):
    count = nx * ny * nz * 2
    inp = count // 2
    k = np.arange(FRAME)[None, :]
    q = np.arange(count * CHAN)[:, None]
    phase = ((q * k) % FRAME).astype(np.float64) * (2.0 * math.pi / FRAME)
    parts = np.stack([np.cos(phase), -np.sin(phase)], axis=1) / math.sqrt(FRAME)
    parts = parts.astype(np.float32).astype(ml_dtypes.bfloat16)
    parts = parts.reshape(2, nx, nz, ny // 2, 2, CHAN * 2, FRAME)
    parts = parts.transpose(1, 3, 0, 2, 4, 5, 6)
    assert inp * 2 == count
    return parts.reshape(nx * ny * nz, 2 * CHAN * 2, FRAME)


def rem(a, b):
    return lax.rem(a, jnp.int32(b))


def div(a, b):
    return lax.div(a, jnp.int32(b))


class Work:
    def __init__(self, dims, delays, flags, refs):
        self.dims = dims
        self.delays, self.flags = delays, flags
        self.rows_table, self.runs, self.tap_rows, self.delayed, self.frames, self.turned = refs
        nx, ny, nz = dims
        self.inp = nx * nz * ny
        self.tseg = lax.axis_index("tseg")
        self.here = lax.axis_index("inp")
        self.me = self.tseg * self.inp + self.here
        self.my_core = rem(self.here, 2)
        self.my_y = rem(div(self.here, 2), ny // 2) * 2 + self.tseg
        self.my_z = rem(div(self.here, ny), nz)
        self.my_x = div(self.here, ny * nz)
        self.sign = 1 - 2 * self.my_core
        self.lane = lax.broadcasted_iota(jnp.int32, (HERE, LANES), 1)

    def offset(self, group, step):
        nx, ny, nz = self.dims
        dx = rem(step, nx)
        dy = div(step, nx)
        return dx, dy, rem(group + 2 * nz - dx - dy, nz)

    def chip_at(self, dx, dy, dz):
        nx, ny, nz = self.dims
        return (
            rem(self.my_x + nx + dx, nx),
            rem(self.my_y + ny + dy, ny),
            rem(self.my_z + nz + dz, nz),
        )

    def chip_of(self, group, step):
        return self.chip_at(*[self.sign * d for d in self.offset(group, step)])

    def tied(self, group, step):
        dx, dy, dz = self.offset(group, step)
        return jnp.logical_or(jnp.logical_or(dx == 2, dy == 2), dz == 2)

    def device(self, chip, core):
        nx, ny, nz = self.dims
        x, y, z = chip
        return rem(y, 2), ((x * nz + z) * (ny // 2) + div(y, 2)) * 2 + core

    def place_taps(self, taps):
        for block in range(BLOCKS):
            for p in range(TAPS):
                self.tap_rows[pl.ds((block * TAPS + p) * 8, 8), :] = jnp.broadcast_to(
                    taps[p : p + 1, block * LANES : (block + 1) * LANES], (8, LANES)
                )

    def spread(self, source, first, frame_range, unroll, each=None):
        row = lax.broadcasted_iota(jnp.int32, (HERE, LANES), 0)
        turn = jnp.zeros((HERE, LANES), jnp.int32)
        for i in range(HERE):
            turn = jnp.where(row == i, self.delays[i] % LANES, turn)
        index = (self.lane - turn + LANES) % LANES

        @pl.loop(*frame_range, step=unroll)
        def _(start):
            for frame in range(unroll):
                frame = start + frame
                values = source[:, pl.ds(pl.multiple_of(frame * FRAME, FRAME), FRAME)].astype(
                    jnp.float32
                )
                for block in range(BLOCKS):
                    moved = jnp.take_along_axis(
                        values[:, block * LANES : (block + 1) * LANES], index, axis=1
                    )
                    self.runs[pl.ds(block * HERE * RUN + first + frame, HERE, stride=RUN), :] = (
                        moved
                    )
            if each is not None:
                each(div(start - frame_range[0], unroll))

    def run_half(self, half, each=None):
        base = half * HALF - (TAPS - 1)

        @pl.loop(0, HERE * BLOCKS)
        def _(run):
            i = div(run, BLOCKS)
            block = rem(run, BLOCKS)
            delay = self.delays[i]
            keep = self.lane >= delay % LANES
            weight = self.flags[i].astype(jnp.float32)

            def start(back):
                moved = block - delay // LANES - back + 9 * BLOCKS
                return (moved % BLOCKS * HERE + i) * RUN + moved // BLOCKS - 9 + FIRST + base

            now, before = start(0), start(1)
            for f in range(0, WINDOW, 8):
                self.delayed[pl.ds(pl.multiple_of(run * WINDOW, 8) + f, 8), :] = jnp.where(
                    keep, self.runs[pl.ds(now + f, 8), :], self.runs[pl.ds(before + f, 8), :]
                )
            tap = [self.tap_rows[pl.ds((block * TAPS + p) * 8, 8), :] for p in range(TAPS)]
            total = {}
            for f in range(HALF + 8):
                values = self.delayed[pl.ds(run * WINDOW + f, 8), :]
                for p in (f % 8 + 8, f % 8):
                    s = f - p
                    if 0 <= s < HALF:
                        total[s] = tap[p] * values if p == 0 else total[s] + tap[p] * values
                if f % 16 == 15 and f > 16:
                    pair = [total.pop(f - 31), total.pop(f - 23)]
                    self.frames[
                        pl.ds(pl.multiple_of(i * HALF, HALF) + f - 31, 16),
                        pl.ds(pl.multiple_of(block * LANES, LANES), LANES),
                    ] = (jnp.concatenate(pair, axis=0) * weight).astype(jnp.bfloat16)
            pair = [total.pop(HALF - 16), total.pop(HALF - 8)]
            self.frames[
                pl.ds(pl.multiple_of(i * HALF, HALF) + HALF - 16, 16),
                pl.ds(pl.multiple_of(block * LANES, LANES), LANES),
            ] = (jnp.concatenate(pair, axis=0) * weight).astype(jnp.bfloat16)
            assert not total
            if each is not None:
                each(run)

    def transform(self, group):
        nx, ny, nz = self.dims
        per_group = nx * ny
        chips = [self.chip_of(group, jnp.int32(step)) for step in range(per_group)]
        rows = jnp.concatenate(
            [self.rows_table[(x * ny + y) * nz + z] for x, y, z in chips], axis=0
        )

        for pair in range(HERE // 2):
            values = self.frames[pair * 2 * HALF : (pair + 1) * 2 * HALF, :]
            spectra = lax.dot_general(
                rows, values, (((1,), (1,)), ((), ())), preferred_element_type=jnp.float32
            )
            for dest in range(2 * per_group):
                for j in range(2):
                    self.turned[
                        pl.ds(dest * 8 * O_STRIDE + pair * 2 + j, 8, stride=O_STRIDE), :
                    ] = spectra[dest * 8 : (dest + 1) * 8, j * HALF : (j + 1) * HALF]

    def pack(self, dest, target):
        for m in range(0, 8, 2):
            pair_rows = jnp.concatenate(
                [
                    self.turned[pl.ds((dest * 8 + m) * O_STRIDE, HERE), :],
                    self.turned[pl.ds((dest * 8 + m + 1) * O_STRIDE, HERE), :],
                ],
                axis=0,
            )
            target[m * 8 : (m + 2) * 8, :] = pair_rows.astype(jnp.bfloat16)

    def send(self, source, target, device, send_sem, recv_sem):
        pltpu.make_async_remote_copy(
            src_ref=source,
            dst_ref=target,
            send_sem=send_sem,
            recv_sem=recv_sem,
            device_id=device,
            device_id_type=MESH,
        ).start()

    def pass_by(self, group, step, change, source, relay, send_sem, relay_sem):
        way = (1, -1)[change]
        chip = self.chip_at(*[jnp.where(d == 2, way, 0) for d in self.offset(group, step)])
        slot = (group * self.dims[0] * self.dims[1] + step) * 2
        core = self.my_core if change == 0 else 1 - self.my_core
        self.send(
            source.at[slot + core],
            relay.at[slot + change],
            self.device(chip, self.my_core),
            send_sem,
            relay_sem.at[slot + change],
        )

    def pass_on(self, group, step, change, relay, relay_sem, target, send_sem, recv_sem):
        way = (1, -1)[change]
        offset = self.offset(group, step)
        slot = (group * self.dims[0] * self.dims[1] + step) * 2 + change
        message = relay.at[slot]
        pltpu.make_async_copy(message, message, relay_sem.at[slot]).wait()
        origin_y, origin_inp = self.device(
            self.chip_at(*[jnp.where(d == 2, -way, 0) for d in offset]), self.my_core
        )
        chip = self.chip_at(*[jnp.where(d == 2, way, self.sign * d) for d in offset])
        self.send(
            message,
            target.at[origin_y * self.inp + origin_inp],
            self.device(chip, self.my_core if change == 0 else 1 - self.my_core),
            send_sem,
            recv_sem,
        )

    def send_direct(self, group, step, change, source, target, send_sem, recv_sem):
        core = self.my_core if change == 0 else 1 - self.my_core
        slot = (group * self.dims[0] * self.dims[1] + step) * 2 + core
        chip = self.chip_of(group, step)
        self.send(
            source.at[slot], target.at[self.me], self.device(chip, core), send_sem, recv_sem
        )


def exchange_kernel(dims, samples, delays, flags, taps, table, out, raw, rim, ready, *rest):
    relay, refs, sems = rest[0], rest[1:7], rest[7:]
    load_sem, table_sem, rim_send, rim_recv, send_sem, recv_sem, own_sem = sems[:7]
    relay_send, relay_sem = sems[7:]
    work = Work(dims, delays, flags, refs)
    nx, ny, nz = dims
    per_group = nx * ny
    inp = nx * ny * nz
    devices = 2 * inp
    ties = 2 * (inp - (nx - 1) * (ny - 1) * (nz - 1))

    def load(first, count, sem):
        part = pl.ds(first * FRAME, count * FRAME)
        copy = pltpu.make_async_copy(samples.at[:, part], raw.at[:, part], sem)
        copy.start()
        return copy

    late_loads = [
        load(first, count, load_sem.at[piece]) for piece, (first, count) in enumerate(PIECES)
    ]
    fetch = pltpu.make_async_copy(table, work.rows_table, table_sem)
    fetch.start()
    early_load = load(0, SPLIT, load_sem.at[len(PIECES)])
    barrier = pltpu.get_barrier_semaphore()

    def greet(step):
        other = rem(work.me + step, devices)
        pl.semaphore_signal(
            barrier, inc=1, device_id=(div(other, inp), rem(other, inp)), device_id_type=MESH
        )

    @pl.loop(1, 1 + GREET_FIRST)
    def _(step):
        greet(step)

    work.place_taps(taps)

    def send_chip(half, group, step):
        common = (ready.at[half], out.at[half], send_sem.at[half], recv_sem.at[half])
        tied = work.tied(group, step)

        @pl.when(tied)
        def _():
            for change in range(2):
                work.pass_by(
                    group,
                    step,
                    change,
                    ready.at[half],
                    relay.at[half],
                    send_sem.at[half],
                    relay_sem.at[half],
                )

        @pl.when(jnp.logical_not(tied))
        def _():
            @pl.when(group + step > 0)
            def _():
                work.send_direct(group, step, 0, *common)

            @pl.when(group + step == 0)
            def _():
                pltpu.make_async_copy(
                    ready.at[half, work.my_core], out.at[half, work.me], own_sem.at[half]
                ).start()

            work.send_direct(group, step, 1, *common)

    def pass_on(half, group, step):
        @pl.when(work.tied(group, step))
        def _():
            for change in range(2):
                work.pass_on(
                    group,
                    step,
                    change,
                    relay.at[half],
                    relay_sem.at[half],
                    out.at[half],
                    relay_send.at[half],
                    recv_sem.at[half],
                )

    later = per_group - AT_ONCE

    def pass_early(order):
        pass_on(1, div(order, AT_ONCE), rem(order, AT_ONCE))

    def pass_later(order):
        pass_on(1, div(order, later), AT_ONCE + rem(order, later))

    def send_later(order):
        send_chip(1, div(order, later), AT_ONCE + rem(order, later))
        early = nz * AT_ONCE

        @pl.when(order < early)
        def _():
            pass_early(order)

        @pl.when(order >= early)
        def _():
            pass_later(order - early)

    def transform_half(half, each_group, each_step):
        @pl.loop(0, nz)
        def _(group):
            work.transform(group)

            @pl.loop(0, per_group, step=4)
            def _(chips):
                for dest in range(8):
                    dest = chips * 2 + dest
                    work.pack(dest, ready.at[half, group * 2 * per_group + dest])
                if each_step is not None:
                    each_step(group * 4 + div(chips, 4))

            if each_group is not None:
                each_group(group)

    def some_now(group):
        @pl.loop(0, AT_ONCE)
        def _(step):
            send_chip(1, group, step)

    def in_spread(step):
        @pl.when(rem(step, 3) == 0)
        def _():
            send_later(div(step, 3))

    def in_filter(run):
        @pl.when(rem(run, 3) == 0)
        def _():
            send_later(9 + div(run, 3))

    def in_transform(step):
        @pl.when(step < 13)
        def _():
            send_later(31 + step)

    greeted = 1 + GREET_FIRST
    for piece, (first, count) in enumerate(PIECES):
        late_loads[piece].wait()
        whole = count // 4 * 4

        def in_late(step, begin=greeted):
            for k in range(GREET_STEP):
                greet(begin + step * GREET_STEP + k)

        greeting = greeted < devices
        work.spread(raw, FIRST, (first, first + whole), 4, in_late if greeting else None)
        if greeting:
            greeted += whole // 4 * GREET_STEP
        if whole < count:
            work.spread(raw, FIRST, (first + whole, first + count), 1)
    assert greeted == devices
    pl.semaphore_wait(barrier, devices - 1)
    rim_copy = pltpu.make_async_remote_copy(
        src_ref=samples.at[:, pl.ds(S_DEV * FRAME - HALO, HALO)],
        dst_ref=rim,
        send_sem=rim_send,
        recv_sem=rim_recv,
        device_id=(1 - work.tseg, work.here),
        device_id_type=MESH,
    )
    rim_copy.start()
    work.run_half(1)
    fetch.wait()
    transform_half(1, some_now, None)

    early_load.wait()
    work.spread(raw, FIRST, (0, SPLIT - 3), 4, in_spread)
    work.spread(raw, FIRST, (SPLIT - 3, SPLIT), 1)
    rim_copy.wait()

    @pl.when(work.tseg == 0)
    def _():
        rim[...] = jnp.zeros_like(rim)

    work.spread(rim, 1, (0, 20), 4)
    work.spread(rim, 1, (20, HALO // FRAME), 1)
    work.run_half(0, in_filter)
    transform_half(0, None, in_transform)

    chips = nz * per_group
    left = nz * AT_ONCE

    def send_second(slot):
        send_chip(0, div(slot, per_group), rem(slot, per_group))

    def pass_second(slot):
        pass_on(0, div(slot, per_group), rem(slot, per_group))

    @pl.loop(0, left)
    def _(slot):
        pass_later(nz * later - left + slot)
        send_second(slot)

    @pl.loop(left, BEHIND)
    def _(slot):
        send_second(slot)

    @pl.loop(BEHIND, chips)
    def _(slot):
        send_second(slot)
        pass_second(slot - BEHIND)

    @pl.loop(chips - BEHIND, chips)
    def _(slot):
        pass_second(slot)

    for half in (1, 0):
        pltpu.make_async_copy(
            ready.at[half, work.my_core], out.at[half, work.me], own_sem.at[half]
        ).wait()
        sent = ready.at[half, pl.ds(0, devices - 1)]
        pltpu.make_async_copy(sent, sent, send_sem.at[half]).wait()
        passed = relay.at[half, pl.ds(0, ties)]
        pltpu.make_async_copy(passed, passed, relay_send.at[half]).wait()
        arrived = out.at[half, pl.ds(0, devices - 1)]
        pltpu.make_async_copy(arrived, arrived, recv_sem.at[half]).wait()


def correlate_kernel(segments, scale, source, vis_real, vis_imag, loaded, sem):
    channel = pl.program_id(0)

    def load(c, half):
        rows = pl.ds(pl.multiple_of(c * 2 * HERE, 2 * HERE), 2 * HERE)
        return pltpu.make_async_copy(
            source.at[half, :, rows, :], loaded.at[c, half], sem.at[c, half]
        )

    @pl.when(channel == 0)
    def _():
        for c in range(CHAN):
            for half in range(2):
                load(c, half).start()

    for half in range(2):
        load(channel, half).wait()
    spectra = loaded.at[channel]
    sources = spectra.shape[1] // segments
    inputs = sources * HERE
    real, imag = [], []
    for half in range(2):
        for segment in range(segments):
            piece = spectra[half, segment * sources : (segment + 1) * sources].astype(jnp.float32)
            real.append(piece[:, :HERE].reshape(inputs, HALF).astype(jnp.bfloat16))
            imag.append(piece[:, HERE:].reshape(inputs, HALF).astype(jnp.bfloat16))
    real = jnp.concatenate(real, axis=1)
    imag = jnp.concatenate(imag, axis=1)

    def product(a, b):
        return lax.dot_general(a, b, (((1,), (1,)), ((), ())), preferred_element_type=jnp.float32)

    middle = inputs // 2
    low, high = slice(0, middle), slice(middle, inputs)
    for rows, columns in ((low, low), (high, high), (low, high)):
        block = product(real[rows], real[columns]) + product(imag[rows], imag[columns])
        vis_real[0, rows, columns] = block * scale
        if rows != columns:
            vis_real[0, columns, rows] = block.T * scale
    cross = product(real, imag)
    vis_imag[0] = (cross - cross.T) * scale


def per_device(samples, delays, flags, taps, *, segments, inp):
    nx, nz, ny_hi = SHAPES[inp]
    dims = (nx, 2 * ny_hi, nz)
    devices = segments * inp
    per_group = nx * 2 * ny_hi
    table = jnp.asarray(dft_rows(*dims))
    anywhere = pl.BlockSpec(memory_space=pl.ANY)
    in_specs = [
        anywhere,
        pl.BlockSpec(memory_space=pltpu.SMEM),
        pl.BlockSpec(memory_space=pltpu.SMEM),
        pl.BlockSpec(memory_space=pltpu.VMEM),
        anywhere,
    ]
    work_scratch = [
        pltpu.VMEM((nz * per_group, 16, FRAME), jnp.bfloat16),
        pltpu.VMEM((BLOCKS * HERE * RUN + 8, LANES), jnp.float32),
        pltpu.VMEM((BLOCKS * TAPS * 8, LANES), jnp.float32),
        pltpu.VMEM((HERE * BLOCKS * WINDOW, LANES), jnp.float32),
        pltpu.VMEM((HERE * HALF, FRAME), jnp.bfloat16),
        pltpu.VMEM((2 * per_group * 8 * O_STRIDE, LANES), jnp.float32),
    ]
    raw = pltpu.VMEM((HERE, S_DEV * FRAME), jnp.bfloat16)
    dma = pltpu.SemaphoreType.DMA
    spectra = pl.pallas_call(
        functools.partial(exchange_kernel, dims),
        out_shape=jax.ShapeDtypeStruct((2, devices, ROWS, HALF), jnp.bfloat16),
        in_specs=in_specs,
        out_specs=anywhere,
        scratch_shapes=[
            raw,
            pltpu.VMEM((HERE, HALO), jnp.bfloat16),
            pltpu.VMEM((2, devices, ROWS, HALF), jnp.bfloat16),
            pltpu.VMEM((2, devices, ROWS, HALF), jnp.bfloat16),
            *work_scratch,
            dma((len(PIECES) + 1,)),
            *[dma] * 3,
            *[dma((2,))] * 4,
            dma((2, devices)),
        ],
        compiler_params=pltpu.CompilerParams(
            collective_id=0, has_side_effects=True, vmem_limit_bytes=60 * 2**20
        ),
        name="exchange",
    )(samples, delays, flags, taps, table)
    inputs = inp * HERE
    visibility = jax.ShapeDtypeStruct((CHAN, inputs, inputs), jnp.float32)
    return pl.pallas_call(
        functools.partial(correlate_kernel, segments, 1.0 / (S_DEV * segments)),
        out_shape=(visibility, visibility),
        grid=(CHAN,),
        in_specs=[anywhere],
        out_specs=(
            pl.BlockSpec((1, inputs, inputs), lambda c: (c, 0, 0)),
            pl.BlockSpec((1, inputs, inputs), lambda c: (c, 0, 0)),
        ),
        scratch_shapes=[
            pltpu.VMEM((CHAN, 2, devices, 2 * HERE, HALF), jnp.bfloat16),
            dma((CHAN, 2)),
        ],
        compiler_params=pltpu.CompilerParams(vmem_limit_bytes=60 * 2**20),
        name="correlate",
    )(spectra)


def solution(mesh):
    segments, inp = mesh.shape["tseg"], mesh.shape["inp"]
    return jax.shard_map(
        functools.partial(per_device, segments=segments, inp=inp),
        mesh=mesh,
        in_specs=(P("inp", "tseg"), P("inp"), P("inp"), P()),
        out_specs=(P(("tseg", "inp"), None, None), P(("tseg", "inp"), None, None)),
        check_vma=False,
    )
```

```python
import functools
import math

import jax
import jax.numpy as jnp
import ml_dtypes
import numpy as np
from jax import lax
from jax.experimental import pallas as pl
from jax.experimental.pallas import tpu as pltpu
from jax.sharding import PartitionSpec as P

MESH = pl.DeviceIdType.MESH
TAPS = 16
FRAME = 1024
HALO = 23552
LANES = 128
BLOCKS = FRAME // LANES
HERE = 8
S_DEV = 256
HALF = 128
CHAN = 4
ROWS = CHAN * 2 * HERE
FIRST = HALO // FRAME + 1
RUN = FIRST + S_DEV + 1
WINDOW = HALF + TAPS
SPLIT = 103
O_STRIDE = HERE + 1
PIECES = ((103, 40), (143, 40), (183, 40), (223, 33))
GREET_FIRST = 37
GREET_STEP = 3
PART = ROWS // 2
AT_ONCE = 8
SHAPES = {64: (4, 4, 2), 4: (2, 1, 1)}


def dft_rows(nx, ny, nz):
    count = nx * ny * nz * 2
    inp = count // 2
    k = np.arange(FRAME)[None, :]
    q = np.arange(count * CHAN)[:, None]
    phase = ((q * k) % FRAME).astype(np.float64) * (2.0 * math.pi / FRAME)
    parts = np.stack([np.cos(phase), -np.sin(phase)], axis=1) / math.sqrt(FRAME)
    parts = parts.astype(np.float32).astype(ml_dtypes.bfloat16)
    parts = parts.reshape(2, nx, nz, ny // 2, 2, CHAN * 2, FRAME)
    parts = parts.transpose(1, 3, 0, 2, 4, 5, 6)
    assert inp * 2 == count
    return parts.reshape(nx * ny * nz, 2 * CHAN * 2, FRAME)


def rem(a, b):
    return lax.rem(a, jnp.int32(b))


def div(a, b):
    return lax.div(a, jnp.int32(b))


class Work:
    def __init__(self, dims, delays, flags, refs):
        self.dims = dims
        self.delays, self.flags = delays, flags
        self.rows_table, self.runs, self.tap_rows, self.delayed, self.frames, self.turned = refs
        nx, ny, nz = dims
        self.inp = nx * nz * ny
        self.tseg = lax.axis_index("tseg")
        self.here = lax.axis_index("inp")
        self.me = self.tseg * self.inp + self.here
        self.my_core = rem(self.here, 2)
        self.my_y = rem(div(self.here, 2), ny // 2) * 2 + self.tseg
        self.my_z = rem(div(self.here, ny), nz)
        self.my_x = div(self.here, ny * nz)
        self.sign = 1 - 2 * self.my_core
        self.lane = lax.broadcasted_iota(jnp.int32, (HERE, LANES), 1)

    def chip_of(self, group, step):
        nx, ny, nz = self.dims
        dx = rem(step, nx)
        dy = div(step, nx)
        dz = group + 2 * nz - dx - dy
        return (
            rem(self.my_x + nx + self.sign * dx, nx),
            rem(self.my_y + ny + self.sign * dy, ny),
            rem(self.my_z + 4 * nz + self.sign * dz, nz),
        )

    def device(self, chip, core):
        nx, ny, nz = self.dims
        x, y, z = chip
        return rem(y, 2), ((x * nz + z) * (ny // 2) + div(y, 2)) * 2 + core

    def place_taps(self, taps):
        for block in range(BLOCKS):
            for p in range(TAPS):
                self.tap_rows[pl.ds((block * TAPS + p) * 8, 8), :] = jnp.broadcast_to(
                    taps[p : p + 1, block * LANES : (block + 1) * LANES], (8, LANES)
                )

    def spread(self, source, first, frame_range, unroll, each=None):
        row = lax.broadcasted_iota(jnp.int32, (HERE, LANES), 0)
        turn = jnp.zeros((HERE, LANES), jnp.int32)
        for i in range(HERE):
            turn = jnp.where(row == i, self.delays[i] % LANES, turn)
        index = (self.lane - turn + LANES) % LANES

        @pl.loop(*frame_range, step=unroll)
        def _(start):
            for frame in range(unroll):
                frame = start + frame
                values = source[:, pl.ds(pl.multiple_of(frame * FRAME, FRAME), FRAME)].astype(
                    jnp.float32
                )
                for block in range(BLOCKS):
                    moved = jnp.take_along_axis(
                        values[:, block * LANES : (block + 1) * LANES], index, axis=1
                    )
                    self.runs[pl.ds(block * HERE * RUN + first + frame, HERE, stride=RUN), :] = (
                        moved
                    )
            if each is not None:
                each(div(start - frame_range[0], unroll))

    def run_half(self, half, inputs, each=None):
        base = half * HALF - (TAPS - 1)

        @pl.loop(inputs[0] * BLOCKS, inputs[1] * BLOCKS)
        def _(run):
            i = div(run, BLOCKS)
            block = rem(run, BLOCKS)
            delay = self.delays[i]
            keep = self.lane >= delay % LANES
            weight = self.flags[i].astype(jnp.float32)

            def start(back):
                moved = block - delay // LANES - back + 9 * BLOCKS
                return (moved % BLOCKS * HERE + i) * RUN + moved // BLOCKS - 9 + FIRST + base

            now, before = start(0), start(1)
            for f in range(0, WINDOW, 8):
                self.delayed[pl.ds(pl.multiple_of(run * WINDOW, 8) + f, 8), :] = jnp.where(
                    keep, self.runs[pl.ds(now + f, 8), :], self.runs[pl.ds(before + f, 8), :]
                )
            tap = [self.tap_rows[pl.ds((block * TAPS + p) * 8, 8), :] for p in range(TAPS)]
            total = {}
            for f in range(HALF + 8):
                values = self.delayed[pl.ds(run * WINDOW + f, 8), :]
                for p in (f % 8 + 8, f % 8):
                    s = f - p
                    if 0 <= s < HALF:
                        total[s] = tap[p] * values if p == 0 else total[s] + tap[p] * values
                if f % 16 == 15 and f > 16:
                    pair = [total.pop(f - 31), total.pop(f - 23)]
                    self.frames[
                        pl.ds(pl.multiple_of(i * HALF, HALF) + f - 31, 16),
                        pl.ds(pl.multiple_of(block * LANES, LANES), LANES),
                    ] = (jnp.concatenate(pair, axis=0) * weight).astype(jnp.bfloat16)
            pair = [total.pop(HALF - 16), total.pop(HALF - 8)]
            self.frames[
                pl.ds(pl.multiple_of(i * HALF, HALF) + HALF - 16, 16),
                pl.ds(pl.multiple_of(block * LANES, LANES), LANES),
            ] = (jnp.concatenate(pair, axis=0) * weight).astype(jnp.bfloat16)
            assert not total
            if each is not None:
                each(run)

    def transform(self, group, inputs, stride):
        nx, ny, nz = self.dims
        per_group = nx * ny
        chips = [self.chip_of(group, jnp.int32(step)) for step in range(per_group)]
        rows = jnp.concatenate(
            [self.rows_table[(x * ny + y) * nz + z] for x, y, z in chips], axis=0
        )

        for first in range(*inputs, 2):
            values = self.frames[first * HALF : (first + 2) * HALF, :]
            spectra = lax.dot_general(
                rows, values, (((1,), (1,)), ((), ())), preferred_element_type=jnp.float32
            )
            for dest in range(2 * per_group):
                for j in range(2):
                    self.turned[
                        pl.ds(dest * 8 * stride + first - inputs[0] + j, 8, stride=stride), :
                    ] = spectra[dest * 8 : (dest + 1) * 8, j * HALF : (j + 1) * HALF]

    def pack(self, dest, target):
        for m in range(0, 8, 2):
            pair_rows = jnp.concatenate(
                [
                    self.turned[pl.ds((dest * 8 + m) * O_STRIDE, HERE), :],
                    self.turned[pl.ds((dest * 8 + m + 1) * O_STRIDE, HERE), :],
                ],
                axis=0,
            )
            target[m * 8 : (m + 2) * 8, :] = pair_rows.astype(jnp.bfloat16)

    def pack_part(self, dest, target, part):
        rows = self.turned[pl.ds(pl.multiple_of(dest * PART, PART), PART), :]
        target[part * PART : (part + 1) * PART, :] = rows.astype(jnp.bfloat16)

    def send(self, source, target, device, send_sem, recv_sem):
        pltpu.make_async_remote_copy(
            src_ref=source,
            dst_ref=target,
            send_sem=send_sem,
            recv_sem=recv_sem,
            device_id=device,
            device_id_type=MESH,
        ).start()

    def send_direct(self, group, step, change, rows, source, target, send_sem, recv_sem):
        core = self.my_core if change == 0 else 1 - self.my_core
        slot = (group * self.dims[0] * self.dims[1] + step) * 2 + core
        chip = self.chip_of(group, step)
        self.send(
            source.at[slot, rows],
            target.at[self.me, rows],
            self.device(chip, core),
            send_sem,
            recv_sem,
        )


def exchange_kernel(dims, samples, delays, flags, taps, table, out, raw, rim, ready, *rest):
    refs, sems = rest[:6], rest[6:]
    load_sem, table_sem, rim_send, rim_recv, send_sem, recv_sem, own_sem = sems
    work = Work(dims, delays, flags, refs)
    nx, ny, nz = dims
    per_group = nx * ny
    inp = nx * ny * nz
    devices = 2 * inp

    def load(first, count, sem):
        part = pl.ds(first * FRAME, count * FRAME)
        copy = pltpu.make_async_copy(samples.at[:, part], raw.at[:, part], sem)
        copy.start()
        return copy

    late_loads = [
        load(first, count, load_sem.at[piece]) for piece, (first, count) in enumerate(PIECES)
    ]
    fetch = pltpu.make_async_copy(table, work.rows_table, table_sem)
    fetch.start()
    early_load = load(0, SPLIT, load_sem.at[len(PIECES)])
    barrier = pltpu.get_barrier_semaphore()

    def greet(step):
        other = rem(work.me + step, devices)
        pl.semaphore_signal(
            barrier, inc=1, device_id=(div(other, inp), rem(other, inp)), device_id_type=MESH
        )

    @pl.loop(1, 1 + GREET_FIRST)
    def _(step):
        greet(step)

    work.place_taps(taps)

    def send_chip(half, group, step, part=None):
        rows = pl.ds(0, ROWS) if part is None else pl.ds(part * PART, PART)
        common = (rows, ready.at[half], out.at[half], send_sem.at[half], recv_sem.at[half])

        @pl.when(group + step > 0)
        def _():
            work.send_direct(group, step, 0, *common)

        @pl.when(group + step == 0)
        def _():
            pltpu.make_async_copy(
                ready.at[half, work.my_core, rows], out.at[half, work.me, rows], own_sem.at[half]
            ).start()

        work.send_direct(group, step, 1, *common)

    later = per_group - AT_ONCE

    def send_later(order, part):
        send_chip(1, div(order, later), AT_ONCE + rem(order, later), part)

    def transform_part(part):
        @pl.loop(0, nz)
        def _(group):
            work.transform(group, (part * 4, part * 4 + 4), 4)

            @pl.loop(0, 2 * per_group, step=8)
            def _(dests):
                for dest in range(8):
                    dest = dests + dest
                    work.pack_part(dest, ready.at[1, group * 2 * per_group + dest], part)

            @pl.loop(0, AT_ONCE)
            def _(step):
                send_chip(1, group, step, part)

    def transform_second():
        @pl.loop(0, nz)
        def _(group):
            work.transform(group, (0, HERE), O_STRIDE)

            @pl.loop(0, per_group, step=4)
            def _(chips):
                for dest in range(8):
                    dest = chips * 2 + dest
                    work.pack(dest, ready.at[0, group * 2 * per_group + dest])

    def in_first(run):
        send_later(run - 4 * BLOCKS, 0)

    def in_spread(step):
        @pl.when(rem(step, 3) == 0)
        def _():
            send_later(div(step, 3), 1)

    def in_filter(run):
        @pl.when(rem(run, 3) == 0)
        def _():
            send_later(9 + div(run, 3), 1)

    greeted = 1 + GREET_FIRST
    for piece, (first, count) in enumerate(PIECES):
        late_loads[piece].wait()
        whole = count // 4 * 4

        def in_late(step, begin=greeted):
            for k in range(GREET_STEP):
                greet(begin + step * GREET_STEP + k)

        greeting = greeted < devices
        work.spread(raw, FIRST, (first, first + whole), 4, in_late if greeting else None)
        if greeting:
            greeted += whole // 4 * GREET_STEP
        if whole < count:
            work.spread(raw, FIRST, (first + whole, first + count), 1)
    assert greeted == devices
    pl.semaphore_wait(barrier, devices - 1)
    rim_copy = pltpu.make_async_remote_copy(
        src_ref=samples.at[:, pl.ds(S_DEV * FRAME - HALO, HALO)],
        dst_ref=rim,
        send_sem=rim_send,
        recv_sem=rim_recv,
        device_id=(1 - work.tseg, work.here),
        device_id_type=MESH,
    )
    rim_copy.start()
    work.run_half(1, (0, 4))
    fetch.wait()
    transform_part(0)
    work.run_half(1, (4, HERE), in_first)
    transform_part(1)

    early_load.wait()
    work.spread(raw, FIRST, (0, SPLIT - 3), 4, in_spread)
    work.spread(raw, FIRST, (SPLIT - 3, SPLIT), 1)
    rim_copy.wait()

    @pl.when(work.tseg == 0)
    def _():
        rim[...] = jnp.zeros_like(rim)

    work.spread(rim, 1, (0, 20), 4)
    work.spread(rim, 1, (20, HALO // FRAME), 1)
    work.run_half(0, (0, HERE), in_filter)
    send_later(jnp.int32(31), 1)
    transform_second()

    @pl.loop(0, nz * per_group)
    def _(slot):
        send_chip(0, div(slot, per_group), rem(slot, per_group))

    for half in (1, 0):
        pltpu.make_async_copy(
            ready.at[half, work.my_core], out.at[half, work.me], own_sem.at[half]
        ).wait()
        sent = ready.at[half, pl.ds(0, devices - 1)]
        pltpu.make_async_copy(sent, sent, send_sem.at[half]).wait()
        arrived = out.at[half, pl.ds(0, devices - 1)]
        pltpu.make_async_copy(arrived, arrived, recv_sem.at[half]).wait()


def correlate_kernel(segments, scale, source, vis_real, vis_imag, loaded, sem):
    channel = pl.program_id(0)
    odd = lax.rem(channel, 2)
    tile = 2 * HERE

    def second(c):
        rows = pl.ds(pl.multiple_of(c * tile, tile), tile)
        return pltpu.make_async_copy(source.at[0, :, rows, :], loaded.at[0, c], sem.at[0, c])

    def first(pair, part):
        rows = pl.ds(pl.multiple_of(part * PART + pair * tile, tile), tile)
        place = pair * 2 + part
        return pltpu.make_async_copy(
            source.at[1, :, rows, :], loaded.at[1, place], sem.at[1, place]
        )

    @pl.when(channel == 0)
    def _():
        for pair in range(2):
            for part in range(2):
                first(pair, part).start()
            for c in range(2):
                second(pair * 2 + c).start()

    pair = lax.div(channel, 2)

    @pl.when(odd == 0)
    def _():
        for part in range(2):
            first(pair, part).wait()

    second(channel).wait()
    sources = loaded.shape[2] // segments
    inputs = sources * HERE
    upper = lax.broadcasted_iota(jnp.int32, (sources, HERE, HALF), 1) < HERE // 2
    real, imag = [], []

    def keep(to, values):
        to.append(values.reshape(inputs, HALF).astype(jnp.bfloat16))

    for segment in range(segments):
        here = pl.ds(segment * sources, sources)
        piece = loaded[0, channel, here].astype(jnp.float32)
        keep(real, piece[:, :HERE])
        keep(imag, piece[:, HERE:])
        parts = []
        for part in range(2):
            piece = loaded[1, pair * 2 + part, here].astype(jnp.float32)
            parts.append(jnp.where(odd == 1, piece[:, HERE:], piece[:, :HERE]))
        keep(real, jnp.where(upper, parts[0], pltpu.roll(parts[1], 4, 1)))
        keep(imag, jnp.where(upper, pltpu.roll(parts[0], 4, 1), parts[1]))
    real = jnp.concatenate(real, axis=1)
    imag = jnp.concatenate(imag, axis=1)

    def product(a, b):
        return lax.dot_general(a, b, (((1,), (1,)), ((), ())), preferred_element_type=jnp.float32)

    middle = inputs // 2
    low, high = slice(0, middle), slice(middle, inputs)
    for rows, columns in ((low, low), (high, high), (low, high)):
        block = product(real[rows], real[columns]) + product(imag[rows], imag[columns])
        vis_real[0, rows, columns] = block * scale
        if rows != columns:
            vis_real[0, columns, rows] = block.T * scale
    cross = product(real, imag)
    vis_imag[0] = (cross - cross.T) * scale


def per_device(samples, delays, flags, taps, *, segments, inp):
    nx, nz, ny_hi = SHAPES[inp]
    dims = (nx, 2 * ny_hi, nz)
    devices = segments * inp
    per_group = nx * 2 * ny_hi
    table = jnp.asarray(dft_rows(*dims))
    anywhere = pl.BlockSpec(memory_space=pl.ANY)
    in_specs = [
        anywhere,
        pl.BlockSpec(memory_space=pltpu.SMEM),
        pl.BlockSpec(memory_space=pltpu.SMEM),
        pl.BlockSpec(memory_space=pltpu.VMEM),
        anywhere,
    ]
    work_scratch = [
        pltpu.VMEM((nz * per_group, 16, FRAME), jnp.bfloat16),
        pltpu.VMEM((BLOCKS * HERE * RUN + 8, LANES), jnp.float32),
        pltpu.VMEM((BLOCKS * TAPS * 8, LANES), jnp.float32),
        pltpu.VMEM((HERE * BLOCKS * WINDOW, LANES), jnp.float32),
        pltpu.VMEM((HERE * HALF, FRAME), jnp.bfloat16),
        pltpu.VMEM((2 * per_group * 8 * O_STRIDE, LANES), jnp.float32),
    ]
    raw = pltpu.VMEM((HERE, S_DEV * FRAME), jnp.bfloat16)
    dma = pltpu.SemaphoreType.DMA
    spectra = pl.pallas_call(
        functools.partial(exchange_kernel, dims),
        out_shape=jax.ShapeDtypeStruct((2, devices, ROWS, HALF), jnp.bfloat16),
        in_specs=in_specs,
        out_specs=anywhere,
        scratch_shapes=[
            raw,
            pltpu.VMEM((HERE, HALO), jnp.bfloat16),
            pltpu.VMEM((2, devices, ROWS, HALF), jnp.bfloat16),
            *work_scratch,
            dma((len(PIECES) + 1,)),
            *[dma] * 3,
            *[dma((2,))] * 3,
        ],
        compiler_params=pltpu.CompilerParams(
            collective_id=0, has_side_effects=True, vmem_limit_bytes=60 * 2**20
        ),
        name="exchange",
    )(samples, delays, flags, taps, table)
    inputs = inp * HERE
    visibility = jax.ShapeDtypeStruct((CHAN, inputs, inputs), jnp.float32)
    return pl.pallas_call(
        functools.partial(correlate_kernel, segments, 1.0 / (S_DEV * segments)),
        out_shape=(visibility, visibility),
        grid=(CHAN,),
        in_specs=[anywhere],
        out_specs=(
            pl.BlockSpec((1, inputs, inputs), lambda c: (c, 0, 0)),
            pl.BlockSpec((1, inputs, inputs), lambda c: (c, 0, 0)),
        ),
        scratch_shapes=[
            pltpu.VMEM((2, CHAN, devices, 2 * HERE, HALF), jnp.bfloat16),
            dma((2, CHAN)),
        ],
        compiler_params=pltpu.CompilerParams(vmem_limit_bytes=60 * 2**20),
        name="correlate",
    )(spectra)


def solution(mesh):
    segments, inp = mesh.shape["tseg"], mesh.shape["inp"]
    return jax.shard_map(
        functools.partial(per_device, segments=segments, inp=inp),
        mesh=mesh,
        in_specs=(P("inp", "tseg"), P("inp"), P("inp"), P()),
        out_specs=(P(("tseg", "inp"), None, None), P(("tseg", "inp"), None, None)),
        check_vma=False,
    )
```

```python
import functools
import math

import jax
import jax.numpy as jnp
import ml_dtypes
import numpy as np
from jax import lax
from jax.experimental import pallas as pl
from jax.experimental.pallas import tpu as pltpu
from jax.sharding import PartitionSpec as P

MESH = pl.DeviceIdType.MESH
TAPS = 16
FRAME = 1024
HALO = 23552
LANES = 128
BLOCKS = FRAME // LANES
HERE = 8
S_DEV = 256
HALF = 128
CHAN = 4
ROWS = CHAN * 2 * HERE
FIRST = HALO // FRAME + 1
RUN = FIRST + S_DEV + 1
WINDOW = HALF + TAPS
SPLIT = 103
O_STRIDE = HERE + 1
PIECES = ((103, 40), (143, 40), (183, 40), (223, 33))
GREET_FIRST = 37
GREET_STEP = 3
PART = ROWS // 2
AT_ONCE = 8
SHAPES = {64: (4, 4, 2), 4: (2, 1, 1)}


def dft_rows(nx, ny, nz):
    count = nx * ny * nz * 2
    inp = count // 2
    k = np.arange(FRAME)[None, :]
    q = np.arange(count * CHAN)[:, None]
    phase = ((q * k) % FRAME).astype(np.float64) * (2.0 * math.pi / FRAME)
    parts = np.stack([np.cos(phase), -np.sin(phase)], axis=1) / math.sqrt(FRAME)
    parts = parts.astype(np.float32).astype(ml_dtypes.bfloat16)
    parts = parts.reshape(2, nx, nz, ny // 2, 2, CHAN * 2, FRAME)
    parts = parts.transpose(1, 3, 0, 2, 4, 5, 6)
    assert inp * 2 == count
    return parts.reshape(nx * ny * nz, 2 * CHAN * 2, FRAME)


def rem(a, b):
    return lax.rem(a, jnp.int32(b))


def div(a, b):
    return lax.div(a, jnp.int32(b))


class Work:
    def __init__(self, dims, delays, flags, refs):
        self.dims = dims
        self.delays, self.flags = delays, flags
        self.rows_table, self.runs, self.tap_rows, self.delayed, self.frames, self.turned = refs
        nx, ny, nz = dims
        self.inp = nx * nz * ny
        self.tseg = lax.axis_index("tseg")
        self.here = lax.axis_index("inp")
        self.me = self.tseg * self.inp + self.here
        self.my_core = rem(self.here, 2)
        self.my_y = rem(div(self.here, 2), ny // 2) * 2 + self.tseg
        self.my_z = rem(div(self.here, ny), nz)
        self.my_x = div(self.here, ny * nz)
        self.sign = 1 - 2 * self.my_core
        self.lane = lax.broadcasted_iota(jnp.int32, (HERE, LANES), 1)

    def chip_of(self, group, step):
        nx, ny, nz = self.dims
        dx = rem(step, nx)
        dy = div(step, nx)
        dz = group + 2 * nz - dx - dy
        return (
            rem(self.my_x + nx + self.sign * dx, nx),
            rem(self.my_y + ny + self.sign * dy, ny),
            rem(self.my_z + 4 * nz + self.sign * dz, nz),
        )

    def device(self, chip, core):
        nx, ny, nz = self.dims
        x, y, z = chip
        return rem(y, 2), ((x * nz + z) * (ny // 2) + div(y, 2)) * 2 + core

    def place_taps(self, taps):
        for block in range(BLOCKS):
            for p in range(TAPS):
                self.tap_rows[pl.ds((block * TAPS + p) * 8, 8), :] = jnp.broadcast_to(
                    taps[p : p + 1, block * LANES : (block + 1) * LANES], (8, LANES)
                )

    def spread(self, source, first, frame_range, unroll, each=None):
        row = lax.broadcasted_iota(jnp.int32, (HERE, LANES), 0)
        turn = jnp.zeros((HERE, LANES), jnp.int32)
        for i in range(HERE):
            turn = jnp.where(row == i, self.delays[i] % LANES, turn)
        index = (self.lane - turn + LANES) % LANES

        @pl.loop(*frame_range, step=unroll)
        def _(start):
            for frame in range(unroll):
                frame = start + frame
                values = source[:, pl.ds(pl.multiple_of(frame * FRAME, FRAME), FRAME)].astype(
                    jnp.float32
                )
                for block in range(BLOCKS):
                    moved = jnp.take_along_axis(
                        values[:, block * LANES : (block + 1) * LANES], index, axis=1
                    )
                    self.runs[pl.ds(block * HERE * RUN + first + frame, HERE, stride=RUN), :] = (
                        moved
                    )
            if each is not None:
                each(div(start - frame_range[0], unroll))

    def run_half(self, half, inputs, each=None):
        base = half * HALF - (TAPS - 1)

        @pl.loop(inputs[0] * BLOCKS, inputs[1] * BLOCKS)
        def _(run):
            i = div(run, BLOCKS)
            block = rem(run, BLOCKS)
            delay = self.delays[i]
            keep = self.lane >= delay % LANES
            weight = self.flags[i].astype(jnp.float32)

            def start(back):
                moved = block - delay // LANES - back + 9 * BLOCKS
                return (moved % BLOCKS * HERE + i) * RUN + moved // BLOCKS - 9 + FIRST + base

            now, before = start(0), start(1)
            for f in range(0, WINDOW, 8):
                self.delayed[pl.ds(pl.multiple_of(run * WINDOW, 8) + f, 8), :] = jnp.where(
                    keep, self.runs[pl.ds(now + f, 8), :], self.runs[pl.ds(before + f, 8), :]
                )
            tap = [self.tap_rows[pl.ds((block * TAPS + p) * 8, 8), :] for p in range(TAPS)]
            total = {}
            for f in range(HALF + 8):
                values = self.delayed[pl.ds(run * WINDOW + f, 8), :]
                for p in (f % 8 + 8, f % 8):
                    s = f - p
                    if 0 <= s < HALF:
                        total[s] = tap[p] * values if p == 0 else total[s] + tap[p] * values
                if f % 16 == 15 and f > 16:
                    pair = [total.pop(f - 31), total.pop(f - 23)]
                    self.frames[
                        pl.ds(pl.multiple_of(i * HALF, HALF) + f - 31, 16),
                        pl.ds(pl.multiple_of(block * LANES, LANES), LANES),
                    ] = (jnp.concatenate(pair, axis=0) * weight).astype(jnp.bfloat16)
            pair = [total.pop(HALF - 16), total.pop(HALF - 8)]
            self.frames[
                pl.ds(pl.multiple_of(i * HALF, HALF) + HALF - 16, 16),
                pl.ds(pl.multiple_of(block * LANES, LANES), LANES),
            ] = (jnp.concatenate(pair, axis=0) * weight).astype(jnp.bfloat16)
            assert not total
            if each is not None:
                each(run)

    def transform(self, group, inputs, stride):
        nx, ny, nz = self.dims
        per_group = nx * ny
        chips = [self.chip_of(group, jnp.int32(step)) for step in range(per_group)]
        rows = jnp.concatenate(
            [self.rows_table[(x * ny + y) * nz + z] for x, y, z in chips], axis=0
        )

        for first in range(*inputs, 2):
            values = self.frames[first * HALF : (first + 2) * HALF, :]
            spectra = lax.dot_general(
                rows, values, (((1,), (1,)), ((), ())), preferred_element_type=jnp.float32
            )
            for dest in range(2 * per_group):
                for j in range(2):
                    self.turned[
                        pl.ds(dest * 8 * stride + first - inputs[0] + j, 8, stride=stride), :
                    ] = spectra[dest * 8 : (dest + 1) * 8, j * HALF : (j + 1) * HALF]

    def pack(self, dest, target):
        for m in range(0, 8, 2):
            pair_rows = jnp.concatenate(
                [
                    self.turned[pl.ds((dest * 8 + m) * O_STRIDE, HERE), :],
                    self.turned[pl.ds((dest * 8 + m + 1) * O_STRIDE, HERE), :],
                ],
                axis=0,
            )
            target[m * 8 : (m + 2) * 8, :] = pair_rows.astype(jnp.bfloat16)

    def pack_part(self, dest, target, part):
        rows = self.turned[pl.ds(pl.multiple_of(dest * PART, PART), PART), :]
        target[part * PART : (part + 1) * PART, :] = rows.astype(jnp.bfloat16)

    def send(self, source, target, device, send_sem, recv_sem):
        pltpu.make_async_remote_copy(
            src_ref=source,
            dst_ref=target,
            send_sem=send_sem,
            recv_sem=recv_sem,
            device_id=device,
            device_id_type=MESH,
        ).start()

    def send_direct(self, group, step, change, rows, source, target, send_sem, recv_sem):
        core = self.my_core if change == 0 else 1 - self.my_core
        slot = (group * self.dims[0] * self.dims[1] + step) * 2 + core
        chip = self.chip_of(group, step)
        self.send(
            source.at[slot, rows],
            target.at[self.me, rows],
            self.device(chip, core),
            send_sem,
            recv_sem,
        )


def exchange_kernel(dims, samples, delays, flags, taps, table, out, raw, rim, ready, *rest):
    refs, sems = rest[:6], rest[6:]
    load_sem, table_sem, rim_send, rim_recv, send_sem, recv_sem, own_sem = sems
    work = Work(dims, delays, flags, refs)
    nx, ny, nz = dims
    per_group = nx * ny
    inp = nx * ny * nz
    devices = 2 * inp

    def load(first, count, sem):
        part = pl.ds(first * FRAME, count * FRAME)
        return pltpu.make_async_copy(samples.at[:, part], raw.at[:, part], sem)

    late_loads = [
        load(first, count, load_sem.at[piece]) for piece, (first, count) in enumerate(PIECES)
    ]
    for copy in late_loads:
        copy.start()
    fetch = pltpu.make_async_copy(table, work.rows_table, table_sem)
    early_load = load(0, SPLIT, load_sem.at[len(PIECES)])
    barrier = pltpu.get_barrier_semaphore()

    def greet(step):
        other = rem(work.me + step, devices)
        pl.semaphore_signal(
            barrier, inc=1, device_id=(div(other, inp), rem(other, inp)), device_id_type=MESH
        )

    @pl.loop(1, 1 + GREET_FIRST)
    def _(step):
        greet(step)

    work.place_taps(taps)

    def send_chip(half, group, step, part=None):
        rows = pl.ds(0, ROWS) if part is None else pl.ds(part * PART, PART)
        common = (rows, ready.at[half], out.at[half], send_sem.at[half], recv_sem.at[half])

        @pl.when(group + step > 0)
        def _():
            work.send_direct(group, step, 0, *common)

        @pl.when(group + step == 0)
        def _():
            pltpu.make_async_copy(
                ready.at[half, work.my_core, rows], out.at[half, work.me, rows], own_sem.at[half]
            ).start()

        work.send_direct(group, step, 1, *common)

    later = per_group - AT_ONCE

    def send_later(order, part):
        send_chip(1, div(order, later), AT_ONCE + rem(order, later), part)

    def transform_part(part):
        @pl.loop(0, nz)
        def _(group):
            work.transform(group, (part * 4, part * 4 + 4), 4)

            @pl.loop(0, 2 * per_group, step=8)
            def _(dests):
                for dest in range(8):
                    dest = dests + dest
                    work.pack_part(dest, ready.at[1, group * 2 * per_group + dest], part)

            @pl.loop(0, AT_ONCE)
            def _(step):
                send_chip(1, group, step, part)

    def transform_second():
        @pl.loop(0, nz)
        def _(group):
            work.transform(group, (0, HERE), O_STRIDE)

            @pl.loop(0, per_group, step=4)
            def _(chips):
                for dest in range(8):
                    dest = chips * 2 + dest
                    work.pack(dest, ready.at[0, group * 2 * per_group + dest])

    def in_first(run):
        send_later(run - 4 * BLOCKS, 0)

    def in_spread(step):
        @pl.when(rem(step, 3) == 0)
        def _():
            send_later(div(step, 3), 1)

    def in_filter(run):
        @pl.when(rem(run, 3) == 0)
        def _():
            send_later(9 + div(run, 3), 1)

    greeted = 1 + GREET_FIRST
    for piece, (first, count) in enumerate(PIECES):
        late_loads[piece].wait()
        if piece == 1:
            fetch.start()
            early_load.start()
        whole = count // 4 * 4

        def in_late(step, begin=greeted):
            for k in range(GREET_STEP):
                greet(begin + step * GREET_STEP + k)

        greeting = greeted < devices
        work.spread(raw, FIRST, (first, first + whole), 4, in_late if greeting else None)
        if greeting:
            greeted += whole // 4 * GREET_STEP
        if whole < count:
            work.spread(raw, FIRST, (first + whole, first + count), 1)
    assert greeted == devices
    pl.semaphore_wait(barrier, devices - 1)
    rim_copy = pltpu.make_async_remote_copy(
        src_ref=samples.at[:, pl.ds(S_DEV * FRAME - HALO, HALO)],
        dst_ref=rim,
        send_sem=rim_send,
        recv_sem=rim_recv,
        device_id=(1 - work.tseg, work.here),
        device_id_type=MESH,
    )
    rim_copy.start()
    work.run_half(1, (0, 4))
    fetch.wait()
    transform_part(0)
    work.run_half(1, (4, HERE), in_first)
    transform_part(1)

    early_load.wait()
    work.spread(raw, FIRST, (0, SPLIT - 3), 4, in_spread)
    work.spread(raw, FIRST, (SPLIT - 3, SPLIT), 1)
    rim_copy.wait()

    @pl.when(work.tseg == 0)
    def _():
        rim[...] = jnp.zeros_like(rim)

    work.spread(rim, 1, (0, 20), 4)
    work.spread(rim, 1, (20, HALO // FRAME), 1)
    work.run_half(0, (0, HERE), in_filter)
    send_later(jnp.int32(31), 1)
    transform_second()

    @pl.loop(0, nz * per_group)
    def _(slot):
        send_chip(0, div(slot, per_group), rem(slot, per_group))

    for half in (1, 0):
        pltpu.make_async_copy(
            ready.at[half, work.my_core], out.at[half, work.me], own_sem.at[half]
        ).wait()
        sent = ready.at[half, pl.ds(0, devices - 1)]
        pltpu.make_async_copy(sent, sent, send_sem.at[half]).wait()
        arrived = out.at[half, pl.ds(0, devices - 1)]
        pltpu.make_async_copy(arrived, arrived, recv_sem.at[half]).wait()


def correlate_kernel(segments, scale, source, vis_real, vis_imag, loaded, sem):
    channel = pl.program_id(0)
    odd = lax.rem(channel, 2)
    tile = 2 * HERE

    def second(c):
        rows = pl.ds(pl.multiple_of(c * tile, tile), tile)
        return pltpu.make_async_copy(source.at[0, :, rows, :], loaded.at[0, c], sem.at[0, c])

    def first(pair, part):
        rows = pl.ds(pl.multiple_of(part * PART + pair * tile, tile), tile)
        place = pair * 2 + part
        return pltpu.make_async_copy(
            source.at[1, :, rows, :], loaded.at[1, place], sem.at[1, place]
        )

    @pl.when(channel == 0)
    def _():
        for part in range(2):
            first(0, part).start()
        second(0).start()

    pair = lax.div(channel, 2)

    @pl.when(odd == 0)
    def _():
        for part in range(2):
            first(pair, part).wait()

    second(channel).wait()

    @pl.when(channel == 0)
    def _():
        second(1).start()
        for part in range(2):
            first(1, part).start()
        for c in range(2, CHAN):
            second(c).start()

    sources = loaded.shape[2] // segments
    inputs = sources * HERE
    upper = lax.broadcasted_iota(jnp.int32, (sources, HERE, HALF), 1) < HERE // 2
    real, imag = [], []

    def keep(to, values):
        to.append(values.reshape(inputs, HALF).astype(jnp.bfloat16))

    for segment in range(segments):
        here = pl.ds(segment * sources, sources)
        piece = loaded[0, channel, here].astype(jnp.float32)
        keep(real, piece[:, :HERE])
        keep(imag, piece[:, HERE:])
        parts = []
        for part in range(2):
            piece = loaded[1, pair * 2 + part, here].astype(jnp.float32)
            parts.append(jnp.where(odd == 1, piece[:, HERE:], piece[:, :HERE]))
        keep(real, jnp.where(upper, parts[0], pltpu.roll(parts[1], 4, 1)))
        keep(imag, jnp.where(upper, pltpu.roll(parts[0], 4, 1), parts[1]))
    real = jnp.concatenate(real, axis=1)
    imag = jnp.concatenate(imag, axis=1)

    def product(a, b):
        return lax.dot_general(a, b, (((1,), (1,)), ((), ())), preferred_element_type=jnp.float32)

    middle = inputs // 2
    low, high = slice(0, middle), slice(middle, inputs)
    for rows, columns in ((low, low), (high, high), (low, high)):
        block = product(real[rows], real[columns]) + product(imag[rows], imag[columns])
        vis_real[0, rows, columns] = block * scale
        if rows != columns:
            vis_real[0, columns, rows] = block.T * scale
    cross = product(real, imag)
    vis_imag[0] = (cross - cross.T) * scale


def per_device(samples, delays, flags, taps, *, segments, inp):
    nx, nz, ny_hi = SHAPES[inp]
    dims = (nx, 2 * ny_hi, nz)
    devices = segments * inp
    per_group = nx * 2 * ny_hi
    table = jnp.asarray(dft_rows(*dims))
    anywhere = pl.BlockSpec(memory_space=pl.ANY)
    in_specs = [
        anywhere,
        pl.BlockSpec(memory_space=pltpu.SMEM),
        pl.BlockSpec(memory_space=pltpu.SMEM),
        pl.BlockSpec(memory_space=pltpu.VMEM),
        anywhere,
    ]
    work_scratch = [
        pltpu.VMEM((nz * per_group, 16, FRAME), jnp.bfloat16),
        pltpu.VMEM((BLOCKS * HERE * RUN + 8, LANES), jnp.float32),
        pltpu.VMEM((BLOCKS * TAPS * 8, LANES), jnp.float32),
        pltpu.VMEM((HERE * BLOCKS * WINDOW, LANES), jnp.float32),
        pltpu.VMEM((HERE * HALF, FRAME), jnp.bfloat16),
        pltpu.VMEM((2 * per_group * 8 * O_STRIDE, LANES), jnp.float32),
    ]
    raw = pltpu.VMEM((HERE, S_DEV * FRAME), jnp.bfloat16)
    dma = pltpu.SemaphoreType.DMA
    spectra = pl.pallas_call(
        functools.partial(exchange_kernel, dims),
        out_shape=jax.ShapeDtypeStruct((2, devices, ROWS, HALF), jnp.bfloat16),
        in_specs=in_specs,
        out_specs=anywhere,
        scratch_shapes=[
            raw,
            pltpu.VMEM((HERE, HALO), jnp.bfloat16),
            pltpu.VMEM((2, devices, ROWS, HALF), jnp.bfloat16),
            *work_scratch,
            dma((len(PIECES) + 1,)),
            *[dma] * 3,
            *[dma((2,))] * 3,
        ],
        compiler_params=pltpu.CompilerParams(
            collective_id=0, has_side_effects=True, vmem_limit_bytes=60 * 2**20
        ),
        name="exchange",
    )(samples, delays, flags, taps, table)
    inputs = inp * HERE
    visibility = jax.ShapeDtypeStruct((CHAN, inputs, inputs), jnp.float32)
    return pl.pallas_call(
        functools.partial(correlate_kernel, segments, 1.0 / (S_DEV * segments)),
        out_shape=(visibility, visibility),
        grid=(CHAN,),
        in_specs=[anywhere],
        out_specs=(
            pl.BlockSpec((1, inputs, inputs), lambda c: (c, 0, 0)),
            pl.BlockSpec((1, inputs, inputs), lambda c: (c, 0, 0)),
        ),
        scratch_shapes=[
            pltpu.VMEM((2, CHAN, devices, 2 * HERE, HALF), jnp.bfloat16),
            dma((2, CHAN)),
        ],
        compiler_params=pltpu.CompilerParams(vmem_limit_bytes=60 * 2**20),
        name="correlate",
    )(spectra)


def solution(mesh):
    segments, inp = mesh.shape["tseg"], mesh.shape["inp"]
    return jax.shard_map(
        functools.partial(per_device, segments=segments, inp=inp),
        mesh=mesh,
        in_specs=(P("inp", "tseg"), P("inp"), P("inp"), P()),
        out_specs=(P(("tseg", "inp"), None, None), P(("tseg", "inp"), None, None)),
        check_vma=False,
    )
```

```python
import functools
import math

import jax
import jax.numpy as jnp
import ml_dtypes
import numpy as np
from jax import lax
from jax.experimental import pallas as pl
from jax.experimental.pallas import tpu as pltpu
from jax.sharding import PartitionSpec as P

MESH = pl.DeviceIdType.MESH
TAPS = 16
FRAME = 1024
HALO = 23552
LANES = 128
BLOCKS = FRAME // LANES
HERE = 8
S_DEV = 256
HALF = 128
CHAN = 4
ROWS = CHAN * 2 * HERE
FIRST = HALO // FRAME + 1
RUN = FIRST + S_DEV + 1
WINDOW = HALF + TAPS
SPLIT = 103
O_STRIDE = HERE + 1
PIECES = ((103, 40), (143, 40), (183, 40), (223, 33))
GREET_FIRST = 37
GREET_STEP = 3
PART = ROWS // 2
AT_ONCE = 8
SHAPES = {64: (4, 4, 2), 4: (2, 1, 1)}


def dft_rows(nx, ny, nz):
    count = nx * ny * nz * 2
    inp = count // 2
    k = np.arange(FRAME)[None, :]
    q = np.arange(count * CHAN)[:, None]
    phase = ((q * k) % FRAME).astype(np.float64) * (2.0 * math.pi / FRAME)
    parts = np.stack([np.cos(phase), -np.sin(phase)], axis=1) / math.sqrt(FRAME)
    parts = parts.astype(np.float32).astype(ml_dtypes.bfloat16)
    parts = parts.reshape(2, nx, nz, ny // 2, 2, CHAN * 2, FRAME)
    parts = parts.transpose(1, 3, 0, 2, 4, 5, 6)
    assert inp * 2 == count
    return parts.reshape(nx * ny * nz, 2 * CHAN * 2, FRAME)


def rem(a, b):
    return lax.rem(a, jnp.int32(b))


def div(a, b):
    return lax.div(a, jnp.int32(b))


class Work:
    def __init__(self, dims, delays, flags, refs):
        self.dims = dims
        self.delays, self.flags = delays, flags
        self.rows_table, self.runs, self.tap_rows, self.delayed, self.frames, self.turned = refs
        nx, ny, nz = dims
        self.inp = nx * nz * ny
        self.tseg = lax.axis_index("tseg")
        self.here = lax.axis_index("inp")
        self.me = self.tseg * self.inp + self.here
        self.my_core = rem(self.here, 2)
        self.my_y = rem(div(self.here, 2), ny // 2) * 2 + self.tseg
        self.my_z = rem(div(self.here, ny), nz)
        self.my_x = div(self.here, ny * nz)
        self.sign = 1 - 2 * self.my_core
        self.lane = lax.broadcasted_iota(jnp.int32, (HERE, LANES), 1)

    def chip_of(self, group, step):
        nx, ny, nz = self.dims
        dx = rem(step, nx)
        dy = div(step, nx)
        dz = group + 2 * nz - dx - dy
        return (
            rem(self.my_x + nx + self.sign * dx, nx),
            rem(self.my_y + ny + self.sign * dy, ny),
            rem(self.my_z + 4 * nz + self.sign * dz, nz),
        )

    def device(self, chip, core):
        nx, ny, nz = self.dims
        x, y, z = chip
        return rem(y, 2), ((x * nz + z) * (ny // 2) + div(y, 2)) * 2 + core

    def place_taps(self, taps):
        for block in range(BLOCKS):
            for p in range(TAPS):
                self.tap_rows[pl.ds((block * TAPS + p) * 8, 8), :] = jnp.broadcast_to(
                    taps[p : p + 1, block * LANES : (block + 1) * LANES], (8, LANES)
                )

    def spread(self, source, first, frame_range, unroll, each=None):
        row = lax.broadcasted_iota(jnp.int32, (HERE, LANES), 0)
        turn = jnp.zeros((HERE, LANES), jnp.int32)
        for i in range(HERE):
            turn = jnp.where(row == i, self.delays[i] % LANES, turn)
        index = (self.lane - turn + LANES) % LANES

        @pl.loop(*frame_range, step=unroll)
        def _(start):
            for frame in range(unroll):
                frame = start + frame
                values = source[:, pl.ds(pl.multiple_of(frame * FRAME, FRAME), FRAME)].astype(
                    jnp.float32
                )
                for block in range(BLOCKS):
                    moved = jnp.take_along_axis(
                        values[:, block * LANES : (block + 1) * LANES], index, axis=1
                    )
                    self.runs[pl.ds(block * HERE * RUN + first + frame, HERE, stride=RUN), :] = (
                        moved
                    )
            if each is not None:
                each(div(start - frame_range[0], unroll))

    def run_half(self, half, inputs, each=None):
        base = half * HALF - (TAPS - 1)

        @pl.loop(inputs[0] * BLOCKS, inputs[1] * BLOCKS)
        def _(run):
            i = div(run, BLOCKS)
            block = rem(run, BLOCKS)
            delay = self.delays[i]
            keep = self.lane >= delay % LANES
            weight = self.flags[i].astype(jnp.float32)

            def start(back):
                moved = block - delay // LANES - back + 9 * BLOCKS
                return (moved % BLOCKS * HERE + i) * RUN + moved // BLOCKS - 9 + FIRST + base

            now, before = start(0), start(1)
            for f in range(0, WINDOW, 8):
                self.delayed[pl.ds(pl.multiple_of(run * WINDOW, 8) + f, 8), :] = jnp.where(
                    keep, self.runs[pl.ds(now + f, 8), :], self.runs[pl.ds(before + f, 8), :]
                )
            tap = [self.tap_rows[pl.ds((block * TAPS + p) * 8, 8), :] for p in range(TAPS)]
            total = {}
            for f in range(HALF + 8):
                values = self.delayed[pl.ds(run * WINDOW + f, 8), :]
                for p in (f % 8 + 8, f % 8):
                    s = f - p
                    if 0 <= s < HALF:
                        total[s] = tap[p] * values if p == 0 else total[s] + tap[p] * values
                if f % 16 == 15 and f > 16:
                    pair = [total.pop(f - 31), total.pop(f - 23)]
                    self.frames[
                        pl.ds(pl.multiple_of(i * HALF, HALF) + f - 31, 16),
                        pl.ds(pl.multiple_of(block * LANES, LANES), LANES),
                    ] = (jnp.concatenate(pair, axis=0) * weight).astype(jnp.bfloat16)
            pair = [total.pop(HALF - 16), total.pop(HALF - 8)]
            self.frames[
                pl.ds(pl.multiple_of(i * HALF, HALF) + HALF - 16, 16),
                pl.ds(pl.multiple_of(block * LANES, LANES), LANES),
            ] = (jnp.concatenate(pair, axis=0) * weight).astype(jnp.bfloat16)
            assert not total
            if each is not None:
                each(run)

    def transform(self, group, inputs, stride):
        nx, ny, nz = self.dims
        per_group = nx * ny
        chips = [self.chip_of(group, jnp.int32(step)) for step in range(per_group)]
        rows = jnp.concatenate(
            [self.rows_table[(x * ny + y) * nz + z] for x, y, z in chips], axis=0
        )

        for first in range(*inputs, 2):
            values = self.frames[first * HALF : (first + 2) * HALF, :]
            spectra = lax.dot_general(
                rows, values, (((1,), (1,)), ((), ())), preferred_element_type=jnp.float32
            )
            for dest in range(2 * per_group):
                for j in range(2):
                    self.turned[
                        pl.ds(dest * 8 * stride + first - inputs[0] + j, 8, stride=stride), :
                    ] = spectra[dest * 8 : (dest + 1) * 8, j * HALF : (j + 1) * HALF]

    def pack(self, dest, target):
        for m in range(0, 8, 2):
            pair_rows = jnp.concatenate(
                [
                    self.turned[pl.ds((dest * 8 + m) * O_STRIDE, HERE), :],
                    self.turned[pl.ds((dest * 8 + m + 1) * O_STRIDE, HERE), :],
                ],
                axis=0,
            )
            target[m * 8 : (m + 2) * 8, :] = pair_rows.astype(jnp.bfloat16)

    def pack_part(self, dest, target, part):
        rows = self.turned[pl.ds(pl.multiple_of(dest * PART, PART), PART), :]
        target[part * PART : (part + 1) * PART, :] = rows.astype(jnp.bfloat16)

    def send(self, source, target, device, send_sem, recv_sem):
        pltpu.make_async_remote_copy(
            src_ref=source,
            dst_ref=target,
            send_sem=send_sem,
            recv_sem=recv_sem,
            device_id=device,
            device_id_type=MESH,
        ).start()

    def send_direct(self, group, step, change, rows, source, target, send_sem, recv_sem):
        core = self.my_core if change == 0 else 1 - self.my_core
        slot = (group * self.dims[0] * self.dims[1] + step) * 2 + core
        chip = self.chip_of(group, step)
        self.send(
            source.at[slot, rows],
            target.at[self.me, rows],
            self.device(chip, core),
            send_sem,
            recv_sem,
        )


def exchange_kernel(dims, samples, delays, flags, taps, table, out, raw, rim, ready, *rest):
    refs, sems = rest[:6], rest[6:]
    load_sem, table_sem, rim_send, rim_recv, send_sem, recv_sem, own_sem = sems
    work = Work(dims, delays, flags, refs)
    nx, ny, nz = dims
    per_group = nx * ny
    inp = nx * ny * nz
    devices = 2 * inp

    def load(first, count, sem):
        part = pl.ds(first * FRAME, count * FRAME)
        return pltpu.make_async_copy(samples.at[:, part], raw.at[:, part], sem)

    late_loads = [
        load(first, count, load_sem.at[piece]) for piece, (first, count) in enumerate(PIECES)
    ]
    for copy in late_loads:
        copy.start()
    fetch = pltpu.make_async_copy(table, work.rows_table, table_sem)
    early_load = load(0, SPLIT, load_sem.at[len(PIECES)])
    barrier = pltpu.get_barrier_semaphore()

    def greet(step):
        other = rem(work.me + step, devices)
        pl.semaphore_signal(
            barrier, inc=1, device_id=(div(other, inp), rem(other, inp)), device_id_type=MESH
        )

    @pl.loop(1, 1 + GREET_FIRST)
    def _(step):
        greet(step)

    work.place_taps(taps)

    def send_chip(half, group, step, part=None):
        rows = pl.ds(0, ROWS) if part is None else pl.ds(part * PART, PART)
        common = (rows, ready.at[half], out.at[half], send_sem.at[half], recv_sem.at[half])

        @pl.when(group + step > 0)
        def _():
            work.send_direct(group, step, 0, *common)

        @pl.when(group + step == 0)
        def _():
            pltpu.make_async_copy(
                ready.at[half, work.my_core, rows], out.at[half, work.me, rows], own_sem.at[half]
            ).start()

        work.send_direct(group, step, 1, *common)

    later = per_group - AT_ONCE

    def send_later(order, part):
        send_chip(1, div(order, later), AT_ONCE + rem(order, later), part)

    def transform_part(part):
        @pl.loop(0, nz)
        def _(group):
            work.transform(group, (part * 4, part * 4 + 4), 4)

            @pl.loop(0, 2 * per_group, step=8)
            def _(dests):
                for dest in range(8):
                    dest = dests + dest
                    work.pack_part(dest, ready.at[1, group * 2 * per_group + dest], part)

            @pl.loop(0, AT_ONCE)
            def _(step):
                send_chip(1, group, step, part)

    def transform_second():
        @pl.loop(0, nz)
        def _(group):
            work.transform(group, (0, HERE), O_STRIDE)

            @pl.loop(0, per_group, step=4)
            def _(chips):
                for dest in range(8):
                    dest = chips * 2 + dest
                    work.pack(dest, ready.at[0, group * 2 * per_group + dest])

    def in_first(run):
        send_later(run - 4 * BLOCKS, 0)

    def in_spread(step):
        @pl.when(rem(step, 3) == 0)
        def _():
            send_later(div(step, 3), 1)

    def in_filter(run):
        @pl.when(rem(run, 3) == 0)
        def _():
            send_later(9 + div(run, 3), 1)

    greeted = 1 + GREET_FIRST
    for piece, (first, count) in enumerate(PIECES):
        late_loads[piece].wait()
        if piece == 1:
            fetch.start()
            early_load.start()
        whole = count // 4 * 4

        def in_late(step, begin=greeted):
            for k in range(GREET_STEP):
                greet(begin + step * GREET_STEP + k)

        greeting = greeted < devices
        work.spread(raw, FIRST, (first, first + whole), 4, in_late if greeting else None)
        if greeting:
            greeted += whole // 4 * GREET_STEP
        if whole < count:
            work.spread(raw, FIRST, (first + whole, first + count), 1)
    assert greeted == devices
    pl.semaphore_wait(barrier, devices - 1)
    rim_copy = pltpu.make_async_remote_copy(
        src_ref=samples.at[:, pl.ds(S_DEV * FRAME - HALO, HALO)],
        dst_ref=rim,
        send_sem=rim_send,
        recv_sem=rim_recv,
        device_id=(1 - work.tseg, work.here),
        device_id_type=MESH,
    )
    rim_copy.start()
    work.run_half(1, (0, 4))
    fetch.wait()
    transform_part(0)
    work.run_half(1, (4, HERE), in_first)
    transform_part(1)

    early_load.wait()
    work.spread(raw, FIRST, (0, SPLIT - 3), 4, in_spread)
    work.spread(raw, FIRST, (SPLIT - 3, SPLIT), 1)
    rim_copy.wait()

    @pl.when(work.tseg == 0)
    def _():
        rim[...] = jnp.zeros_like(rim)

    work.spread(rim, 1, (0, 20), 4)
    work.spread(rim, 1, (20, HALO // FRAME), 1)
    work.run_half(0, (0, HERE), in_filter)
    send_later(jnp.int32(31), 1)
    transform_second()

    @pl.loop(0, nz * per_group)
    def _(slot):
        send_chip(0, div(slot, per_group), rem(slot, per_group))

    for half in (1, 0):
        pltpu.make_async_copy(
            ready.at[half, work.my_core], out.at[half, work.me], own_sem.at[half]
        ).wait()
        sent = ready.at[half, pl.ds(0, devices - 1)]
        pltpu.make_async_copy(sent, sent, send_sem.at[half]).wait()
        arrived = out.at[half, pl.ds(0, devices - 1)]
        pltpu.make_async_copy(arrived, arrived, recv_sem.at[half]).wait()


def correlate_kernel(segments, scale, source, vis_real, vis_imag, loaded, sem):
    channel = pl.program_id(0)
    odd = lax.rem(channel, 2)
    tile = 2 * HERE

    def second(c):
        rows = pl.ds(pl.multiple_of(c * tile, tile), tile)
        return pltpu.make_async_copy(source.at[0, :, rows, :], loaded.at[0, c], sem.at[0, c])

    def first(pair, part):
        rows = pl.ds(pl.multiple_of(part * PART + pair * tile, tile), tile)
        place = pair * 2 + part
        return pltpu.make_async_copy(
            source.at[1, :, rows, :], loaded.at[1, place], sem.at[1, place]
        )

    @pl.when(channel == 0)
    def _():
        for part in range(2):
            first(0, part).start()
        second(0).start()

    pair = lax.div(channel, 2)

    @pl.when(odd == 0)
    def _():
        for part in range(2):
            first(pair, part).wait()

    second(channel).wait()

    @pl.when(channel == 0)
    def _():
        second(1).start()
        for part in range(2):
            first(1, part).start()
        for c in range(2, CHAN):
            second(c).start()

    sources = loaded.shape[2] // segments
    inputs = sources * HERE
    upper = lax.broadcasted_iota(jnp.int32, (sources, HERE, HALF), 1) < HERE // 2
    real, imag = [], []

    def keep(to, values):
        to.append(values.reshape(inputs, HALF).astype(jnp.bfloat16))

    for segment in range(segments):
        here = pl.ds(segment * sources, sources)
        piece = loaded[0, channel, here].astype(jnp.float32)
        keep(real, piece[:, :HERE])
        keep(imag, piece[:, HERE:])
        parts = []
        for part in range(2):
            piece = loaded[1, pair * 2 + part, here].astype(jnp.float32)
            parts.append(jnp.where(odd == 1, piece[:, HERE:], piece[:, :HERE]))
        keep(real, jnp.where(upper, parts[0], pltpu.roll(parts[1], 4, 1)))
        keep(imag, jnp.where(upper, pltpu.roll(parts[0], 4, 1), parts[1]))
    real = jnp.concatenate(real, axis=1)
    imag = jnp.concatenate(imag, axis=1)

    def product(a, b):
        return lax.dot_general(a, b, (((1,), (1,)), ((), ())), preferred_element_type=jnp.float32)

    middle = inputs // 2
    low, high = slice(0, middle), slice(middle, inputs)
    for rows, columns in ((low, high), (low, low), (high, high)):
        real_rows, imag_rows = real[rows], imag[rows]
        real_columns, imag_columns = real[columns], imag[columns]
        block_real = product(real_rows, real_columns) + product(imag_rows, imag_columns)
        block_imag = product(real_rows, imag_columns) - product(imag_rows, real_columns)
        vis_real[0, rows, columns] = block_real * scale
        vis_imag[0, rows, columns] = block_imag * scale
        if rows != columns:
            vis_real[0, columns, rows] = block_real.T * scale
            vis_imag[0, columns, rows] = block_imag.T * -scale


def per_device(samples, delays, flags, taps, *, segments, inp):
    nx, nz, ny_hi = SHAPES[inp]
    dims = (nx, 2 * ny_hi, nz)
    devices = segments * inp
    per_group = nx * 2 * ny_hi
    table = jnp.asarray(dft_rows(*dims))
    anywhere = pl.BlockSpec(memory_space=pl.ANY)
    in_specs = [
        anywhere,
        pl.BlockSpec(memory_space=pltpu.SMEM),
        pl.BlockSpec(memory_space=pltpu.SMEM),
        pl.BlockSpec(memory_space=pltpu.VMEM),
        anywhere,
    ]
    work_scratch = [
        pltpu.VMEM((nz * per_group, 16, FRAME), jnp.bfloat16),
        pltpu.VMEM((BLOCKS * HERE * RUN + 8, LANES), jnp.float32),
        pltpu.VMEM((BLOCKS * TAPS * 8, LANES), jnp.float32),
        pltpu.VMEM((HERE * BLOCKS * WINDOW, LANES), jnp.float32),
        pltpu.VMEM((HERE * HALF, FRAME), jnp.bfloat16),
        pltpu.VMEM((2 * per_group * 8 * O_STRIDE, LANES), jnp.float32),
    ]
    raw = pltpu.VMEM((HERE, S_DEV * FRAME), jnp.bfloat16)
    dma = pltpu.SemaphoreType.DMA
    spectra = pl.pallas_call(
        functools.partial(exchange_kernel, dims),
        out_shape=jax.ShapeDtypeStruct((2, devices, ROWS, HALF), jnp.bfloat16),
        in_specs=in_specs,
        out_specs=anywhere,
        scratch_shapes=[
            raw,
            pltpu.VMEM((HERE, HALO), jnp.bfloat16),
            pltpu.VMEM((2, devices, ROWS, HALF), jnp.bfloat16),
            *work_scratch,
            dma((len(PIECES) + 1,)),
            *[dma] * 3,
            *[dma((2,))] * 3,
        ],
        compiler_params=pltpu.CompilerParams(
            collective_id=0, has_side_effects=True, vmem_limit_bytes=60 * 2**20
        ),
        name="exchange",
    )(samples, delays, flags, taps, table)
    inputs = inp * HERE
    visibility = jax.ShapeDtypeStruct((CHAN, inputs, inputs), jnp.float32)
    return pl.pallas_call(
        functools.partial(correlate_kernel, segments, 1.0 / (S_DEV * segments)),
        out_shape=(visibility, visibility),
        grid=(CHAN,),
        in_specs=[anywhere],
        out_specs=(
            pl.BlockSpec((1, inputs, inputs), lambda c: (c, 0, 0)),
            pl.BlockSpec((1, inputs, inputs), lambda c: (c, 0, 0)),
        ),
        scratch_shapes=[
            pltpu.VMEM((2, CHAN, devices, 2 * HERE, HALF), jnp.bfloat16),
            dma((2, CHAN)),
        ],
        compiler_params=pltpu.CompilerParams(vmem_limit_bytes=60 * 2**20),
        name="correlate",
    )(spectra)


def solution(mesh):
    segments, inp = mesh.shape["tseg"], mesh.shape["inp"]
    return jax.shard_map(
        functools.partial(per_device, segments=segments, inp=inp),
        mesh=mesh,
        in_specs=(P("inp", "tseg"), P("inp"), P("inp"), P()),
        out_specs=(P(("tseg", "inp"), None, None), P(("tseg", "inp"), None, None)),
        check_vma=False,
    )
```

```python
import functools
import math

import jax
import jax.numpy as jnp
import ml_dtypes
import numpy as np
from jax import lax
from jax.experimental import pallas as pl
from jax.experimental.pallas import tpu as pltpu
from jax.sharding import PartitionSpec as P

MESH = pl.DeviceIdType.MESH
TAPS = 16
FRAME = 1024
HALO = 23552
LANES = 128
BLOCKS = FRAME // LANES
HERE = 8
S_DEV = 256
HALF = 128
CHAN = 4
ROWS = CHAN * 2 * HERE
FIRST = HALO // FRAME + 1
RUN = FIRST + S_DEV + 1
WINDOW = HALF + TAPS
SPLIT = 103
O_STRIDE = HERE + 1
PIECES = ((103, 40), (143, 40), (183, 40), (223, 33))
GREET_FIRST = 37
GREET_STEP = 3
PART = ROWS // 2
AT_ONCE = 8
SHAPES = {64: (4, 4, 2), 4: (2, 1, 1)}


def dft_rows(nx, ny, nz):
    count = nx * ny * nz * 2
    inp = count // 2
    k = np.arange(FRAME)[None, :]
    q = np.arange(count * CHAN)[:, None]
    phase = ((q * k) % FRAME).astype(np.float64) * (2.0 * math.pi / FRAME)
    parts = np.stack([np.cos(phase), -np.sin(phase)], axis=1) / math.sqrt(FRAME)
    parts = parts.astype(np.float32).astype(ml_dtypes.bfloat16)
    parts = parts.reshape(2, nx, nz, ny // 2, 2, CHAN * 2, FRAME)
    parts = parts.transpose(1, 3, 0, 2, 4, 5, 6)
    assert inp * 2 == count
    return parts.reshape(nx * ny * nz, 2 * CHAN * 2, FRAME)


def rem(a, b):
    return lax.rem(a, jnp.int32(b))


def div(a, b):
    return lax.div(a, jnp.int32(b))


class Work:
    def __init__(self, dims, delays, flags, refs):
        self.dims = dims
        self.delays, self.flags = delays, flags
        self.rows_table, self.runs, self.tap_rows, self.delayed, self.frames, self.turned = refs
        nx, ny, nz = dims
        self.inp = nx * nz * ny
        self.tseg = lax.axis_index("tseg")
        self.here = lax.axis_index("inp")
        self.me = self.tseg * self.inp + self.here
        self.my_core = rem(self.here, 2)
        self.my_y = rem(div(self.here, 2), ny // 2) * 2 + self.tseg
        self.my_z = rem(div(self.here, ny), nz)
        self.my_x = div(self.here, ny * nz)
        self.sign = 1 - 2 * self.my_core
        self.lane = lax.broadcasted_iota(jnp.int32, (HERE, LANES), 1)

    def chip_of(self, group, step):
        nx, ny, nz = self.dims
        dx = rem(step, nx)
        dy = div(step, nx)
        dz = group
        return (
            rem(self.my_x + nx + self.sign * dx, nx),
            rem(self.my_y + ny + self.sign * dy, ny),
            rem(self.my_z + 4 * nz + self.sign * dz, nz),
        )

    def device(self, chip, core):
        nx, ny, nz = self.dims
        x, y, z = chip
        return rem(y, 2), ((x * nz + z) * (ny // 2) + div(y, 2)) * 2 + core

    def place_taps(self, taps):
        for block in range(BLOCKS):
            for p in range(TAPS):
                self.tap_rows[pl.ds((block * TAPS + p) * 8, 8), :] = jnp.broadcast_to(
                    taps[p : p + 1, block * LANES : (block + 1) * LANES], (8, LANES)
                )

    def spread(self, source, first, frame_range, unroll, each=None):
        row = lax.broadcasted_iota(jnp.int32, (HERE, LANES), 0)
        turn = jnp.zeros((HERE, LANES), jnp.int32)
        for i in range(HERE):
            turn = jnp.where(row == i, self.delays[i] % LANES, turn)
        index = (self.lane - turn + LANES) % LANES

        @pl.loop(*frame_range, step=unroll)
        def _(start):
            for frame in range(unroll):
                frame = start + frame
                values = source[:, pl.ds(pl.multiple_of(frame * FRAME, FRAME), FRAME)].astype(
                    jnp.float32
                )
                for block in range(BLOCKS):
                    moved = jnp.take_along_axis(
                        values[:, block * LANES : (block + 1) * LANES], index, axis=1
                    )
                    self.runs[pl.ds(block * HERE * RUN + first + frame, HERE, stride=RUN), :] = (
                        moved
                    )
            if each is not None:
                each(div(start - frame_range[0], unroll))

    def run_half(self, half, inputs, each=None):
        base = half * HALF - (TAPS - 1)

        @pl.loop(inputs[0] * BLOCKS, inputs[1] * BLOCKS)
        def _(run):
            i = div(run, BLOCKS)
            block = rem(run, BLOCKS)
            delay = self.delays[i]
            keep = self.lane >= delay % LANES
            weight = self.flags[i].astype(jnp.float32)

            def start(back):
                moved = block - delay // LANES - back + 9 * BLOCKS
                return (moved % BLOCKS * HERE + i) * RUN + moved // BLOCKS - 9 + FIRST + base

            now, before = start(0), start(1)
            for f in range(0, WINDOW, 8):
                self.delayed[pl.ds(pl.multiple_of(run * WINDOW, 8) + f, 8), :] = jnp.where(
                    keep, self.runs[pl.ds(now + f, 8), :], self.runs[pl.ds(before + f, 8), :]
                )
            tap = [self.tap_rows[pl.ds((block * TAPS + p) * 8, 8), :] for p in range(TAPS)]
            total = {}
            for f in range(HALF + 8):
                values = self.delayed[pl.ds(run * WINDOW + f, 8), :]
                for p in (f % 8 + 8, f % 8):
                    s = f - p
                    if 0 <= s < HALF:
                        total[s] = tap[p] * values if p == 0 else total[s] + tap[p] * values
                if f % 16 == 15 and f > 16:
                    pair = [total.pop(f - 31), total.pop(f - 23)]
                    self.frames[
                        pl.ds(pl.multiple_of(i * HALF, HALF) + f - 31, 16),
                        pl.ds(pl.multiple_of(block * LANES, LANES), LANES),
                    ] = (jnp.concatenate(pair, axis=0) * weight).astype(jnp.bfloat16)
            pair = [total.pop(HALF - 16), total.pop(HALF - 8)]
            self.frames[
                pl.ds(pl.multiple_of(i * HALF, HALF) + HALF - 16, 16),
                pl.ds(pl.multiple_of(block * LANES, LANES), LANES),
            ] = (jnp.concatenate(pair, axis=0) * weight).astype(jnp.bfloat16)
            assert not total
            if each is not None:
                each(run)

    def transform(self, group, inputs, stride):
        nx, ny, nz = self.dims
        per_group = nx * ny
        chips = [self.chip_of(group, jnp.int32(step)) for step in range(per_group)]
        rows = jnp.concatenate(
            [self.rows_table[(x * ny + y) * nz + z] for x, y, z in chips], axis=0
        )

        for first in range(*inputs, 2):
            values = self.frames[first * HALF : (first + 2) * HALF, :]
            spectra = lax.dot_general(
                rows, values, (((1,), (1,)), ((), ())), preferred_element_type=jnp.float32
            )
            for dest in range(2 * per_group):
                for j in range(2):
                    self.turned[
                        pl.ds(dest * 8 * stride + first - inputs[0] + j, 8, stride=stride), :
                    ] = spectra[dest * 8 : (dest + 1) * 8, j * HALF : (j + 1) * HALF]

    def pack(self, dest, target):
        for m in range(0, 8, 2):
            pair_rows = jnp.concatenate(
                [
                    self.turned[pl.ds((dest * 8 + m) * O_STRIDE, HERE), :],
                    self.turned[pl.ds((dest * 8 + m + 1) * O_STRIDE, HERE), :],
                ],
                axis=0,
            )
            target[m * 8 : (m + 2) * 8, :] = pair_rows.astype(jnp.bfloat16)

    def pack_part(self, dest, target, part):
        rows = self.turned[pl.ds(pl.multiple_of(dest * PART, PART), PART), :]
        target[part * PART : (part + 1) * PART, :] = rows.astype(jnp.bfloat16)

    def send(self, source, target, device, send_sem, recv_sem):
        pltpu.make_async_remote_copy(
            src_ref=source,
            dst_ref=target,
            send_sem=send_sem,
            recv_sem=recv_sem,
            device_id=device,
            device_id_type=MESH,
        ).start()

    def send_direct(self, group, step, change, rows, source, target, send_sem, recv_sem):
        core = self.my_core if change == 0 else 1 - self.my_core
        slot = (group * self.dims[0] * self.dims[1] + step) * 2 + core
        chip = self.chip_of(group, step)
        self.send(
            source.at[slot, rows],
            target.at[self.me, rows],
            self.device(chip, core),
            send_sem,
            recv_sem,
        )


def exchange_kernel(dims, samples, delays, flags, taps, table, out, raw, rim, ready, *rest):
    refs, sems = rest[:6], rest[6:]
    load_sem, table_sem, rim_send, rim_recv, send_sem, recv_sem, own_sem = sems
    work = Work(dims, delays, flags, refs)
    nx, ny, nz = dims
    per_group = nx * ny
    inp = nx * ny * nz
    devices = 2 * inp

    def load(first, count, sem):
        part = pl.ds(first * FRAME, count * FRAME)
        return pltpu.make_async_copy(samples.at[:, part], raw.at[:, part], sem)

    late_loads = [
        load(first, count, load_sem.at[piece]) for piece, (first, count) in enumerate(PIECES)
    ]
    for copy in late_loads:
        copy.start()
    fetch = pltpu.make_async_copy(table, work.rows_table, table_sem)
    early_load = load(0, SPLIT, load_sem.at[len(PIECES)])
    barrier = pltpu.get_barrier_semaphore()

    def greet(step):
        other = rem(work.me + step, devices)
        pl.semaphore_signal(
            barrier, inc=1, device_id=(div(other, inp), rem(other, inp)), device_id_type=MESH
        )

    @pl.loop(1, 1 + GREET_FIRST)
    def _(step):
        greet(step)

    work.place_taps(taps)

    def send_chip(half, group, step, part=None):
        rows = pl.ds(0, ROWS) if part is None else pl.ds(part * PART, PART)
        common = (rows, ready.at[half], out.at[half], send_sem.at[half], recv_sem.at[half])

        @pl.when(group + step > 0)
        def _():
            work.send_direct(group, step, 0, *common)

        @pl.when(group + step == 0)
        def _():
            pltpu.make_async_copy(
                ready.at[half, work.my_core, rows], out.at[half, work.me, rows], own_sem.at[half]
            ).start()

        work.send_direct(group, step, 1, *common)

    later = per_group - AT_ONCE

    def send_later(order, part):
        send_chip(1, div(order, later), AT_ONCE + rem(order, later), part)

    def transform_part(part):
        @pl.loop(0, nz)
        def _(group):
            work.transform(group, (part * 4, part * 4 + 4), 4)

            @pl.loop(0, 2 * per_group, step=8)
            def _(dests):
                for dest in range(8):
                    dest = dests + dest
                    work.pack_part(dest, ready.at[1, group * 2 * per_group + dest], part)

            @pl.loop(0, AT_ONCE)
            def _(step):
                send_chip(1, group, step, part)

    def transform_second():
        @pl.loop(0, nz)
        def _(group):
            work.transform(group, (0, HERE), O_STRIDE)

            @pl.loop(0, per_group, step=4)
            def _(chips):
                for dest in range(8):
                    dest = chips * 2 + dest
                    work.pack(dest, ready.at[0, group * 2 * per_group + dest])

    def in_first(run):
        send_later(run - 4 * BLOCKS, 0)

    def in_spread(step):
        @pl.when(rem(step, 3) == 0)
        def _():
            send_later(div(step, 3), 1)

    def in_filter(run):
        @pl.when(rem(run, 3) == 0)
        def _():
            send_later(9 + div(run, 3), 1)

    greeted = 1 + GREET_FIRST
    for piece, (first, count) in enumerate(PIECES):
        late_loads[piece].wait()
        if piece == 1:
            fetch.start()
            early_load.start()
        whole = count // 4 * 4

        def in_late(step, begin=greeted):
            for k in range(GREET_STEP):
                greet(begin + step * GREET_STEP + k)

        greeting = greeted < devices
        work.spread(raw, FIRST, (first, first + whole), 4, in_late if greeting else None)
        if greeting:
            greeted += whole // 4 * GREET_STEP
        if whole < count:
            work.spread(raw, FIRST, (first + whole, first + count), 1)
    assert greeted == devices
    pl.semaphore_wait(barrier, devices - 1)
    rim_copy = pltpu.make_async_remote_copy(
        src_ref=samples.at[:, pl.ds(S_DEV * FRAME - HALO, HALO)],
        dst_ref=rim,
        send_sem=rim_send,
        recv_sem=rim_recv,
        device_id=(1 - work.tseg, work.here),
        device_id_type=MESH,
    )
    rim_copy.start()
    work.run_half(1, (0, 4))
    fetch.wait()
    transform_part(0)
    work.run_half(1, (4, HERE), in_first)
    transform_part(1)

    early_load.wait()
    work.spread(raw, FIRST, (0, SPLIT - 3), 4, in_spread)
    work.spread(raw, FIRST, (SPLIT - 3, SPLIT), 1)
    rim_copy.wait()

    @pl.when(work.tseg == 0)
    def _():
        rim[...] = jnp.zeros_like(rim)

    work.spread(rim, 1, (0, 20), 4)
    work.spread(rim, 1, (20, HALO // FRAME), 1)
    work.run_half(0, (0, HERE), in_filter)
    send_later(jnp.int32(31), 1)
    transform_second()

    @pl.loop(0, nz * per_group)
    def _(slot):
        send_chip(0, div(slot, per_group), rem(slot, per_group))

    for half in (1, 0):
        pltpu.make_async_copy(
            ready.at[half, work.my_core], out.at[half, work.me], own_sem.at[half]
        ).wait()
        sent = ready.at[half, pl.ds(0, devices - 1)]
        pltpu.make_async_copy(sent, sent, send_sem.at[half]).wait()
        arrived = out.at[half, pl.ds(0, devices - 1)]
        pltpu.make_async_copy(arrived, arrived, recv_sem.at[half]).wait()


def correlate_kernel(segments, scale, source, vis_real, vis_imag, loaded, sem):
    channel = pl.program_id(0)
    odd = lax.rem(channel, 2)
    tile = 2 * HERE

    def second(c):
        rows = pl.ds(pl.multiple_of(c * tile, tile), tile)
        return pltpu.make_async_copy(source.at[0, :, rows, :], loaded.at[0, c], sem.at[0, c])

    def first(pair, part):
        rows = pl.ds(pl.multiple_of(part * PART + pair * tile, tile), tile)
        place = pair * 2 + part
        return pltpu.make_async_copy(
            source.at[1, :, rows, :], loaded.at[1, place], sem.at[1, place]
        )

    @pl.when(channel == 0)
    def _():
        for part in range(2):
            first(0, part).start()
        second(0).start()

    pair = lax.div(channel, 2)

    @pl.when(odd == 0)
    def _():
        for part in range(2):
            first(pair, part).wait()

    second(channel).wait()

    @pl.when(channel == 0)
    def _():
        second(1).start()
        for part in range(2):
            first(1, part).start()
        for c in range(2, CHAN):
            second(c).start()

    sources = loaded.shape[2] // segments
    inputs = sources * HERE
    upper = lax.broadcasted_iota(jnp.int32, (sources, HERE, HALF), 1) < HERE // 2
    real, imag = [], []

    def keep(to, values):
        to.append(values.reshape(inputs, HALF).astype(jnp.bfloat16))

    for segment in range(segments):
        here = pl.ds(segment * sources, sources)
        piece = loaded[0, channel, here].astype(jnp.float32)
        keep(real, piece[:, :HERE])
        keep(imag, piece[:, HERE:])
        parts = []
        for part in range(2):
            piece = loaded[1, pair * 2 + part, here].astype(jnp.float32)
            parts.append(jnp.where(odd == 1, piece[:, HERE:], piece[:, :HERE]))
        keep(real, jnp.where(upper, parts[0], pltpu.roll(parts[1], 4, 1)))
        keep(imag, jnp.where(upper, pltpu.roll(parts[0], 4, 1), parts[1]))
    real = jnp.concatenate(real, axis=1)
    imag = jnp.concatenate(imag, axis=1)

    def product(a, b):
        return lax.dot_general(a, b, (((1,), (1,)), ((), ())), preferred_element_type=jnp.float32)

    middle = inputs // 2
    low, high = slice(0, middle), slice(middle, inputs)
    for rows, columns in ((low, low), (high, high), (low, high)):
        block = product(real[rows], real[columns]) + product(imag[rows], imag[columns])
        vis_real[0, rows, columns] = block * scale
        if rows != columns:
            vis_real[0, columns, rows] = block.T * scale
    cross = product(real, imag)
    vis_imag[0] = (cross - cross.T) * scale


def per_device(samples, delays, flags, taps, *, segments, inp):
    nx, nz, ny_hi = SHAPES[inp]
    dims = (nx, 2 * ny_hi, nz)
    devices = segments * inp
    per_group = nx * 2 * ny_hi
    table = jnp.asarray(dft_rows(*dims))
    anywhere = pl.BlockSpec(memory_space=pl.ANY)
    in_specs = [
        anywhere,
        pl.BlockSpec(memory_space=pltpu.SMEM),
        pl.BlockSpec(memory_space=pltpu.SMEM),
        pl.BlockSpec(memory_space=pltpu.VMEM),
        anywhere,
    ]
    work_scratch = [
        pltpu.VMEM((nz * per_group, 16, FRAME), jnp.bfloat16),
        pltpu.VMEM((BLOCKS * HERE * RUN + 8, LANES), jnp.float32),
        pltpu.VMEM((BLOCKS * TAPS * 8, LANES), jnp.float32),
        pltpu.VMEM((HERE * BLOCKS * WINDOW, LANES), jnp.float32),
        pltpu.VMEM((HERE * HALF, FRAME), jnp.bfloat16),
        pltpu.VMEM((2 * per_group * 8 * O_STRIDE, LANES), jnp.float32),
    ]
    raw = pltpu.VMEM((HERE, S_DEV * FRAME), jnp.bfloat16)
    dma = pltpu.SemaphoreType.DMA
    spectra = pl.pallas_call(
        functools.partial(exchange_kernel, dims),
        out_shape=jax.ShapeDtypeStruct((2, devices, ROWS, HALF), jnp.bfloat16),
        in_specs=in_specs,
        out_specs=anywhere,
        scratch_shapes=[
            raw,
            pltpu.VMEM((HERE, HALO), jnp.bfloat16),
            pltpu.VMEM((2, devices, ROWS, HALF), jnp.bfloat16),
            *work_scratch,
            dma((len(PIECES) + 1,)),
            *[dma] * 3,
            *[dma((2,))] * 3,
        ],
        compiler_params=pltpu.CompilerParams(
            collective_id=0, has_side_effects=True, vmem_limit_bytes=60 * 2**20
        ),
        name="exchange",
    )(samples, delays, flags, taps, table)
    inputs = inp * HERE
    visibility = jax.ShapeDtypeStruct((CHAN, inputs, inputs), jnp.float32)
    return pl.pallas_call(
        functools.partial(correlate_kernel, segments, 1.0 / (S_DEV * segments)),
        out_shape=(visibility, visibility),
        grid=(CHAN,),
        in_specs=[anywhere],
        out_specs=(
            pl.BlockSpec((1, inputs, inputs), lambda c: (c, 0, 0)),
            pl.BlockSpec((1, inputs, inputs), lambda c: (c, 0, 0)),
        ),
        scratch_shapes=[
            pltpu.VMEM((2, CHAN, devices, 2 * HERE, HALF), jnp.bfloat16),
            dma((2, CHAN)),
        ],
        compiler_params=pltpu.CompilerParams(vmem_limit_bytes=60 * 2**20),
        name="correlate",
    )(spectra)


def solution(mesh):
    segments, inp = mesh.shape["tseg"], mesh.shape["inp"]
    return jax.shard_map(
        functools.partial(per_device, segments=segments, inp=inp),
        mesh=mesh,
        in_specs=(P("inp", "tseg"), P("inp"), P("inp"), P()),
        out_specs=(P(("tseg", "inp"), None, None), P(("tseg", "inp"), None, None)),
        check_vma=False,
    )
```

```python
import functools
import math

import jax
import jax.numpy as jnp
import ml_dtypes
import numpy as np
from jax import lax
from jax.experimental import pallas as pl
from jax.experimental.pallas import tpu as pltpu
from jax.sharding import PartitionSpec as P

MESH = pl.DeviceIdType.MESH
TAPS = 16
FRAME = 1024
HALO = 23552
LANES = 128
BLOCKS = FRAME // LANES
HERE = 8
S_DEV = 256
HALF = 128
CHAN = 4
ROWS = CHAN * 2 * HERE
FIRST = HALO // FRAME + 1
RUN = FIRST + S_DEV + 1
WINDOW = HALF + TAPS
SPLIT = 103
O_STRIDE = HERE + 1
PIECES = ((103, 40), (143, 40), (183, 40), (223, 33))
GREET_FIRST = 37
GREET_STEP = 3
PART = ROWS // 2
AT_ONCE = 8
SHAPES = {64: (4, 4, 2), 4: (2, 1, 1)}


def dft_rows(nx, ny, nz):
    count = nx * ny * nz * 2
    inp = count // 2
    k = np.arange(FRAME)[None, :]
    q = np.arange(count * CHAN)[:, None]
    phase = ((q * k) % FRAME).astype(np.float64) * (2.0 * math.pi / FRAME)
    parts = np.stack([np.cos(phase), -np.sin(phase)], axis=1) / math.sqrt(FRAME)
    parts = parts.astype(np.float32).astype(ml_dtypes.bfloat16)
    parts = parts.reshape(2, nx, nz, ny // 2, 2, CHAN * 2, FRAME)
    parts = parts.transpose(1, 3, 0, 2, 4, 5, 6)
    assert inp * 2 == count
    return parts.reshape(nx * ny * nz, 2 * CHAN * 2, FRAME)


def rem(a, b):
    return lax.rem(a, jnp.int32(b))


def div(a, b):
    return lax.div(a, jnp.int32(b))


class Work:
    def __init__(self, dims, delays, flags, refs):
        self.dims = dims
        self.delays, self.flags = delays, flags
        self.rows_table, self.runs, self.tap_rows, self.delayed, self.frames, self.turned = refs
        nx, ny, nz = dims
        self.inp = nx * nz * ny
        self.tseg = lax.axis_index("tseg")
        self.here = lax.axis_index("inp")
        self.me = self.tseg * self.inp + self.here
        self.my_core = rem(self.here, 2)
        self.my_y = rem(div(self.here, 2), ny // 2) * 2 + self.tseg
        self.my_z = rem(div(self.here, ny), nz)
        self.my_x = div(self.here, ny * nz)
        self.sign = 1 - 2 * self.my_core
        self.lane = lax.broadcasted_iota(jnp.int32, (HERE, LANES), 1)

    def chip_of(self, group, step):
        nx, ny, nz = self.dims
        dx = rem(step, nx)
        dy = rem(dx + div(step, nx), ny)
        dz = group + 2 * nz - dx
        return (
            rem(self.my_x + nx + self.sign * dx, nx),
            rem(self.my_y + ny + self.sign * dy, ny),
            rem(self.my_z + 4 * nz + self.sign * dz, nz),
        )

    def device(self, chip, core):
        nx, ny, nz = self.dims
        x, y, z = chip
        return rem(y, 2), ((x * nz + z) * (ny // 2) + div(y, 2)) * 2 + core

    def place_taps(self, taps):
        for block in range(BLOCKS):
            for p in range(TAPS):
                self.tap_rows[pl.ds((block * TAPS + p) * 8, 8), :] = jnp.broadcast_to(
                    taps[p : p + 1, block * LANES : (block + 1) * LANES], (8, LANES)
                )

    def spread(self, source, first, frame_range, unroll, each=None):
        row = lax.broadcasted_iota(jnp.int32, (HERE, LANES), 0)
        turn = jnp.zeros((HERE, LANES), jnp.int32)
        for i in range(HERE):
            turn = jnp.where(row == i, self.delays[i] % LANES, turn)
        index = (self.lane - turn + LANES) % LANES

        @pl.loop(*frame_range, step=unroll)
        def _(start):
            for frame in range(unroll):
                frame = start + frame
                values = source[:, pl.ds(pl.multiple_of(frame * FRAME, FRAME), FRAME)].astype(
                    jnp.float32
                )
                for block in range(BLOCKS):
                    moved = jnp.take_along_axis(
                        values[:, block * LANES : (block + 1) * LANES], index, axis=1
                    )
                    self.runs[pl.ds(block * HERE * RUN + first + frame, HERE, stride=RUN), :] = (
                        moved
                    )
            if each is not None:
                each(div(start - frame_range[0], unroll))

    def run_half(self, half, inputs, each=None):
        base = half * HALF - (TAPS - 1)

        @pl.loop(inputs[0] * BLOCKS, inputs[1] * BLOCKS)
        def _(run):
            i = div(run, BLOCKS)
            block = rem(run, BLOCKS)
            delay = self.delays[i]
            keep = self.lane >= delay % LANES
            weight = self.flags[i].astype(jnp.float32)

            def start(back):
                moved = block - delay // LANES - back + 9 * BLOCKS
                return (moved % BLOCKS * HERE + i) * RUN + moved // BLOCKS - 9 + FIRST + base

            now, before = start(0), start(1)
            for f in range(0, WINDOW, 8):
                self.delayed[pl.ds(pl.multiple_of(run * WINDOW, 8) + f, 8), :] = jnp.where(
                    keep, self.runs[pl.ds(now + f, 8), :], self.runs[pl.ds(before + f, 8), :]
                )
            tap = [self.tap_rows[pl.ds((block * TAPS + p) * 8, 8), :] for p in range(TAPS)]
            total = {}
            for f in range(HALF + 8):
                values = self.delayed[pl.ds(run * WINDOW + f, 8), :]
                for p in (f % 8 + 8, f % 8):
                    s = f - p
                    if 0 <= s < HALF:
                        total[s] = tap[p] * values if p == 0 else total[s] + tap[p] * values
                if f % 16 == 15 and f > 16:
                    pair = [total.pop(f - 31), total.pop(f - 23)]
                    self.frames[
                        pl.ds(pl.multiple_of(i * HALF, HALF) + f - 31, 16),
                        pl.ds(pl.multiple_of(block * LANES, LANES), LANES),
                    ] = (jnp.concatenate(pair, axis=0) * weight).astype(jnp.bfloat16)
            pair = [total.pop(HALF - 16), total.pop(HALF - 8)]
            self.frames[
                pl.ds(pl.multiple_of(i * HALF, HALF) + HALF - 16, 16),
                pl.ds(pl.multiple_of(block * LANES, LANES), LANES),
            ] = (jnp.concatenate(pair, axis=0) * weight).astype(jnp.bfloat16)
            assert not total
            if each is not None:
                each(run)

    def transform(self, group, inputs, stride):
        nx, ny, nz = self.dims
        per_group = nx * ny
        chips = [self.chip_of(group, jnp.int32(step)) for step in range(per_group)]
        rows = jnp.concatenate(
            [self.rows_table[(x * ny + y) * nz + z] for x, y, z in chips], axis=0
        )

        for first in range(*inputs, 2):
            values = self.frames[first * HALF : (first + 2) * HALF, :]
            spectra = lax.dot_general(
                rows, values, (((1,), (1,)), ((), ())), preferred_element_type=jnp.float32
            )
            for dest in range(2 * per_group):
                for j in range(2):
                    self.turned[
                        pl.ds(dest * 8 * stride + first - inputs[0] + j, 8, stride=stride), :
                    ] = spectra[dest * 8 : (dest + 1) * 8, j * HALF : (j + 1) * HALF]

    def pack(self, dest, target):
        for m in range(0, 8, 2):
            pair_rows = jnp.concatenate(
                [
                    self.turned[pl.ds((dest * 8 + m) * O_STRIDE, HERE), :],
                    self.turned[pl.ds((dest * 8 + m + 1) * O_STRIDE, HERE), :],
                ],
                axis=0,
            )
            target[m * 8 : (m + 2) * 8, :] = pair_rows.astype(jnp.bfloat16)

    def pack_part(self, dest, target, part):
        rows = self.turned[pl.ds(pl.multiple_of(dest * PART, PART), PART), :]
        target[part * PART : (part + 1) * PART, :] = rows.astype(jnp.bfloat16)

    def send(self, source, target, device, send_sem, recv_sem):
        pltpu.make_async_remote_copy(
            src_ref=source,
            dst_ref=target,
            send_sem=send_sem,
            recv_sem=recv_sem,
            device_id=device,
            device_id_type=MESH,
        ).start()

    def send_direct(self, group, step, change, rows, source, target, send_sem, recv_sem):
        core = self.my_core if change == 0 else 1 - self.my_core
        slot = (group * self.dims[0] * self.dims[1] + step) * 2 + core
        chip = self.chip_of(group, step)
        self.send(
            source.at[slot, rows],
            target.at[self.me, rows],
            self.device(chip, core),
            send_sem,
            recv_sem,
        )


def exchange_kernel(dims, samples, delays, flags, taps, table, out, raw, rim, ready, *rest):
    refs, sems = rest[:6], rest[6:]
    load_sem, table_sem, rim_send, rim_recv, send_sem, recv_sem, own_sem = sems
    work = Work(dims, delays, flags, refs)
    nx, ny, nz = dims
    per_group = nx * ny
    inp = nx * ny * nz
    devices = 2 * inp

    def load(first, count, sem):
        part = pl.ds(first * FRAME, count * FRAME)
        return pltpu.make_async_copy(samples.at[:, part], raw.at[:, part], sem)

    late_loads = [
        load(first, count, load_sem.at[piece]) for piece, (first, count) in enumerate(PIECES)
    ]
    for copy in late_loads:
        copy.start()
    fetch = pltpu.make_async_copy(table, work.rows_table, table_sem)
    early_load = load(0, SPLIT, load_sem.at[len(PIECES)])
    barrier = pltpu.get_barrier_semaphore()

    def greet(step):
        other = rem(work.me + step, devices)
        pl.semaphore_signal(
            barrier, inc=1, device_id=(div(other, inp), rem(other, inp)), device_id_type=MESH
        )

    @pl.loop(1, 1 + GREET_FIRST)
    def _(step):
        greet(step)

    work.place_taps(taps)

    def send_chip(half, group, step, part=None):
        rows = pl.ds(0, ROWS) if part is None else pl.ds(part * PART, PART)
        common = (rows, ready.at[half], out.at[half], send_sem.at[half], recv_sem.at[half])

        @pl.when(group + step > 0)
        def _():
            work.send_direct(group, step, 0, *common)

        @pl.when(group + step == 0)
        def _():
            pltpu.make_async_copy(
                ready.at[half, work.my_core, rows], out.at[half, work.me, rows], own_sem.at[half]
            ).start()

        work.send_direct(group, step, 1, *common)

    later = per_group - AT_ONCE

    def send_later(order, part):
        send_chip(1, div(order, later), AT_ONCE + rem(order, later), part)

    def transform_part(part):
        @pl.loop(0, nz)
        def _(group):
            work.transform(group, (part * 4, part * 4 + 4), 4)

            @pl.loop(0, 2 * per_group, step=8)
            def _(dests):
                for dest in range(8):
                    dest = dests + dest
                    work.pack_part(dest, ready.at[1, group * 2 * per_group + dest], part)

            @pl.loop(0, AT_ONCE)
            def _(step):
                send_chip(1, group, step, part)

    def transform_second():
        @pl.loop(0, nz)
        def _(group):
            work.transform(group, (0, HERE), O_STRIDE)

            @pl.loop(0, per_group, step=4)
            def _(chips):
                for dest in range(8):
                    dest = chips * 2 + dest
                    work.pack(dest, ready.at[0, group * 2 * per_group + dest])

    def in_first(run):
        send_later(run - 4 * BLOCKS, 0)

    def in_spread(step):
        @pl.when(rem(step, 3) == 0)
        def _():
            send_later(div(step, 3), 1)

    def in_filter(run):
        @pl.when(rem(run, 3) == 0)
        def _():
            send_later(9 + div(run, 3), 1)

    greeted = 1 + GREET_FIRST
    for piece, (first, count) in enumerate(PIECES):
        late_loads[piece].wait()
        if piece == 1:
            fetch.start()
            early_load.start()
        whole = count // 4 * 4

        def in_late(step, begin=greeted):
            for k in range(GREET_STEP):
                greet(begin + step * GREET_STEP + k)

        greeting = greeted < devices
        work.spread(raw, FIRST, (first, first + whole), 4, in_late if greeting else None)
        if greeting:
            greeted += whole // 4 * GREET_STEP
        if whole < count:
            work.spread(raw, FIRST, (first + whole, first + count), 1)
    assert greeted == devices
    pl.semaphore_wait(barrier, devices - 1)
    rim_copy = pltpu.make_async_remote_copy(
        src_ref=samples.at[:, pl.ds(S_DEV * FRAME - HALO, HALO)],
        dst_ref=rim,
        send_sem=rim_send,
        recv_sem=rim_recv,
        device_id=(1 - work.tseg, work.here),
        device_id_type=MESH,
    )
    rim_copy.start()
    work.run_half(1, (0, 4))
    fetch.wait()
    transform_part(0)
    work.run_half(1, (4, HERE), in_first)
    transform_part(1)

    early_load.wait()
    work.spread(raw, FIRST, (0, SPLIT - 3), 4, in_spread)
    work.spread(raw, FIRST, (SPLIT - 3, SPLIT), 1)
    rim_copy.wait()

    @pl.when(work.tseg == 0)
    def _():
        rim[...] = jnp.zeros_like(rim)

    work.spread(rim, 1, (0, 20), 4)
    work.spread(rim, 1, (20, HALO // FRAME), 1)
    work.run_half(0, (0, HERE), in_filter)
    send_later(jnp.int32(31), 1)
    transform_second()

    @pl.loop(0, nz * per_group)
    def _(slot):
        send_chip(0, div(slot, per_group), rem(slot, per_group))

    for half in (1, 0):
        pltpu.make_async_copy(
            ready.at[half, work.my_core], out.at[half, work.me], own_sem.at[half]
        ).wait()
        sent = ready.at[half, pl.ds(0, devices - 1)]
        pltpu.make_async_copy(sent, sent, send_sem.at[half]).wait()
        arrived = out.at[half, pl.ds(0, devices - 1)]
        pltpu.make_async_copy(arrived, arrived, recv_sem.at[half]).wait()


def correlate_kernel(segments, scale, source, vis_real, vis_imag, loaded, sem):
    channel = pl.program_id(0)
    odd = lax.rem(channel, 2)
    tile = 2 * HERE

    def second(c):
        rows = pl.ds(pl.multiple_of(c * tile, tile), tile)
        return pltpu.make_async_copy(source.at[0, :, rows, :], loaded.at[0, c], sem.at[0, c])

    def first(pair, part):
        rows = pl.ds(pl.multiple_of(part * PART + pair * tile, tile), tile)
        place = pair * 2 + part
        return pltpu.make_async_copy(
            source.at[1, :, rows, :], loaded.at[1, place], sem.at[1, place]
        )

    @pl.when(channel == 0)
    def _():
        for part in range(2):
            first(0, part).start()
        second(0).start()

    pair = lax.div(channel, 2)

    @pl.when(odd == 0)
    def _():
        for part in range(2):
            first(pair, part).wait()

    second(channel).wait()

    @pl.when(channel == 0)
    def _():
        second(1).start()
        for part in range(2):
            first(1, part).start()
        for c in range(2, CHAN):
            second(c).start()

    sources = loaded.shape[2] // segments
    inputs = sources * HERE
    upper = lax.broadcasted_iota(jnp.int32, (sources, HERE, HALF), 1) < HERE // 2
    real, imag = [], []

    def keep(to, values):
        to.append(values.reshape(inputs, HALF).astype(jnp.bfloat16))

    for segment in range(segments):
        here = pl.ds(segment * sources, sources)
        piece = loaded[0, channel, here].astype(jnp.float32)
        keep(real, piece[:, :HERE])
        keep(imag, piece[:, HERE:])
        parts = []
        for part in range(2):
            piece = loaded[1, pair * 2 + part, here].astype(jnp.float32)
            parts.append(jnp.where(odd == 1, piece[:, HERE:], piece[:, :HERE]))
        keep(real, jnp.where(upper, parts[0], pltpu.roll(parts[1], 4, 1)))
        keep(imag, jnp.where(upper, pltpu.roll(parts[0], 4, 1), parts[1]))
    real = jnp.concatenate(real, axis=1)
    imag = jnp.concatenate(imag, axis=1)

    def product(a, b):
        return lax.dot_general(a, b, (((1,), (1,)), ((), ())), preferred_element_type=jnp.float32)

    middle = inputs // 2
    low, high = slice(0, middle), slice(middle, inputs)
    for rows, columns in ((low, low), (high, high), (low, high)):
        block = product(real[rows], real[columns]) + product(imag[rows], imag[columns])
        vis_real[0, rows, columns] = block * scale
        if rows != columns:
            vis_real[0, columns, rows] = block.T * scale
    cross = product(real, imag)
    vis_imag[0] = (cross - cross.T) * scale


def per_device(samples, delays, flags, taps, *, segments, inp):
    nx, nz, ny_hi = SHAPES[inp]
    dims = (nx, 2 * ny_hi, nz)
    devices = segments * inp
    per_group = nx * 2 * ny_hi
    table = jnp.asarray(dft_rows(*dims))
    anywhere = pl.BlockSpec(memory_space=pl.ANY)
    in_specs = [
        anywhere,
        pl.BlockSpec(memory_space=pltpu.SMEM),
        pl.BlockSpec(memory_space=pltpu.SMEM),
        pl.BlockSpec(memory_space=pltpu.VMEM),
        anywhere,
    ]
    work_scratch = [
        pltpu.VMEM((nz * per_group, 16, FRAME), jnp.bfloat16),
        pltpu.VMEM((BLOCKS * HERE * RUN + 8, LANES), jnp.float32),
        pltpu.VMEM((BLOCKS * TAPS * 8, LANES), jnp.float32),
        pltpu.VMEM((HERE * BLOCKS * WINDOW, LANES), jnp.float32),
        pltpu.VMEM((HERE * HALF, FRAME), jnp.bfloat16),
        pltpu.VMEM((2 * per_group * 8 * O_STRIDE, LANES), jnp.float32),
    ]
    raw = pltpu.VMEM((HERE, S_DEV * FRAME), jnp.bfloat16)
    dma = pltpu.SemaphoreType.DMA
    spectra = pl.pallas_call(
        functools.partial(exchange_kernel, dims),
        out_shape=jax.ShapeDtypeStruct((2, devices, ROWS, HALF), jnp.bfloat16),
        in_specs=in_specs,
        out_specs=anywhere,
        scratch_shapes=[
            raw,
            pltpu.VMEM((HERE, HALO), jnp.bfloat16),
            pltpu.VMEM((2, devices, ROWS, HALF), jnp.bfloat16),
            *work_scratch,
            dma((len(PIECES) + 1,)),
            *[dma] * 3,
            *[dma((2,))] * 3,
        ],
        compiler_params=pltpu.CompilerParams(
            collective_id=0, has_side_effects=True, vmem_limit_bytes=60 * 2**20
        ),
        name="exchange",
    )(samples, delays, flags, taps, table)
    inputs = inp * HERE
    visibility = jax.ShapeDtypeStruct((CHAN, inputs, inputs), jnp.float32)
    return pl.pallas_call(
        functools.partial(correlate_kernel, segments, 1.0 / (S_DEV * segments)),
        out_shape=(visibility, visibility),
        grid=(CHAN,),
        in_specs=[anywhere],
        out_specs=(
            pl.BlockSpec((1, inputs, inputs), lambda c: (c, 0, 0)),
            pl.BlockSpec((1, inputs, inputs), lambda c: (c, 0, 0)),
        ),
        scratch_shapes=[
            pltpu.VMEM((2, CHAN, devices, 2 * HERE, HALF), jnp.bfloat16),
            dma((2, CHAN)),
        ],
        compiler_params=pltpu.CompilerParams(vmem_limit_bytes=60 * 2**20),
        name="correlate",
    )(spectra)


def solution(mesh):
    segments, inp = mesh.shape["tseg"], mesh.shape["inp"]
    return jax.shard_map(
        functools.partial(per_device, segments=segments, inp=inp),
        mesh=mesh,
        in_specs=(P("inp", "tseg"), P("inp"), P("inp"), P()),
        out_specs=(P(("tseg", "inp"), None, None), P(("tseg", "inp"), None, None)),
        check_vma=False,
    )
```
